128 devices in a mesh: section: 2 (over core), dp: 16 (over z, y), tensor: 4 (over x).
Axes of the slice: x: 4, y: 4, z: 4, core: 2. Of those that a mesh axis runs over, the one named last changes fastest.
Arguments:
- tokens_in: bfloat16 [2, 8192, 1024], P(None, ('dp', 'tensor')), may hold values from -6 to 6
- cotangent: bfloat16 [2, 8192, 1024], P(None, ('dp', 'tensor')), may hold values from -6 to 6
- seq_lengths: int32 [2, 16], P(None, 'dp'), may hold values from 64 to 512, as said below
- gain_in: float32 [2, 1024], P('section'), may hold values from 0.5 to 1.5
- weight_x: bfloat16 [2, 1024, 2048], P('section', 'dp', 'tensor'), may hold values from -0.1875 to 0.1875
- weight_z: bfloat16 [2, 1024, 2048], P('section', 'dp', 'tensor'), may hold values from -0.1875 to 0.1875
- weight_bc: bfloat16 [2, 1024, 256], P('section', 'dp', 'tensor'), may hold values from -0.1875 to 0.1875
- weight_dt: bfloat16 [2, 1024, 32], P('section', 'dp', 'tensor'), may hold values from -0.1875 to 0.1875
- conv_x: float32 [2, 4, 2048], P('section', None, 'tensor'), may hold values from -0.5 to 0.5
- conv_bc: float32 [2, 4, 256], P('section', None, 'tensor'), may hold values from -0.5 to 0.5
- bias_x: float32 [2, 2048], P('section', 'tensor'), may hold values from -0.5 to 0.5
- bias_bc: float32 [2, 256], P('section', 'tensor'), may hold values from -0.5 to 0.5
- dt_bias: float32 [2, 32], P('section', 'tensor'), may hold values from -6 to -2
- decay_log: float32 [2, 32], P('section', 'tensor'), may hold values from -1 to 1.5
- skip_gain: float32 [2, 32], P('section', 'tensor'), may hold values from 0.5 to 1.5
- gain_out: float32 [2, 2048], P('section', 'tensor'), may hold values from 0.5 to 1.5
- weight_out: bfloat16 [2, 2048, 1024], P('section', 'tensor', 'dp'), may hold values from -0.125 to 0.125
Outputs:
- layer_outputs: bfloat16 [2, 2, 8192, 1024], P('section', None, ('dp', 'tensor'))
- input_grads: float32 [2, 2, 8192, 1024], P('section', None, ('dp', 'tensor'))
- grad_gain_in: float32 [2, 1024], P('section')
- grad_weight_x: float32 [2, 1024, 2048], P('section', 'dp', 'tensor')
- grad_weight_z: float32 [2, 1024, 2048], P('section', 'dp', 'tensor')
- grad_weight_bc: float32 [2, 1024, 256], P('section', 'dp', 'tensor')
- grad_weight_dt: float32 [2, 1024, 32], P('section', 'dp', 'tensor')
- grad_conv_x: float32 [2, 4, 2048], P('section', None, 'tensor')
- grad_conv_bc: float32 [2, 4, 256], P('section', None, 'tensor')
- grad_bias_x: float32 [2, 2048], P('section', 'tensor')
- grad_bias_bc: float32 [2, 256], P('section', 'tensor')
- grad_dt_bias: float32 [2, 32], P('section', 'tensor')
- grad_decay_log: float32 [2, 32], P('section', 'tensor')
- grad_skip_gain: float32 [2, 32], P('section', 'tensor')
- grad_gain_out: float32 [2, 2048], P('section', 'tensor')
- grad_weight_out: float32 [2, 2048, 1024], P('section', 'tensor', 'dp')
The draws below stay inside these ranges and needn't reach their ends.
Inputs may be any that keep to these rules, and one draw needn't show every extreme that they name: `seq_lengths`: in every data group one micro-batch, drawn from the seed, holds a sequence of exactly 512 tokens; every length is at least 64.
All inputs are finite; a program needn't handle non-finite values.
Results may differ from the reference program's by a relative error of at most 0.018.
Values may be sent and summed in bfloat16 or wider, within the bound.
A program may use at most 128 MiB of HBM per device.

```python
import jax
import jax.numpy as jnp
from jax import lax

D = 1024
INNER = 2048
HEADS = 32
STATE = 128
CONV = 4
SPAN = 256
MB = 2
SLOT = 512
TOKENS = 8192
N_DP = 16


def draw_seq_lengths(key, part):
    key = jax.random.fold_in(key, 7)
    first_key, second_key = jax.random.split(key)
    full_pick = jax.random.randint(first_key, (N_DP,), 0, MB)
    others = jax.random.randint(second_key, (MB, N_DP), max(1, SLOT // 8), SLOT + 1)
    micro_rows = jnp.arange(MB)[:, None]
    return jnp.where(micro_rows == full_pick[None, :], SLOT, others).astype(jnp.int32)


def block_levels(stream_key, dims, shards, least, top_value):
    def one(position, shards_of):
        steps = jax.random.uniform(jax.random.fold_in(jax.random.fold_in(stream_key, 6), position), (shards_of,), jnp.float32, least / len(shards), top_value / len(shards))
        return jnp.repeat(jnp.exp(steps), dims[position] // shards_of).reshape((-1,) + (1,) * (len(dims) - position - 1))

    level = one(*shards[0])
    for cut in shards[1:]:
        level = level * one(*cut)
    return level


def centred(stream_key, extent, deviation, most, cuts=(), held_as=jnp.bfloat16):
    array = jax.random.normal(stream_key, extent, jnp.float32) * deviation
    if len(cuts) > 0:
        array = block_levels(stream_key, extent, cuts, -0.22, 0.18) * array
    return jnp.clip(array, min=-most, max=most).astype(held_as)


def setup_inputs(seed: int = 0) -> dict:
    splits = jax.random.split(jax.random.key(seed), 18)
    tokens_in = centred(splits[0], (MB, TOKENS, D), 1.0, 6.0, ((1, 64),))
    cotangent = centred(splits[1], (MB, TOKENS, D), 1.0, 6.0, ((1, 64),))
    seq_lengths = draw_seq_lengths(jax.random.fold_in(splits[17], 71), 0)
    gain_in = jnp.clip(1.0 + 0.1 * jax.random.normal(splits[3], (2, D), jnp.float32), 0.5, 1.5)
    weight_x = centred(splits[4], (2, D, INNER), D ** -0.5, 0.1875, ((0, 2), (1, 16), (2, 4)))
    weight_z = centred(splits[5], (2, D, INNER), D ** -0.5, 0.1875, ((0, 2), (1, 16), (2, 4)))
    weight_bc = centred(splits[6], (2, D, 2 * STATE), D ** -0.5, 0.1875, ((0, 2), (1, 16), (2, 4)))
    weight_dt = centred(splits[7], (2, D, HEADS), D ** -0.5, 0.1875, ((0, 2), (1, 16), (2, 4)))
    conv_x = jnp.clip(jax.random.uniform(splits[8], (2, CONV, INNER), jnp.float32, -0.5, 0.5) * block_levels(splits[8], (2, CONV, INNER), ((0, 2), (2, 4)), -0.4, 0.0), -0.5, 0.5)
    conv_bc = jnp.clip(jax.random.uniform(splits[9], (2, CONV, 2 * STATE), jnp.float32, -0.5, 0.5) * block_levels(splits[9], (2, CONV, 2 * STATE), ((0, 2), (2, 4)), -0.4, 0.0), -0.5, 0.5)
    bias_x = jnp.clip(jax.random.uniform(splits[10], (2, INNER), jnp.float32, -0.5, 0.5) * block_levels(splits[10], (2, INNER), ((0, 2), (1, 4)), -0.4, 0.0), -0.5, 0.5)
    bias_bc = jnp.clip(jax.random.uniform(splits[11], (2, 2 * STATE), jnp.float32, -0.5, 0.5) * block_levels(splits[11], (2, 2 * STATE), ((0, 2), (1, 4)), -0.4, 0.0), -0.5, 0.5)
    dt_bias = jnp.clip(-6.0 + 4.0 * jax.random.uniform(splits[12], (2, HEADS), jnp.float32) ** block_levels(splits[12], (2, HEADS), ((0, 2), (1, 4)), -0.2, 0.2), -6.0, -2.0)
    decay_log = jnp.clip(-1.0 + 2.5 * jax.random.uniform(splits[13], (2, HEADS), jnp.float32) ** block_levels(splits[13], (2, HEADS), ((0, 2), (1, 4)), -0.2, 0.2), -1.0, 1.5)
    skip_gain = jnp.clip(0.5 + 1.0 * jax.random.uniform(splits[14], (2, HEADS), jnp.float32) ** block_levels(splits[14], (2, HEADS), ((0, 2), (1, 4)), -0.2, 0.2), 0.5, 1.5)
    gain_out = jnp.clip(1.0 + 0.1 * jax.random.normal(splits[15], (2, INNER), jnp.float32), 0.5, 1.5)
    weight_out = centred(splits[16], (2, INNER, D), INNER ** -0.5, 0.125, ((0, 2), (1, 4), (2, 16)))
    return dict(tokens_in=tokens_in, cotangent=cotangent, seq_lengths=seq_lengths, gain_in=gain_in, weight_x=weight_x, weight_z=weight_z, weight_bc=weight_bc, weight_dt=weight_dt, conv_x=conv_x, conv_bc=conv_bc, bias_x=bias_x, bias_bc=bias_bc, dt_bias=dt_bias, decay_log=decay_log, skip_gain=skip_gain, gain_out=gain_out, weight_out=weight_out)


epsilon = 1e-05
highest = lax.Precision.HIGHEST

@jax.custom_vjp
def low(v):
    return lax.optimization_barrier(v.astype(jnp.bfloat16)).astype(jnp.float32)

@jax.custom_vjp
def low_back(v):
    return v

def low_keep(v):
    return (low(v), None)

def low_pass(kept, grad):
    return (grad,)

def back_keep(v):
    return (v, None)

def back_low(kept, grad):
    return (low(grad),)
low.defvjp(low_keep, low_pass)
low_back.defvjp(back_keep, back_low)

def causal_conv(signal, kernel):
    tap_count = kernel.shape[0]
    padded = jnp.pad(signal, ((tap_count - 1, 0), (0, 0)))
    running = jnp.zeros_like(signal)
    for offset in range(tap_count):
        running = running + kernel[offset][None, :] * padded[offset:offset + signal.shape[0]]
    return running

def conv_part(signal, kernel, offsets):
    return jax.nn.silu(causal_conv(signal, kernel) + offsets[None, :])

def scan_blocks(values, step_sizes, rates, inputs_b, inputs_c):
    length, head_count, head_dim = values.shape
    number = length // SPAN
    states = inputs_b.shape[1]
    grouped = (values.reshape(number, SPAN, head_count, head_dim), step_sizes.reshape(number, SPAN, head_count), inputs_b.reshape(number, SPAN, states), inputs_c.reshape(number, SPAN, states))
    positions = jnp.arange(SPAN)
    causal = positions[:, None] >= positions[None, :]

    def block_step(carried, pieces):
        block_x, block_dt, block_b, block_c = pieces
        log_steps = block_dt * rates[None, :]
        totals = jnp.cumsum(log_steps, axis=0)
        across = totals.T
        log_gaps = across[:, :, None] - across[:, None, :]
        decays = jnp.where(causal[None], jnp.exp(jnp.where(causal[None], log_gaps, 0.0)), 0.0)
        intersection = jnp.dot(block_c, block_b.T, precision=highest, preferred_element_type=jnp.float32)
        mixing = decays * intersection[None] * block_dt.T[:, None, :]
        inside = jnp.einsum('hts,shp->thp', mixing, block_x, precision=highest)
        carried_in = jnp.einsum('tn,hpn->thp', block_c, carried, precision=highest) * jnp.exp(totals)[:, :, None]
        final_log = totals[-1]
        weights_tail = jnp.exp(final_log[None, :] - totals) * block_dt
        updated = jnp.exp(final_log)[:, None, None] * carried + jnp.einsum('shp,sn->hpn', weights_tail[:, :, None] * block_x, block_b, precision=highest)
        return (updated, inside + carried_in)
    initial = jnp.zeros((head_count, head_dim, states), jnp.float32)
    _, outputs = lax.scan(jax.checkpoint(block_step), initial, grouped)
    return outputs.reshape(length, head_count, head_dim)

def mixer(proj_x, proj_z, proj_dt, both_bc, conv_x, bias_x, dt_bias, decay_log, skip_gain):
    head_count = dt_bias.shape[0]
    channels = proj_x.shape[1]
    head_dim = channels // head_count
    states = both_bc.shape[1] // 2
    signal = conv_part(proj_x, conv_x, bias_x)
    step_sizes = jax.nn.softplus(proj_dt + dt_bias[None, :])
    rates = -jnp.exp(decay_log)
    shaped = signal.reshape(signal.shape[0], head_count, head_dim)
    scanned = scan_blocks(shaped, step_sizes, rates, both_bc[:, :states], both_bc[:, states:])
    output = scanned + skip_gain[None, :, None] * shaped
    gated = output.reshape(signal.shape[0], channels) * jax.nn.silu(proj_z)
    return (gated, lax.optimization_barrier(jnp.sum(gated * gated, axis=-1)))

def slot_layer(stream, length, params):
    gain_in, weight_x, weight_z, weight_bc, weight_dt, conv_x, conv_bc, bias_x, bias_bc, dt_bias, decay_log, skip_gain, gain_out, weight_out = params
    scale_in = lax.rsqrt(lax.optimization_barrier(jnp.mean(stream * stream, axis=-1, keepdims=True)) + epsilon)
    normed = low(stream * scale_in * gain_in[None, :])
    proj_x = low_back(jnp.dot(normed, weight_x, precision=highest, preferred_element_type=jnp.float32))
    proj_z = low_back(jnp.dot(normed, weight_z, precision=highest, preferred_element_type=jnp.float32))
    proj_bc = low_back(jnp.dot(normed, weight_bc, precision=highest, preferred_element_type=jnp.float32))
    proj_dt = low_back(jnp.dot(normed, weight_dt, precision=highest, preferred_element_type=jnp.float32))
    both_bc = low(conv_part(proj_bc, conv_bc, bias_bc))
    gated, squares = mixer(proj_x, proj_z, proj_dt, both_bc, conv_x, bias_x, dt_bias, decay_log, skip_gain)
    factor = lax.rsqrt(squares / INNER + epsilon)
    normed_out = low(gated * factor[:, None] * gain_out[None, :])
    branch = low_back(jnp.dot(normed_out, weight_out, precision=highest, preferred_element_type=jnp.float32))
    valid_rows = (jnp.arange(SLOT) < length).astype(jnp.float32)
    return valid_rows[:, None] * (stream + branch)

def layer(streams, params, lengths):

    def one_slot(paired):
        return slot_layer(paired[0], paired[1], params)
    return lax.map(jax.checkpoint(one_slot), (streams, lengths))

def reference(tokens_in, cotangent, seq_lengths, gain_in, weight_x, weight_z, weight_bc, weight_dt, conv_x, conv_bc, bias_x, bias_bc, dt_bias, decay_log, skip_gain, gain_out, weight_out):
    lengths = seq_lengths.reshape(-1).astype(jnp.int32)
    slot_count = lengths.shape[0]
    arrays = (gain_in, weight_x, weight_z, weight_bc, weight_dt, conv_x, conv_bc, bias_x, bias_bc, dt_bias, decay_log, skip_gain, gain_out, weight_out)
    first = tuple((member[0].astype(jnp.float32) for member in arrays))
    second = tuple((member[1].astype(jnp.float32) for member in arrays))
    streams = tokens_in.astype(jnp.float32).reshape(slot_count, SLOT, D)
    seeded = cotangent.astype(jnp.float32).reshape(slot_count, SLOT, D)

    def first_layer(values, params):
        return low_back(low(layer(values, params, lengths)))

    def second_layer(values, params):
        return layer(values, params, lengths)
    hidden, pull_first = jax.vjp(first_layer, streams, first)
    final, pull_second = jax.vjp(second_layer, hidden, second)
    back_hidden, grads_second = pull_second(seeded)
    back_input, grads_first = pull_first(back_hidden)
    shape_out = (2, MB, N_DP * SLOT, D)
    layer_outputs = jnp.stack([hidden, final]).astype(jnp.bfloat16).reshape(shape_out)
    input_grads = jnp.stack([back_input, back_hidden]).reshape(shape_out)
    stacked = [jnp.stack([grads_first[index], grads_second[index]]) for index in range(14)]
    return (layer_outputs, input_grads, stacked[0], stacked[1], stacked[2], stacked[3], stacked[4], stacked[5], stacked[6], stacked[7], stacked[8], stacked[9], stacked[10], stacked[11], stacked[12], stacked[13])
```

```python
import functools

import jax
import jax.numpy as jnp
from jax import lax
from jax.experimental import pallas as pl
from jax.experimental.pallas import tpu as pltpu
from jax.sharding import PartitionSpec as P

F32 = jnp.float32
BF16 = jnp.bfloat16
T = 512
L = 128
NB = T // L
D = 1024
CH = 512
INNER = 2048
NST = 128
EPS = 1e-05
X0, Z0, O0, B0, S0, COLS = 0, 512, 1024, 1536, 1792, 1920
VMEM_LIMIT = 56 * 2**20

NN = (((1,), (0,)), ((), ()))
NT = (((1,), (1,)), ((), ()))
TN = (((0,), (0,)), ((), ()))


def mm(a, b, dims=NN):
    return lax.dot_general(a, b, dims, preferred_element_type=F32)


def mm_exact(a, b):
    return lax.dot_general(a, b, NN, precision=lax.Precision.HIGHEST, preferred_element_type=F32)


def mm_split(a, b):
    hi = a.astype(BF16)
    lo = (a - hi.astype(F32)).astype(BF16)
    return mm(hi, b) + mm(lo, b)


def iota(shape, dim):
    return lax.broadcasted_iota(jnp.int32, shape, dim)


def as_row(column):
    return jnp.broadcast_to(column, (L, 128)).T[0:1, :]


def as_column(row):
    return jnp.broadcast_to(row, (128, L)).T[:, 0:1]


def softplus(v):
    return jnp.maximum(v, 0.0) + jnp.log1p(jnp.exp(-jnp.abs(v)))


def head_spread():
    return (iota((128, CH), 1) // 64 == iota((128, CH), 0)).astype(BF16)


def head_collect():
    return (iota((CH, 128), 0) // 64 == iota((CH, 128), 1)).astype(BF16)


def row_mask(length, start, rows, columns):
    return (iota((rows, columns), 0) + start < length).astype(F32)


def rows_of(block):
    return pl.ds(pl.multiple_of(block * L, L), L)


def fwd_kernel(second, *refs):
    if second:
        (len_ref, u_ref, w_ref, par_ref, cot_ref, p_ref, sq_ref, n_ref, px_ref, cx_ref, pz_ref, pbc_ref, cbc_ref,
         v_ref, y_ref, h_ref, gb_ref, dno_ref, padx, padbc, state, step, cum, g_ref) = refs
    else:
        (u_ref, w_ref, par_ref, p_ref, sq_ref, n_ref, px_ref, cx_ref, pz_ref, pbc_ref, cbc_ref,
         v_ref, y_ref, h_ref, padx, padbc, state, step, cum, g_ref) = refs

    def par(row, start, size):
        return par_ref[0, row : row + 1, start : start + size]

    gain_in = jnp.concatenate([par(6, 0, 512), par(7, 0, 512)], axis=1)

    def norm_rows(i, carry):
        rows = pl.ds(pl.multiple_of(i * 64, 64), 64)
        u = u_ref[rows, :].astype(F32)
        r = lax.rsqrt(jnp.mean(u * u, axis=-1, keepdims=True) + EPS)
        n_ref[rows, :] = (u * r * gain_in).astype(BF16)
        return carry

    lax.fori_loop(0, T // 64, norm_rows, 0)

    def weight(start, size):
        return w_ref[0, :, :, start : start + size].reshape(D, size)

    padx[0:8, :] = jnp.zeros((8, CH), F32)
    padbc[0:8, :] = jnp.zeros((8, 256), F32)
    padbc[8 : 8 + T, :] = mm(n_ref[...], weight(B0, 256))
    v_ref[...] = mm(n_ref[...], weight(S0, 128)) + par(8, 0, 128)
    for j in range(2):
        padx[8 : 8 + T, 256 * j : 256 * j + 256] = mm(n_ref[...], weight(X0 + 256 * j, 256))
    for j in range(2):
        pz_ref[:, 256 * j : 256 * j + 256] = mm(n_ref[...], weight(Z0 + 256 * j, 256))
    px_ref[...] = padx[8 : 8 + T, :]
    pbc_ref[...] = padbc[8 : 8 + T, :]

    for b in range(NB):
        for j in range(4):
            cols = slice(128 * j, 128 * j + 128)
            c = par(4, 128 * j, 128)
            for k in range(4):
                c = c + par(k, 128 * j, 128) * padx[5 + k + b * L : 5 + k + b * L + L, cols]
            cx_ref[b * L : b * L + L, cols] = c
        for j in range(2):
            cols = slice(128 * j, 128 * j + 128)
            c = par(13, 128 * j, 128)
            for k in range(4):
                c = c + par(9 + k, 128 * j, 128) * padbc[5 + k + b * L : 5 + k + b * L + L, cols]
            cbc_ref[b * L : b * L + L, cols] = c

    lower = iota((L, L), 0) >= iota((L, L), 1)
    tri = lower.astype(F32)
    off = jnp.where(lower, 0.0, -1e30)
    spread = head_spread()
    rate = -jnp.exp(par(8, 128, 128))
    skip = mm_exact(jnp.broadcast_to(par(8, 256, 128), (8, 128)), spread.astype(F32))[0:1, :]
    gain_out = par(5, 0, CH)
    first_half = iota((L, 128), 1) < 64
    state[...] = jnp.zeros((NST, CH), F32)

    def block(b, carry):
        rows = rows_of(b)
        v = v_ref[rows, :]
        st = softplus(v)
        cu = mm_exact(tri, st * rate)
        cut = cu.T
        ea = jnp.exp(cu)
        tail = jnp.exp(cu[L - 1 : L, :] - cu)
        st_e = mm_split(st, spread)
        ea_e = mm_split(ea, spread)
        tail_e = mm_split(tail, spread)
        cx = cx_ref[rows, :]
        xs = cx * jax.nn.sigmoid(cx)
        cbc = cbc_ref[rows, :]
        bc = (cbc * jax.nn.sigmoid(cbc)).astype(BF16)
        bb, cc = bc[:, :NST], bc[:, NST:]
        xd = xs * st_e
        h_in = state[...].astype(BF16)
        h_ref[b] = h_in
        gram = mm(cc, bb, NT)
        y = mm(cc, h_in) * ea_e
        state[...] = state[...] * ea_e[L - 1 : L, :] + mm(bb, (xd * tail_e).astype(BF16), TN)
        inside = []
        for pair in range(4):
            xp = xd[:, 128 * pair : 128 * pair + 128]
            parts = []
            mixes = []
            for half in range(2):
                h = 2 * pair + half
                mixes.append((gram * jnp.exp(cu[:, h : h + 1] - cut[h : h + 1, :] + off)).astype(BF16))
                parts.append(jnp.where(first_half == (half == 0), xp, 0.0).astype(BF16))
            inside.append(mm(jnp.concatenate(mixes, axis=1), jnp.concatenate(parts, axis=0)))
        y = y + jnp.concatenate(inside, axis=1)
        y_ref[rows, :] = y
        z = pz_ref[rows, :]
        gated = (y + xs * skip) * (z * jax.nn.sigmoid(z))
        sq_ref[pl.ds(b, 1), :] = as_row(jnp.sum(gated * gated, axis=-1, keepdims=True))
        weighted = gated * gain_out
        g_ref[rows, :] = weighted.astype(BF16)
        if second:
            cot = cot_ref[rows, :].astype(F32) * row_mask(len_ref[0, 0], b * L, L, D)
            gb = cot.astype(BF16)
            gb_ref[rows, :] = gb
            dno = jnp.concatenate([mm(gb, weight(O0, 256)), mm(gb, weight(O0 + 256, 256))], axis=1)
            dno_ref[rows, :] = dno
            sq_ref[pl.ds(4 + b, 1), :] = as_row(jnp.sum(dno * weighted, axis=-1, keepdims=True))
        return carry

    lax.fori_loop(0, NB, block, 0)
    if not second:
        sq_ref[4:8, :] = jnp.zeros((4, 128), F32)
    for j in range(4):
        wo = w_ref[0, 4 * j : 4 * j + 4, :, O0 : O0 + CH].reshape(256, CH)
        p_ref[:, 256 * j : 256 * j + 256] = mm(g_ref[...], wo, NT).astype(BF16)


def bwd_kernel(second, *refs):
    if second:
        (gb_ref, w_ref, par_ref, sq_ref, n_ref, px_ref, cx_ref, pz_ref, pbc_ref, cbc_ref, v_ref, y_ref, h_ref, dno_ref,
         dn_ref, dw_ref, sg_ref, padx, padbc, dcx, dcbc, dproj, no_ref, dstate, ggo, gsk, gdt, gdl) = refs
    else:
        (gb_ref, w_ref, par_ref, sq_ref, n_ref, px_ref, cx_ref, pz_ref, pbc_ref, cbc_ref, v_ref, y_ref, h_ref,
         dn_ref, dw_ref, sg_ref, padx, padbc, dcx, dcbc, dproj, no_ref, dstate, ggo, gsk, gdt, gdl) = refs

    def par(row, start, size):
        return par_ref[0, row : row + 1, start : start + size]

    def weight(start, size):
        return w_ref[0, :, :, start : start + size].reshape(D, size)

    lower = iota((L, L), 0) >= iota((L, L), 1)
    upper_inc = (iota((L, L), 1) >= iota((L, L), 0)).astype(F32)
    strict = (iota((L, L), 1) < iota((L, L), 0)).astype(F32)
    upper_low = upper_inc.astype(BF16)
    strict_low = strict.astype(BF16)
    tri = lower.astype(F32)
    off = jnp.where(lower, 0.0, -1e30)
    spread = head_spread()
    collect = head_collect()
    rate = -jnp.exp(par(8, 128, 128))
    skip = mm_exact(jnp.broadcast_to(par(8, 256, 128), (8, 128)), spread.astype(F32))[0:1, :]
    gain_out = par(5, 0, CH)
    first_half = iota((L, 128), 1) < 64
    lanes = iota((L, 128), 1)
    dstate[...] = jnp.zeros((NST, CH), F32)
    ggo[...] = jnp.zeros((8, CH), F32)
    gsk[...] = jnp.zeros((8, CH), F32)
    gdt[...] = jnp.zeros((8, 128), F32)
    gdl[...] = jnp.zeros((8, 128), F32)

    def fold(a):
        return jnp.sum(a.reshape(a.shape[0] // 8, 8, a.shape[1]), axis=0)

    def block(i, carry):
        b = NB - 1 - i
        rows = rows_of(b)
        v = v_ref[rows, :]
        st = softplus(v)
        cu = mm_exact(tri, st * rate)
        cut = cu.T
        ea = jnp.exp(cu)
        tail = jnp.exp(cu[L - 1 : L, :] - cu)
        st_e = mm_split(st, spread)
        ea_e = mm_split(ea, spread)
        tail_e = mm_split(tail, spread)
        cx = cx_ref[rows, :]
        sx = jax.nn.sigmoid(cx)
        xs = cx * sx
        cbc = cbc_ref[rows, :]
        sbc = jax.nn.sigmoid(cbc)
        bc = (cbc * sbc).astype(BF16)
        bb, cc = bc[:, :NST], bc[:, NST:]
        xd = xs * st_e
        factor = as_column(lax.rsqrt(sq_ref[pl.ds(b, 1), :] / INNER + EPS))
        inner = as_column(sq_ref[pl.ds(4 + b, 1), :])
        gb = gb_ref[rows, :]
        if second:
            dno = dno_ref[rows, :]
        else:
            dno = jnp.concatenate([mm(gb, weight(O0, 256)), mm(gb, weight(O0 + 256, 256))], axis=1)
        out = y_ref[rows, :] + xs * skip
        z = pz_ref[rows, :]
        sz = jax.nn.sigmoid(z)
        silu_z = z * sz
        gated = out * silu_z
        scaled = gated * factor
        no_ref[rows, :] = (scaled * gain_out).astype(BF16)
        ggo[...] += fold(dno * scaled)
        dgated = factor * (dno * gain_out) - gated * (factor * factor * factor * (1.0 / INNER) * inner)
        dy = dgated * silu_z
        dproj[rows, Z0 : Z0 + CH] = (dgated * out * (sz * (1.0 + z - silu_z))).astype(BF16)
        gsk[...] += fold(dy * xs)
        dyb = dy.astype(BF16)
        h_in = h_ref[b]
        h_back = dstate[...]
        hb_low = h_back.astype(BF16)
        gram = mm(cc, bb, NT)
        xdt = (xd * tail_e).astype(BF16)
        dye = (dy * ea_e).astype(BF16)
        y_in = mm(cc, h_in) * ea_e
        dxd_in = mm(bb, hb_low) * tail_e
        dcc = mm(dye, h_in, NT)
        dbb = mm(xdt, hb_low, NT)
        dgram = jnp.zeros((L, L), F32)
        inside = []
        crossing = jnp.zeros((L, 128), F32)
        for pair in range(4):
            sl = slice(128 * pair, 128 * pair + 128)
            xp = xd[:, sl].astype(BF16)
            dyp = dy[:, sl]
            decs, mixes, parts = [], [], []
            for half in range(2):
                h = 2 * pair + half
                dec = jnp.exp(cu[:, h : h + 1] - cut[h : h + 1, :] + off)
                decs.append(dec)
                mixes.append(gram * dec)
                parts.append(jnp.where(first_half == (half == 0), dyp, 0.0).astype(BF16))
            dy2 = jnp.concatenate(parts, axis=0)
            dmix = mm(dy2, xp, NT)
            dm0, dm1 = dmix[:L, :], dmix[L:, :]
            dgram = dgram + dm0 * decs[0] + dm1 * decs[1]
            inside.append(mm(jnp.concatenate([mixes[0].astype(BF16), mixes[1].astype(BF16)], axis=0), dy2, TN))
            both = jnp.concatenate([(mixes[0] * dm0).astype(BF16), (mixes[1] * dm1).astype(BF16)], axis=1)
            cross = mm(upper_low, both)
            c0 = (cross[:, :L] * strict).astype(BF16)
            c1 = (cross[:, L:] * strict).astype(BF16)
            pick = jnp.concatenate(
                [(lanes == 2 * pair).astype(BF16), (lanes == 2 * pair + 1).astype(BF16)], axis=0
            )
            crossing = crossing + mm(jnp.concatenate([c0, c1], axis=1), pick)
        dgl = dgram.astype(BF16)
        dcc = dcc + mm(dgl, bb)
        dbb = dbb + mm(dgl, cc, TN)
        dxd = jnp.concatenate(inside, axis=1) + dxd_in
        kept = mm_split(jnp.broadcast_to(jnp.sum(h_in.astype(F32) * h_back, axis=0, keepdims=True), (8, CH)), collect)
        kept = kept[0:1, :] * ea[L - 1 : L, :]
        p_in = mm_split(dy * y_in, collect)
        q_in = mm_split(xd * dxd_in, collect)
        dls = crossing + mm_split_right(upper_low, p_in) + mm_split_right(strict_low, q_in) + kept
        dstate[...] = h_back * ea_e[L - 1 : L, :] + mm(cc, dye, TN)
        dst = dls * rate + mm_split(dxd * xs, collect)
        dv = jnp.where(lanes < 8, dst * jax.nn.sigmoid(v), 0.0)
        dproj[rows, S0 - 512 : S0 - 384] = dv.astype(BF16)
        gdt[...] += fold(dv)
        gdl[...] += fold(dls * st)
        dxs = dy * skip + dxd * st_e
        dcx[rows, :] = dxs * (sx * (1.0 + cx - xs))
        dcbc[rows, :] = jnp.concatenate([dbb, dcc], axis=1) * (sbc * (1.0 + cbc - cbc * sbc))
        return carry

    lax.fori_loop(0, NB, block, 0)

    dcx[T : T + 8, :] = jnp.zeros((8, CH), F32)
    dcbc[T : T + 8, :] = jnp.zeros((8, 256), F32)
    padx[0:8, :] = jnp.zeros((8, CH), F32)
    padx[8 : 8 + T, :] = px_ref[...]
    padbc[0:8, :] = jnp.zeros((8, 256), F32)
    padbc[8 : 8 + T, :] = pbc_ref[...]
    sg_ref[...] = jnp.zeros((16, CH), F32)

    def conv_back(width, first_row, bias_row, dc, pad, start):
        for j in range(width // 128):
            cols = slice(128 * j, 128 * j + 128)
            bias = jnp.zeros((8, 128), F32)
            taps = [jnp.zeros((8, 128), F32) for _ in range(4)]
            for b in range(NB):
                d = dc[b * L : b * L + L, cols]
                bias = bias + fold(d)
                total = jnp.zeros((L, 128), F32)
                for k in range(4):
                    taps[k] = taps[k] + fold(d * pad[5 + k + b * L : 5 + k + b * L + L, cols])
                    total = total + par(first_row + k, 128 * j, 128) * dc[b * L + 3 - k : b * L + 3 - k + L, cols]
                dproj[b * L : b * L + L, start + 128 * j : start + 128 * j + 128] = total.astype(BF16)
            sg_ref[bias_row : bias_row + 1, cols] = jnp.sum(bias, axis=0, keepdims=True)
            for k in range(4):
                sg_ref[first_row + k : first_row + k + 1, cols] = jnp.sum(taps[k], axis=0, keepdims=True)

    conv_back(CH, 0, 4, dcx, padx, X0)
    conv_back(256, 9, 13, dcbc, padbc, B0 - 512)
    sg_ref[5:6, :] = jnp.sum(ggo[...], axis=0, keepdims=True)
    sg_ref[8:9, 0:128] = jnp.sum(gdt[...], axis=0, keepdims=True)
    sg_ref[8:9, 128:256] = jnp.sum(gdl[...], axis=0, keepdims=True) * rate
    gs = mm_split(jnp.broadcast_to(jnp.sum(gsk[...], axis=0, keepdims=True), (8, CH)), collect)
    sg_ref[8:9, 256:384] = gs[0:1, :]

    for j in range(4):
        nt = n_ref[:, 256 * j : 256 * j + 256].T
        gt = gb_ref[:, 256 * j : 256 * j + 256].T
        wr = slice(4 * j, 4 * j + 4)
        for c in range(4):
            dw_ref[wr, :, 256 * c : 256 * c + 256] = (
                mm(nt, dproj[:, 256 * c : 256 * c + 256]).astype(BF16).reshape(4, 64, 256)
            )
        dw_ref[wr, :, B0:S0] = mm(nt, dproj[:, B0 - 512 : S0 - 512]).astype(BF16).reshape(4, 64, 256)
        dw_ref[wr, :, S0:COLS] = mm(nt, dproj[:, S0 - 512 : COLS - 512]).astype(BF16).reshape(4, 64, 128)
        for c in range(2):
            dw_ref[wr, :, O0 + 256 * c : O0 + 256 * c + 256] = (
                mm(gt, no_ref[:, 256 * c : 256 * c + 256]).astype(BF16).reshape(4, 64, 256)
            )
        d = mm(dproj[:, 0:1024], w_ref[0, wr, :, 0:1024].reshape(256, 1024), NT)
        d = d + mm(dproj[:, 1024:1408], w_ref[0, wr, :, B0:COLS].reshape(256, 384), NT)
        dn_ref[:, 256 * j : 256 * j + 256] = d.astype(BF16)


def mm_split_right(a, b):
    hi = b.astype(BF16)
    lo = (b - hi.astype(F32)).astype(BF16)
    return mm(a, hi) + mm(a, lo)


def sds(shape, dtype):
    return jax.ShapeDtypeStruct(shape, dtype)


VM = pl.BlockSpec(memory_space=pltpu.VMEM)


def saved_shapes():
    return [
        sds((T, D), BF16),
        sds((T, CH), F32),
        sds((T, CH), F32),
        sds((T, CH), F32),
        sds((T, 256), F32),
        sds((T, 256), F32),
        sds((T, 128), F32),
        sds((T, CH), F32),
        sds((NB, NST, CH), BF16),
    ]


def layer_spec(k, shape):
    rest = (0,) * (len(shape) - 1)
    return pl.BlockSpec((1,) + shape[1:], lambda i: (k,) + rest)


def whole(shape):
    zeros = (0,) * len(shape)
    return pl.BlockSpec(shape, lambda i: zeros)


def forward(k, u, weights, params, cot=None, length=None):
    second = k == 1
    ins = [u, weights, params]
    specs = [whole(u.shape), layer_spec(k, weights.shape), layer_spec(k, params.shape)]
    outs = [sds((T, D), BF16), sds((8, 128), F32)] + saved_shapes()
    if second:
        ins = [length] + ins + [cot]
        specs = [pl.BlockSpec(memory_space=pltpu.SMEM)] + specs + [whole(cot.shape)]
        outs += [sds((T, D), BF16), sds((T, CH), F32)]
    return pl.pallas_call(
        functools.partial(fwd_kernel, second),
        grid=(1,),
        out_shape=outs,
        in_specs=specs,
        out_specs=[whole(o.shape) for o in outs],
        scratch_shapes=[
            pltpu.VMEM((T + 8, CH), F32),
            pltpu.VMEM((T + 8, 256), F32),
            pltpu.VMEM((NST, CH), F32),
            pltpu.VMEM((8, 128), F32),
            pltpu.VMEM((8, 128), F32),
            pltpu.VMEM((T, CH), BF16),
        ],
        compiler_params=pltpu.CompilerParams(vmem_limit_bytes=VMEM_LIMIT),
    )(*ins)


def backward(k, gb, weights, params, sums, saved, dno=None):
    second = k == 1
    ins = [gb, weights, params, sums] + list(saved)
    if second:
        ins += [dno]
    specs = [whole(a.shape) for a in ins]
    specs[1] = layer_spec(k, weights.shape)
    specs[2] = layer_spec(k, params.shape)
    outs = [sds((T, D), BF16), sds((16, 64, COLS), BF16), sds((16, CH), F32)]
    return pl.pallas_call(
        functools.partial(bwd_kernel, second),
        grid=(1,),
        out_shape=outs,
        in_specs=specs,
        out_specs=[whole(o.shape) for o in outs],
        scratch_shapes=[
            pltpu.VMEM((T + 8, CH), F32),
            pltpu.VMEM((T + 8, 256), F32),
            pltpu.VMEM((T + 8, CH), F32),
            pltpu.VMEM((T + 8, 256), F32),
            pltpu.VMEM((T, 1408), BF16),
            pltpu.VMEM((T, CH), BF16),
            pltpu.VMEM((NST, CH), F32),
            pltpu.VMEM((8, CH), F32),
            pltpu.VMEM((8, CH), F32),
            pltpu.VMEM((8, 128), F32),
            pltpu.VMEM((8, 128), F32),
        ],
        compiler_params=pltpu.CompilerParams(vmem_limit_bytes=VMEM_LIMIT),
    )(*ins)


MESH = pl.DeviceIdType.MESH
ROWS = 128
HALF = 32


def places():
    group = lax.axis_index("dp")
    return lax.axis_index("section"), group // 4, lax.rem(group, 4), lax.axis_index("tensor")


def x_peer(j):
    return {"tensor": lax.rem(lax.axis_index("tensor") + j, 4)}


def y_peer(j):
    _, z, y, _ = places()
    return {"dp": z * 4 + lax.rem(y + j, 4)}


def z_peer(j):
    _, z, y, _ = places()
    return {"dp": lax.rem(z + j, 4) * 4 + y}


def twin():
    return {"section": 1 - lax.axis_index("section")}


ORDER = (1, 3, 2)


def greet(peers):
    barrier = pltpu.get_barrier_semaphore()
    for peer in peers:
        pl.semaphore_signal(barrier, inc=1, device_id=peer, device_id_type=MESH)
    pl.semaphore_wait(barrier, len(peers))


class Sender:
    def __init__(self, send_sems, recv_sems):
        self.send_sems, self.recv_sems, self.copies, self.done = send_sems, recv_sems, [], []

    def __call__(self, src, dst, peer):
        i = len(self.copies)
        copy = pltpu.make_async_remote_copy(
            src_ref=src,
            dst_ref=dst,
            send_sem=self.send_sems.at[i],
            recv_sem=self.recv_sems.at[i],
            device_id=peer,
            device_id_type=MESH,
        )
        copy.start()
        self.copies.append(copy)
        return copy

    def drain(self, copies):
        for copy in copies:
            copy.wait_send()
            self.done.append(copy)

    def finish(self):
        for copy in self.copies:
            if all(copy is not other for other in self.done):
                copy.wait_send()


def own_rows(t):
    return pl.ds(pl.multiple_of(t * ROWS, ROWS), ROWS)


def gather_kernel(wx, wz, wo, wb, par, tok, cot, wall, tok_all, cot_all, par_all, own, bc_in, par_in, lsem, ss, rs):
    s, z, y, t = places()
    d = z * 4 + y
    greet([x_peer(j) for j in ORDER] + [y_peer(j) for j in ORDER] + [z_peer(j) for j in ORDER] + [twin()])
    send = Sender(ss, rs)
    early = []
    for j in ORDER:
        early.append(send(wb, bc_in.at[j], x_peer(j)))
        early.append(send(par, par_in.at[j], x_peer(j)))
    rows = own_rows(t)
    late = []
    for j in ORDER:
        late.append(send(tok.at[s], tok_all.at[rows], x_peer(j)))
    local = [
        pltpu.make_async_copy(tok.at[s], tok_all.at[rows], lsem.at[0]),
        pltpu.make_async_copy(cot.at[s], cot_all.at[rows], lsem.at[1]),
    ]
    for copy in local:
        copy.start()
    bc_in[0] = wb[...]
    par_in[0] = par[...]
    own[:, X0:Z0] = wx[...]
    own[:, Z0:O0] = wz[...]
    own[:, O0:B0] = wo[...]
    for copy in early:
        copy.wait_recv()

    left = iota((64, 128), 1) < 64
    pieces = [bc_in[lax.rem(t - i + 4, 4)].astype(F32) for i in range(4)]
    for i in range(2):
        pair = jnp.where(left, pieces[2 * i], pltpu.roll(pieces[2 * i + 1], 64, 1))
        own[:, B0 + 128 * i : B0 + 128 * i + 128] = pair.astype(BF16)
    steps = pltpu.roll(wb[...].astype(F32), 64, 1)
    own[:, S0:COLS] = jnp.where(iota((64, 128), 1) < 8, steps, 0.0).astype(BF16)
    kept = par[...]
    lanes = iota((16, 128), 1)
    row = iota((16, 128), 0)
    bc_rows = (row >= 9) & (row < 14)
    small = [par_in[lax.rem(t - i + 4, 4), :, 0:128] for i in range(4)]
    for i in range(2):
        pair = jnp.where(lanes < 64, small[2 * i], pltpu.roll(small[2 * i + 1], 64, 1))
        par_all[s, :, 128 * i : 128 * i + 128] = jnp.where(bc_rows, pair, kept[:, 128 * i : 128 * i + 128])
    par_all[s, :, 256:512] = kept[:, 256:512]

    first = []
    for j in ORDER:
        first.append(send(own.at[pl.ds(0, HALF)], wall.at[s, d, pl.ds(0, HALF)], y_peer(j)))
        first.append(send(own.at[pl.ds(HALF, HALF)], wall.at[s, d, pl.ds(HALF, HALF)], z_peer(j)))
    mine = pltpu.make_async_copy(own, wall.at[s, d], lsem.at[2])
    mine.start()
    across = [send(par_all.at[s], par_all.at[s], twin())]
    for j in ORDER:
        late.append(send(cot.at[s], cot_all.at[rows], x_peer(j)))
    for copy in first:
        copy.wait_recv()
    mine.wait()
    grid = wall.reshape(2, 4, 4, 64, COLS)
    upper = grid.at[s, z, :, pl.ds(0, HALF)]
    lower = grid.at[s, :, y, pl.ds(HALF, HALF)]
    second = []
    for j in ORDER:
        second.append(send(upper, upper, z_peer(j)))
        second.append(send(lower, lower, y_peer(j)))
    across.append(send(upper, upper, twin()))
    across.append(send(lower, lower, twin()))
    for i, j in enumerate(ORDER):
        second[2 * i].wait_recv()
        got = grid.at[s, lax.rem(z - j + 4, 4), :, pl.ds(0, HALF)]
        across.append(send(got, got, twin()))
        second[2 * i + 1].wait_recv()
        got = grid.at[s, :, lax.rem(y - j + 4, 4), pl.ds(HALF, HALF)]
        across.append(send(got, got, twin()))
    for copy in across + late:
        copy.wait_recv()
    for copy in local:
        copy.wait()
    send.finish()


def hidden_kernel(p, sq, tok, lens, hid_all, ptot, sums, p_in, sq_in, ss, rs):
    s, _, _, t = places()
    greet([x_peer(j) for j in ORDER])
    send = Sender(ss, rs)
    inner = []
    for j in ORDER:
        inner.append(send(sq, sq_in.at[j], x_peer(j)))
    for j in ORDER:
        inner.append(send(p.at[own_rows(lax.rem(t + j, 4))], p_in.at[j], x_peer(j)))
    for copy in inner:
        copy.wait_recv()
    rows = own_rows(t)
    sums[...] = sq[...] + sq_in[1] + sq_in[2] + sq_in[3]
    factor = as_column(lax.rsqrt(sums[pl.ds(t, 1), :] / INNER + EPS))
    length = lens[pl.ds(s, 1), :]
    mask = (iota((ROWS, 1), 0) + t * ROWS < length).astype(F32)
    total = p[rows, :].astype(F32) + p_in[1].astype(F32) + p_in[2].astype(F32) + p_in[3].astype(F32)
    ptot[...] = total
    hid_all[rows, :] = (mask * (tok[s].astype(F32) + factor * total)).astype(BF16)
    outer = [send(hid_all.at[rows], hid_all.at[rows], x_peer(j)) for j in ORDER]
    for copy in outer:
        copy.wait_recv()
    send.finish()


def sums_kernel(sq, sums, sq_in, ss, rs):
    greet([x_peer(j) for j in ORDER])
    send = Sender(ss, rs)
    for j in ORDER:
        send(sq, sq_in.at[j], x_peer(j))
    for copy in send.copies:
        copy.wait_recv()
    sums[...] = sq[...] + sq_in[1] + sq_in[2] + sq_in[3]
    send.finish()


def input_grad(total, u, gain, upstream):
    r = lax.rsqrt(jnp.mean(u * u, axis=-1, keepdims=True) + EPS)
    b = total * gain
    back = upstream + r * b - u * (r * r * r * (1.0 / D)) * jnp.sum(b * u, axis=-1, keepdims=True)
    return back, jnp.sum(total * (u * r), axis=0, keepdims=True)


def turn_kernel(
    dn, p, sq, hid, par, cot, lens, ptot, sums0, gb_all, sums, back_rows, fin_rows, ggi, dn_in, p_in, s_in, ss, rs
):
    s, _, _, t = places()
    greet([x_peer(j) for j in ORDER])
    send = Sender(ss, rs)
    inner = [send(dn.at[own_rows(lax.rem(t + j, 4))], dn_in.at[j], x_peer(j)) for j in ORDER]
    outer = [send(p.at[own_rows(lax.rem(t + j, 4))], p_in.at[j], x_peer(j)) for j in ORDER]
    rows = own_rows(t)
    length = lens[pl.ds(s, 1), :]
    mask = (iota((ROWS, 1), 0) + t * ROWS < length).astype(F32)
    u = hid[rows, :].astype(F32)
    gain = jnp.concatenate([par[1, 6:7, :], par[1, 7:8, :]], axis=1)
    for copy in inner:
        copy.wait_recv()
    total = dn[rows, :].astype(F32) + dn_in[1].astype(F32) + dn_in[2].astype(F32) + dn_in[3].astype(F32)
    back, gain_grad = input_grad(total, u, gain, mask * cot[s].astype(F32))
    back_rows[...] = back
    ggi[...] = jnp.broadcast_to(gain_grad, (8, D))
    low = (mask * back.astype(BF16).astype(F32)).astype(BF16)
    gb_all[rows, :] = low
    spread = [send(gb_all.at[rows], gb_all.at[rows], x_peer(j)) for j in ORDER]
    inner_row = as_row(jnp.sum(low.astype(F32) * ptot[...], axis=-1, keepdims=True))
    s_in[0] = jnp.broadcast_to(inner_row, (8, 128))
    spread += [send(s_in.at[0], s_in.at[j], x_peer(j)) for j in ORDER]
    for copy in outer:
        copy.wait_recv()
    factor = as_column(lax.rsqrt(sq[pl.ds(t, 1), :] / INNER + EPS))
    total = p[rows, :].astype(F32) + p_in[1].astype(F32) + p_in[2].astype(F32) + p_in[3].astype(F32)
    fin_rows[...] = (mask * (u + factor * total)).astype(BF16)
    for copy in spread:
        copy.wait_recv()
    sums[0:4, :] = sums0[0:4, :]
    for j in range(4):
        sums[pl.ds(4 + lax.rem(t - j + 4, 4), 1), :] = s_in[j, 0:1, :]
    send.finish()


def reduce_kernel(
    dw0, dw1, dn, sg0, sg1, ggi1, tok, par, gb, back, fin, hid,
    lo, ig, o_gi, o_wx, o_wz, o_bc, o_dt, o_cx, o_cb, o_bx, o_bb, o_db, o_dl, o_sk, o_go, o_wo,
    mine, theirs, up_in, low_in, up_mid, low_mid, up_last, low_last, dn_in, own_grad, pack, pack_in, result, bcs, bcs_in,
    lsem, ss, rs,
):
    s, z, y, t = places()
    greet([x_peer(j) for j in ORDER] + [y_peer(j) for j in ORDER] + [z_peer(j) for j in ORDER] + [twin()])
    send = Sender(ss, rs)
    rows = own_rows(t)

    def switched(first, second, dst):
        i = len(send.copies)
        pair = [
            pltpu.make_async_remote_copy(
                src_ref=src, dst_ref=dst, send_sem=ss.at[i], recv_sem=rs.at[i], device_id=twin(), device_id_type=MESH
            )
            for src in (first, second)
        ]
        pl.when(s == 0)(pair[1].start)
        pl.when(s == 1)(pair[0].start)
        send.copies.append(pair[0])
        return pair[0]

    def kept(first, second, dst, i):
        pair = [pltpu.make_async_copy(src, dst, lsem.at[i]) for src in (first, second)]
        pl.when(s == 0)(pair[0].start)
        pl.when(s == 1)(pair[1].start)
        return pair[0]

    swap = switched(dw0, dw1, theirs)
    load = kept(dw0, dw1, mine, 0)
    inner = [send(dn.at[own_rows(lax.rem(t + j, 4))], dn_in.at[j], x_peer(j)) for j in ORDER]
    others = [switched(hid.at[rows], fin, lo.at[s])]
    keeps = [kept(hid.at[rows], fin, lo.at[s], 1)]

    for copy in inner:
        copy.wait_recv()
    u = tok[s].astype(F32)
    gain = jnp.concatenate([par[0, 6:7, :], par[0, 7:8, :]], axis=1)
    total = dn[rows, :].astype(F32) + dn_in[1].astype(F32) + dn_in[2].astype(F32) + dn_in[3].astype(F32)
    grad, gain_grad = input_grad(total, u, gain, gb[rows, :].astype(F32))
    own_grad[...] = grad
    others.append(switched(own_grad, back, ig.at[s]))
    keeps.append(kept(own_grad, back, ig.at[s], 2))
    for k, (sg, gg) in enumerate(((sg0, gain_grad), (sg1, ggi1[0:1, :]))):
        pack[k] = sg[...]
        pack[k, 6:7, :] = gg[:, 0:CH]
        pack[k, 7:8, :] = gg[:, CH:D]
    small = send(pack.at[1 - s], pack_in.at[0], twin())

    load.wait()
    swap.wait_recv()

    def add_twin(i, carry):
        mine[i] = (mine[i].astype(F32) + theirs[i].astype(F32)).astype(BF16)
        return carry

    lax.fori_loop(0, 16, add_twin, 0)
    grid = mine.reshape(4, 4, 64, COLS)
    first = []
    for j in ORDER:
        first.append(send(grid.at[:, lax.rem(y + j, 4), pl.ds(0, HALF)], up_in.at[j], y_peer(j)))
        first.append(send(grid.at[lax.rem(z + j, 4), :, pl.ds(HALF, HALF)], low_in.at[j], z_peer(j)))
    small.wait_recv()
    result[...] = pack[s] + pack_in[0]
    around = [send(result, pack_in.at[j], y_peer(j)) for j in ORDER]
    for copy in first:
        copy.wait_recv()
    up_own = mine.reshape(4, 4, 64, COLS)

    def add_first(i, carry):
        a = up_own[i, y, 0:HALF, :].astype(F32)
        b = up_own[z, i, HALF:64, :].astype(F32)
        for j in (1, 2, 3):
            a = a + up_in[j, i].astype(F32)
            b = b + low_in[j, i].astype(F32)
        up_mid[i] = a.astype(BF16)
        low_mid[i] = b.astype(BF16)
        return carry

    lax.fori_loop(0, 4, add_first, 0)
    second = []
    for j in ORDER:
        second.append(send(up_mid.at[lax.rem(z + j, 4)], up_last.at[j], z_peer(j)))
        second.append(send(low_mid.at[lax.rem(y + j, 4)], low_last.at[j], y_peer(j)))
    for copy in around:
        copy.wait_recv()
    send.drain(around)
    result[...] = result[...] + pack_in[1] + pack_in[2] + pack_in[3]
    around2 = [send(result, pack_in.at[3 + j], z_peer(j)) for j in ORDER]
    for copy in second:
        copy.wait_recv()
    up = up_mid[z].astype(F32) + up_last[1].astype(F32) + up_last[2].astype(F32) + up_last[3].astype(F32)
    low = low_mid[y].astype(F32) + low_last[1].astype(F32) + low_last[2].astype(F32) + low_last[3].astype(F32)
    for half, part in ((0, up), (HALF, low)):
        for i in range(2):
            bcs[i, half : half + HALF, :] = part[:, B0 + 128 * i : B0 + 128 * i + 128]
    last = [send(bcs.at[lax.rem(t + j, 4) // 2], bcs_in.at[j], x_peer(j)) for j in ORDER]
    for copy in around2:
        copy.wait_recv()
    send.drain(around2)
    result[...] = result[...] + pack_in[4] + pack_in[5] + pack_in[6]
    around3 = [send(result, pack_in.at[6 + j], x_peer(j)) for j in ORDER]
    for half, part in ((0, up), (HALF, low)):
        o_wx[half : half + HALF, :] = part[:, X0:Z0]
        o_wz[half : half + HALF, :] = part[:, Z0:O0]
        o_dt[half : half + HALF, :] = part[:, S0 : S0 + 8]
    out_part = jnp.concatenate([up[:, O0:B0], low[:, O0:B0]], axis=0)
    o_wo[...] = jnp.concatenate([out_part, out_part], axis=0).T[:, 0:64]
    o_cx[...] = result[0:4, :]
    o_bx[...] = result[4:5, :]
    o_go[...] = result[5:6, :]
    o_db[...] = result[8:9, 0:8]
    o_dl[...] = result[8:9, 128:136]
    o_sk[...] = result[8:9, 256:264]
    for copy in last:
        copy.wait_recv()
    block = bcs[t // 2] + bcs_in[1] + bcs_in[2] + bcs_in[3]
    o_bc[...] = jnp.where(lax.rem(t, 2) == 0, block[:, 0:64], block[:, 64:128])
    for copy in around3:
        copy.wait_recv()
    whole_sum = result[...] + pack_in[7] + pack_in[8] + pack_in[9]
    o_gi[...] = jnp.concatenate([whole_sum[6:7, :], whole_sum[7:8, :]], axis=1)
    chosen = whole_sum[8:16, 0:64]
    for i in range(1, 4):
        chosen = jnp.where(t == i, whole_sum[8:16, 64 * i : 64 * i + 64], chosen)
    o_cb[...] = chosen[1:5, :]
    o_bb[...] = chosen[5:6, :]
    for copy in others:
        copy.wait_recv()
    for copy in keeps:
        copy.wait()
    send.finish()


ANY = pl.BlockSpec(memory_space=pl.ANY)


def talk(kernel, number, ins, in_specs, outs, out_specs, scratch, copies, locals_=0):
    sems = ([pltpu.SemaphoreType.DMA((locals_,))] if locals_ else []) + [pltpu.SemaphoreType.DMA((copies,))] * 2
    return pl.pallas_call(
        kernel,
        out_shape=outs,
        in_specs=in_specs,
        out_specs=out_specs,
        scratch_shapes=list(scratch) + sems,
        compiler_params=pltpu.CompilerParams(
            collective_id=number, has_side_effects=True, vmem_limit_bytes=VMEM_LIMIT
        ),
    )(*ins)


def body(
    tokens_in, cotangent, seq_lengths, gain_in, weight_x, weight_z, weight_bc, weight_dt, conv_x, conv_bc,
    bias_x, bias_bc, dt_bias, decay_log, skip_gain, gain_out, weight_out,
):
    def wide(a, left, right):
        return jnp.pad(a, ((0, 0), (left, right)))

    heads = jnp.concatenate(
        [wide(dt_bias, 0, 120), wide(decay_log, 0, 120), wide(skip_gain, 0, 120 + 128)], axis=1
    )
    par = jnp.concatenate(
        [
            conv_x[0],
            bias_x,
            gain_out,
            gain_in.reshape(2, CH),
            heads,
            wide(conv_bc[0], 0, CH - 64),
            wide(bias_bc, 0, CH - 64),
            jnp.zeros((2, CH), F32),
        ],
        axis=0,
    )
    wb = jnp.concatenate([weight_bc[0], weight_dt[0], jnp.zeros((64, 56), BF16)], axis=1)
    wall, tok_all, cot_all, par_all = talk(
        gather_kernel,
        0,
        [weight_x[0], weight_z[0], weight_out[0].T, wb, par, tokens_in, cotangent],
        [VM] * 5 + [ANY] * 2,
        [sds((2, 16, 64, COLS), BF16), sds((T, D), BF16), sds((T, D), BF16), sds((2, 16, CH), F32)],
        [ANY, ANY, ANY, VM],
        [pltpu.VMEM((64, COLS), BF16), pltpu.VMEM((4, 64, 128), BF16), pltpu.VMEM((4, 16, CH), F32)],
        40,
        3,
    )
    p0, sq0, *saved0 = forward(0, tok_all, wall, par_all)
    hid_all, ptot0, sums0 = talk(
        hidden_kernel,
        1,
        [p0, sq0, tokens_in, seq_lengths],
        [VM] * 4,
        [sds((T, D), BF16), sds((ROWS, D), F32), sds((8, 128), F32)],
        [VM] * 3,
        [pltpu.VMEM((4, ROWS, D), BF16), pltpu.VMEM((4, 8, 128), F32)],
        9,
    )
    length = lax.dynamic_slice_in_dim(seq_lengths, lax.axis_index("section"), 1, 0)
    p1, sq1, *saved1, gb1, dno1 = forward(1, hid_all, wall, par_all, cot_all, length)
    sums1 = talk(
        sums_kernel, 2, [sq1], [VM], sds((8, 128), F32), VM, [pltpu.VMEM((4, 8, 128), F32)], 3
    )
    dn1, dw1, sg1 = backward(1, gb1, wall, par_all, sums1, saved1, dno1)
    gb0, sums0b, back, fin, ggi1 = talk(
        turn_kernel,
        3,
        [dn1, p1, sums1, hid_all, par_all, cotangent, seq_lengths, ptot0, sums0],
        [VM] * 9,
        [sds((T, D), BF16), sds((8, 128), F32), sds((ROWS, D), F32), sds((ROWS, D), BF16), sds((8, D), F32)],
        [VM] * 5,
        [pltpu.VMEM((4, ROWS, D), BF16), pltpu.VMEM((4, ROWS, D), BF16), pltpu.VMEM((4, 8, 128), F32)],
        12,
    )
    dn0, dw0, sg0 = backward(0, gb0, wall, par_all, sums0b, saved0)
    outs = [
        sds((2, ROWS, D), BF16),
        sds((2, ROWS, D), F32),
        sds((1, D), F32),
        sds((64, CH), F32),
        sds((64, CH), F32),
        sds((64, 64), F32),
        sds((64, 8), F32),
        sds((4, CH), F32),
        sds((4, 64), F32),
        sds((1, CH), F32),
        sds((1, 64), F32),
        sds((1, 8), F32),
        sds((1, 8), F32),
        sds((1, 8), F32),
        sds((1, CH), F32),
        sds((CH, 64), F32),
    ]
    found = talk(
        reduce_kernel,
        4,
        [dw0, dw1, dn0, sg0, sg1, ggi1, tokens_in, par_all, gb0, back, fin, hid_all],
        [ANY, ANY] + [VM] * 7 + [ANY, ANY, ANY],
        outs,
        [ANY, ANY] + [VM] * 14,
        [
            pltpu.VMEM((16, 64, COLS), BF16),
            pltpu.VMEM((16, 64, COLS), BF16),
            pltpu.VMEM((4, 4, HALF, COLS), BF16),
            pltpu.VMEM((4, 4, HALF, COLS), BF16),
            pltpu.VMEM((4, HALF, COLS), BF16),
            pltpu.VMEM((4, HALF, COLS), BF16),
            pltpu.VMEM((4, HALF, COLS), BF16),
            pltpu.VMEM((4, HALF, COLS), BF16),
            pltpu.VMEM((4, ROWS, D), BF16),
            pltpu.VMEM((ROWS, D), F32),
            pltpu.VMEM((2, 16, CH), F32),
            pltpu.VMEM((10, 16, CH), F32),
            pltpu.VMEM((16, CH), F32),
            pltpu.VMEM((2, 64, 128), F32),
            pltpu.VMEM((4, 64, 128), F32),
        ],
        32,
        3,
    )
    return tuple(
        a if i in (2, 9, 10, 11, 12, 13, 14) else a[None] for i, a in enumerate(found)
    )


def solution(mesh):
    in_specs = (
        P(None, ("dp", "tensor"), None),
        P(None, ("dp", "tensor"), None),
        P(None, "dp"),
        P("section", None),
        P("section", "dp", "tensor"),
        P("section", "dp", "tensor"),
        P("section", "dp", "tensor"),
        P("section", "dp", "tensor"),
        P("section", None, "tensor"),
        P("section", None, "tensor"),
        P("section", "tensor"),
        P("section", "tensor"),
        P("section", "tensor"),
        P("section", "tensor"),
        P("section", "tensor"),
        P("section", "tensor"),
        P("section", "tensor", "dp"),
    )
    out_specs = (
        P("section", None, ("dp", "tensor"), None),
        P("section", None, ("dp", "tensor"), None),
        P("section", None),
        P("section", "dp", "tensor"),
        P("section", "dp", "tensor"),
        P("section", "dp", "tensor"),
        P("section", "dp", "tensor"),
        P("section", None, "tensor"),
        P("section", None, "tensor"),
        P("section", "tensor"),
        P("section", "tensor"),
        P("section", "tensor"),
        P("section", "tensor"),
        P("section", "tensor"),
        P("section", "tensor"),
        P("section", "tensor", "dp"),
    )
    return jax.shard_map(body, mesh=mesh, in_specs=in_specs, out_specs=out_specs, check_vma=False)
```

```python
import jax
import jax.numpy as jnp
from jax import lax
from jax.experimental import pallas as pl
from jax.experimental.pallas import tpu as pltpu
from jax.sharding import PartitionSpec as P

F32 = jnp.float32
BF16 = jnp.bfloat16
T = 512
L = 128
NB = T // L
D = 1024
CH = 512
INNER = 2048
NST = 128
EPS = 1e-05
X0, Z0, O0, B0, S0, COLS = 0, 512, 1024, 1536, 1792, 1920
VMEM_LIMIT = 60 * 2**20
MESH = pl.DeviceIdType.MESH
ROWS = 128
HALF = 32
ORDER = (1, 3, 2)

NN = (((1,), (0,)), ((), ()))
NT = (((1,), (1,)), ((), ()))
TN = (((0,), (0,)), ((), ()))


def mm(a, b, dims=NN):
    return lax.dot_general(a, b, dims, preferred_element_type=F32)


def mm_exact(a, b):
    return lax.dot_general(a, b, NN, precision=lax.Precision.HIGHEST, preferred_element_type=F32)


def mm_split(a, b):
    hi = a.astype(BF16)
    lo = (a - hi.astype(F32)).astype(BF16)
    return mm(hi, b) + mm(lo, b)


def mm_split_right(a, b):
    hi = b.astype(BF16)
    lo = (b - hi.astype(F32)).astype(BF16)
    return mm(a, hi) + mm(a, lo)


def iota(shape, dim):
    return lax.broadcasted_iota(jnp.int32, shape, dim)


def as_row(column):
    return jnp.broadcast_to(column, (L, 128)).T[0:1, :]


def as_column(row):
    return jnp.broadcast_to(row, (128, L)).T[:, 0:1]


def softplus(v):
    return jnp.maximum(v, 0.0) + jnp.log1p(jnp.exp(-jnp.abs(v)))


def head_spread():
    return (iota((128, CH), 1) // 64 == iota((128, CH), 0)).astype(BF16)


def head_collect():
    return (iota((CH, 128), 0) // 64 == iota((CH, 128), 1)).astype(BF16)


def fold(a):
    return jnp.sum(a.reshape(a.shape[0] // 8, 8, a.shape[1]), axis=0)


def span(start, size):
    return pl.ds(pl.multiple_of(start, size), size)


def places():
    group = lax.axis_index("dp")
    return lax.axis_index("section"), group // 4, lax.rem(group, 4), lax.axis_index("tensor")


def x_peer(j):
    return {"tensor": lax.rem(lax.axis_index("tensor") + j, 4)}


def twin():
    return {"section": 1 - lax.axis_index("section")}


def greet(peers):
    barrier = pltpu.get_barrier_semaphore()
    for peer in peers:
        pl.semaphore_signal(barrier, inc=1, device_id=peer, device_id_type=MESH)
    pl.semaphore_wait(barrier, len(peers))


class Link:
    def __init__(self, send_sems, recv_sems):
        self.send_sems, self.recv_sems = send_sems, recv_sems

    def copy(self, src, dst, at, peer):
        return pltpu.make_async_remote_copy(
            src_ref=src,
            dst_ref=dst,
            send_sem=self.send_sems.at[at],
            recv_sem=self.recv_sems.at[at],
            device_id=peer,
            device_id_type=MESH,
        )

    def start(self, src, dst, at, peer):
        self.copy(src, dst, at, peer).start()

    def arrived(self, like, at):
        self.copy(like, like, at, twin()).wait_recv()

    def sent(self, like, at):
        self.copy(like, like, at, twin()).wait_send()


SCRATCH = dict(
    wall0=((16, 64, COLS), BF16),
    wall1=((16, 64, COLS), BF16),
    dw1=((16, 64, COLS), BF16),
    theirs=((2, 16, HALF, COLS), BF16),
    first_in=((2, 3, 4, HALF, COLS), BF16),
    mid=((2, 4, HALF, COLS), BF16),
    last_in=((2, 4, HALF, COLS), BF16),
    half=((2, HALF, COLS), F32),
    other_half=((HALF, COLS), F32),
    own=((64, COLS), BF16),
    src=((2, HALF, COLS), BF16),
    bc_in=((4, 64, 128), BF16),
    par_own=((16, CH), F32),
    par_in=((4, 16, CH), F32),
    par_all=((2, 16, CH), F32),
    tok=((T, D), BF16),
    hid=((T, D), BF16),
    gb1=((T, D), BF16),
    gb0=((T, D), BF16),
    pa=((T, D), BF16),
    pb=((T, D), BF16),
    pc=((T, D), BF16),
    ra=((NB, 3, HALF, D), BF16),
    rb=((NB, 3, HALF, D), BF16),
    pb_in=((3, ROWS, D), BF16),
    pc_in=((3, ROWS, D), BF16),
    ptot0=((NB, HALF, D), F32),
    sq_tile=((2, NB, 8, 128), F32),
    sq_in=((2, NB, 4, 8, 128), F32),
    sums=((2, NB, 8, 128), F32),
    inner0=((T, 128), F32),
    factors=((ROWS, 128), F32),
    dno=((T, CH), F32),
    blkx=((L + 8, CH), F32),
    blkbc=((L + 8, 256), F32),
    dcx=((L + 8, CH), F32),
    dcbc=((L + 8, 256), F32),
    gate=((T, CH), BF16),
    dproj=((T, 1408), BF16),
    state=((NST, CH), F32),
    ggo=((8, CH), F32),
    gsk=((8, CH), F32),
    gdt=((8, 128), F32),
    gdl=((8, 128), F32),
    tapx=((5, 8, CH), F32),
    tapbc=((5, 8, 256), F32),
    gi1=((8, D), F32),
    pack=((2, 16, CH), F32),
    pack_in=((10, 16, CH), F32),
    bcs=((2, 64, 128), F32),
    bcs_in=((4, 64, 128), F32),
    los=((2, ROWS, D), BF16),
    igs=((2, ROWS, D), F32),
)
SAVED = dict(
    n=((T, D), BF16),
    px=((T + 8, CH), F32),
    cx=((T, CH), F32),
    pz=((T, CH), F32),
    pbc=((T + 8, 256), F32),
    cbc=((T, 256), F32),
    v=((T, 128), F32),
    y=((T, CH), F32),
    h=((NB, NST, CH), BF16),
)
LINKS = dict(
    early=(2, 3),
    toks=(2, 3),
    halves=(1,),
    params=(1,),
    g_first=(2, 3),
    g_second=(2, 4, 3),
    g_twin=(2, 4, 4),
    p0=(NB, 3),
    sq0=(NB, 3),
    hids=(NB, 3),
    sq1=(NB, 3),
    dn1=(NB, 3),
    gbs=(NB, 3),
    in0=(NB, 3),
    p1=(3,),
    dn0=(3,),
    d_twin=(2, 4),
    d_first=(2, 4, 3),
    d_second=(2, 3),
    shard=(1,),
    small=(10,),
    bcx=(3,),
    outs=(2,),
)
INPUTS = (
    "gain_in", "weight_x", "weight_z", "weight_bc", "weight_dt", "conv_x", "conv_bc", "bias_x", "bias_bc", "dt_bias",
    "decay_log", "skip_gain", "gain_out", "weight_out", "lens", "tokens", "cot",
)
OUTPUTS = ("lo", "ig", "shard_out", "small_out")


class Names:
    def __init__(self, **kw):
        self.__dict__.update(kw)


def layer_kernel(*refs):
    names = list(INPUTS) + list(OUTPUTS) + list(SCRATCH)
    names += [f"{n}{k}" for k in range(2) for n in SAVED]
    k_ = Names(**dict(zip(names, refs)))
    rest = refs[len(names) :]
    lsem = rest[0]
    links = Names(**{n: Link(rest[1 + 2 * i], rest[2 + 2 * i]) for i, n in enumerate(LINKS)})
    saved = [Names(**{n: getattr(k_, f"{n}{k}") for n in SAVED}) for k in range(2)]
    walls = (k_.wall0, k_.wall1)
    s, z, y, t = places()
    own_d = z * 4 + y
    a1 = (1 - s) * y + s * z
    a2 = (1 - s) * z + s * y

    def index(first, second):
        return (1 - s) * (4 * second + first) + s * (4 * first + second)

    def first_peer(j):
        return {"dp": index(lax.rem(a1 + j, 4), a2)}

    def second_peer(j):
        return {"dp": index(a1, lax.rem(a2 + j, 4))}

    def x_of(j):
        return lax.rem(t + j, 4)

    my_half = span(HALF * s, HALF)
    twin_half = span(HALF * (1 - s), HALF)

    greet(
        [x_peer(j) for j in ORDER]
        + [first_peer(j) for j in ORDER]
        + [second_peer(j) for j in ORDER]
        + [twin()]
    )

    k_.par_own[...] = jnp.zeros((16, CH), F32)
    k_.par_own[0:4, :] = k_.conv_x[0]
    k_.par_own[4:5, :] = k_.bias_x[...]
    k_.par_own[5:6, :] = k_.gain_out[...]
    k_.par_own[6:7, :] = k_.gain_in[:, 0:CH]
    k_.par_own[7:8, :] = k_.gain_in[:, CH:D]
    k_.par_own[8:9, 0:8] = k_.dt_bias[...]
    k_.par_own[8:9, 128:136] = k_.decay_log[...]
    k_.par_own[8:9, 256:264] = k_.skip_gain[...]
    k_.par_own[9:13, 0:64] = k_.conv_bc[0]
    k_.par_own[13:14, 0:64] = k_.bias_bc[...]
    k_.bc_in[0] = jnp.zeros((64, 128), BF16)
    k_.bc_in[0, :, 0:64] = k_.weight_bc[0]
    for i, j in enumerate(ORDER):
        links.early.start(k_.bc_in.at[0], k_.bc_in.at[j], (0, i), x_peer(j))
        links.early.start(k_.par_own, k_.par_in.at[j], (1, i), x_peer(j))
    rows_t = span(t * ROWS, ROWS)
    for i, j in enumerate(ORDER):
        links.toks.start(k_.tokens.at[s], k_.tok.at[rows_t], (0, i), x_peer(j))
    local_tok = pltpu.make_async_copy(k_.tokens.at[s], k_.tok.at[rows_t], lsem.at[0])
    local_cot = pltpu.make_async_copy(k_.cot.at[s], k_.gb1.at[rows_t], lsem.at[1])
    local_tok.start()
    local_cot.start()
    k_.own[:, X0:Z0] = k_.weight_x[0]
    k_.own[:, Z0:O0] = k_.weight_z[0]
    k_.own[:, O0:B0] = k_.weight_out[0].T
    k_.own[:, S0:COLS] = jnp.zeros((64, 128), BF16)
    k_.own[:, S0 : S0 + 8] = k_.weight_dt[0]
    k_.par_in[0] = k_.par_own[...]
    for i, j in enumerate(ORDER):
        links.early.arrived(k_.bc_in.at[0], (0, i))
        links.early.arrived(k_.par_own, (1, i))
    left = iota((64, 128), 1) < 64
    lanes16 = iota((16, 128), 1)
    row16 = iota((16, 128), 0)
    bc_rows = (row16 >= 9) & (row16 < 14)
    slots = [lax.rem(t - i + 4, 4) for i in range(4)]
    for i in range(2):
        right = pltpu.roll(k_.bc_in[slots[2 * i + 1]].astype(F32), 64, 1)
        k_.own[:, B0 + 128 * i : B0 + 128 * i + 128] = jnp.where(
            left, k_.bc_in[slots[2 * i]].astype(F32), right
        ).astype(BF16)
        right = pltpu.roll(k_.par_in[slots[2 * i + 1], :, 0:128], 64, 1)
        pair = jnp.where(lanes16 < 64, k_.par_in[slots[2 * i], :, 0:128], right)
        cols = slice(128 * i, 128 * i + 128)
        k_.par_all[s, :, cols] = jnp.where(bc_rows, pair, k_.par_own[:, cols])
    k_.par_all[s, :, 256:512] = k_.par_own[:, 256:512]
    links.halves.start(k_.own.at[twin_half], k_.src.at[s], 0, twin())
    links.params.start(k_.par_all.at[s], k_.par_all.at[s], 0, twin())
    k_.src[s] = k_.own[my_half, :]
    links.halves.arrived(k_.src.at[0], 0)

    def gather_first(k):
        for i, j in enumerate(ORDER):
            links.g_first.start(k_.src.at[k], walls[k].at[own_d, my_half], (k, i), first_peer(j))
        walls[k][own_d, my_half, :] = k_.src[k]

    def gather_second(k):
        for r in (0,) + ORDER:
            piece = walls[k].at[index(lax.rem(a1 - r + 4, 4), a2), my_half]
            if r:
                links.g_first.arrived(piece, (k, ORDER.index(r)))
            for i, j in enumerate(ORDER):
                links.g_second.start(piece, piece, (k, r, i), second_peer(j))
            links.g_twin.start(piece, piece, (k, r, 0), twin())

    def gather_twin(k):
        for i, j in enumerate(ORDER):
            for r in (0,) + ORDER:
                piece = walls[k].at[index(lax.rem(a1 - r + 4, 4), lax.rem(a2 - j + 4, 4)), my_half]
                links.g_second.arrived(piece, (k, r, i))
                links.g_twin.start(piece, piece, (k, r, i + 1), twin())

    def gather_done(k):
        for r in range(4):
            for i in range(4):
                links.g_twin.arrived(walls[k].at[0, pl.ds(0, HALF)], (k, r, i))

    def gather_sent(k):
        for r in range(4):
            for i in range(3):
                links.g_second.sent(k_.src.at[0], (k, r, i))
            for i in range(4):
                links.g_twin.sent(k_.src.at[0], (k, r, i))

    gather_first(0)
    links.params.arrived(k_.par_all.at[0], 0)
    for i, j in enumerate(ORDER):
        links.toks.start(k_.cot.at[s], k_.gb1.at[rows_t], (1, i), x_peer(j))
    gather_second(0)

    length = k_.lens[pl.ds(s, 1), :]

    def row_mask(start, rows):
        return (iota((rows, 1), 0) + start < length).astype(F32)

    lower = iota((L, L), 0) >= iota((L, L), 1)
    tri = lower.astype(F32)
    off = jnp.where(lower, 0.0, -1e30)
    first_half = iota((L, 128), 1) < 64
    lanes = iota((L, 128), 1)

    def make_par(k):
        def par(row, start, size):
            return k_.par_all[k, row : row + 1, start : start + size]

        return par

    def weight(k, start, size):
        return walls[k][:, :, start : start + size].reshape(D, size)

    def forward_block(k, b):
        par, keep = make_par(k), saved[k]
        rows = span(b * L, L)
        spread = head_spread()
        rate = -jnp.exp(par(8, 128, 128))
        skip = mm_exact(jnp.broadcast_to(par(8, 256, 128), (8, 128)), spread.astype(F32))[0:1, :]
        n = keep.n[rows, :]
        k_.blkbc[0:8, :] = k_.blkbc[L : L + 8, :]
        k_.blkx[0:8, :] = k_.blkx[L : L + 8, :]
        k_.blkbc[8 : 8 + L, :] = mm(n, weight(k, B0, 256))
        v = mm(n, weight(k, S0, 128)) + par(8, 0, 128)
        keep.v[rows, :] = v
        for j in range(2):
            k_.blkx[8 : 8 + L, 256 * j : 256 * j + 256] = mm(n, weight(k, X0 + 256 * j, 256))
        for j in range(2):
            keep.pz[rows, 256 * j : 256 * j + 256] = mm(n, weight(k, Z0 + 256 * j, 256))
        shifted = pl.ds(pl.multiple_of(b * L + 8, 8), L)
        keep.px[shifted, :] = k_.blkx[8 : 8 + L, :]
        keep.pbc[shifted, :] = k_.blkbc[8 : 8 + L, :]
        for j in range(4):
            cols = slice(128 * j, 128 * j + 128)
            c = par(4, 128 * j, 128)
            for tap in range(4):
                c = c + par(tap, 128 * j, 128) * k_.blkx[5 + tap : 5 + tap + L, cols]
            keep.cx[rows, cols] = c
        for j in range(2):
            cols = slice(128 * j, 128 * j + 128)
            c = par(13, 128 * j, 128)
            for tap in range(4):
                c = c + par(9 + tap, 128 * j, 128) * k_.blkbc[5 + tap : 5 + tap + L, cols]
            keep.cbc[rows, cols] = c
        st = softplus(v)
        cu = mm_exact(tri, st * rate)
        cut = cu.T
        ea = jnp.exp(cu)
        tail = jnp.exp(cu[L - 1 : L, :] - cu)
        st_e = mm_split(st, spread)
        ea_e = mm_split(ea, spread)
        tail_e = mm_split(tail, spread)
        cx = keep.cx[rows, :]
        xs = cx * jax.nn.sigmoid(cx)
        cbc = keep.cbc[rows, :]
        bc = (cbc * jax.nn.sigmoid(cbc)).astype(BF16)
        bb, cc = bc[:, :NST], bc[:, NST:]
        xd = xs * st_e
        h_in = k_.state[...].astype(BF16)
        keep.h[b] = h_in
        gram = mm(cc, bb, NT)
        yy = mm(cc, h_in) * ea_e
        k_.state[...] = k_.state[...] * ea_e[L - 1 : L, :] + mm(bb, (xd * tail_e).astype(BF16), TN)
        inside = []
        for pair in range(4):
            xp = xd[:, 128 * pair : 128 * pair + 128]
            parts, mixes = [], []
            for part in range(2):
                h = 2 * pair + part
                mixes.append((gram * jnp.exp(cu[:, h : h + 1] - cut[h : h + 1, :] + off)).astype(BF16))
                parts.append(jnp.where(first_half == (part == 0), xp, 0.0).astype(BF16))
            inside.append(mm(jnp.concatenate(mixes, axis=1), jnp.concatenate(parts, axis=0)))
        yy = yy + jnp.concatenate(inside, axis=1)
        keep.y[rows, :] = yy
        zz = keep.pz[rows, :]
        gated = (yy + xs * skip) * (zz * jax.nn.sigmoid(zz))
        k_.sq_tile[k, b, 0:1, :] = as_row(jnp.sum(gated * gated, axis=-1, keepdims=True))
        weighted = gated * par(5, 0, CH)
        k_.gate[rows, :] = weighted.astype(BF16)
        if k == 1:
            gb = (k_.gb1[rows, :].astype(F32) * row_mask(b * L, L)).astype(BF16)
            k_.gb1[rows, :] = gb
            dno = jnp.concatenate([mm(gb, weight(k, O0, 256)), mm(gb, weight(k, O0 + 256, 256))], axis=1)
            k_.dno[rows, :] = dno
            k_.sq_tile[k, b, 1:2, :] = as_row(jnp.sum(dno * weighted, axis=-1, keepdims=True))

    def norm_block(k, b, u):
        par = make_par(k)
        gain = jnp.concatenate([par(6, 0, CH), par(7, 0, CH)], axis=1)
        for i in range(4):
            part = span(b * L + 32 * i, 32)
            a = u[part, :].astype(F32)
            r = lax.rsqrt(jnp.mean(a * a, axis=-1, keepdims=True) + EPS)
            saved[k].n[part, :] = (a * r * gain).astype(BF16)

    def reset_forward(k):
        k_.blkx[...] = jnp.zeros((L + 8, CH), F32)
        k_.blkbc[...] = jnp.zeros((L + 8, 256), F32)
        saved[k].px[0:8, :] = jnp.zeros((8, CH), F32)
        saved[k].pbc[0:8, :] = jnp.zeros((8, 256), F32)
        k_.state[...] = jnp.zeros((NST, CH), F32)

    def output_rows(k, rows, dst):
        for j in range(4):
            wo = walls[k][4 * j : 4 * j + 4, :, O0 : O0 + CH].reshape(256, CH)
            dst[rows, 256 * j : 256 * j + 256] = mm(k_.gate[rows, :], wo, NT).astype(BF16)

    def slice_of(b, place):
        return span(b * L + place * HALF, HALF)

    def spread_slices(link, buf, into, b):
        for i, j in enumerate(ORDER):
            link.start(buf.at[slice_of(b, x_of(j))], into.at[b, j - 1], (b, i), x_peer(j))

    def spread_tile(link, k, b):
        for i, j in enumerate(ORDER):
            link.start(k_.sq_tile.at[k, b], k_.sq_in.at[k, b, j], (b, i), x_peer(j))

    def slice_sum(buf, into, b):
        total = buf[slice_of(b, t), :].astype(F32)
        for j in (1, 2, 3):
            total = total + into[b, j - 1].astype(F32)
        return total

    def tile_sum(link, k, b):
        for i, j in enumerate(ORDER):
            link.arrived(k_.sq_in.at[k, b, j], (b, i))
        k_.sums[k, b] = (
            k_.sq_tile[k, b] + k_.sq_in[k, b, 1] + k_.sq_in[k, b, 2] + k_.sq_in[k, b, 3]
        )

    def factor_column(k, b):
        return as_column(lax.rsqrt(k_.sums[k, b, 0:1, :] / INNER + EPS))

    def hidden_block(b):
        tile_sum(links.sq0, 0, b)
        for i, j in enumerate(ORDER):
            links.p0.arrived(k_.ra.at[b, j - 1], (b, i))
        k_.factors[...] = jnp.broadcast_to(factor_column(0, b), (ROWS, 128))
        factor = k_.factors[span(t * HALF, HALF), :][:, 0:1]
        total = slice_sum(k_.pa, k_.ra, b)
        k_.ptot0[b] = total
        rows = slice_of(b, t)
        mask = row_mask(b * L + t * HALF, HALF)
        k_.hid[rows, :] = (mask * (k_.tok[rows, :].astype(F32) + factor * total)).astype(BF16)
        for i, j in enumerate(ORDER):
            links.hids.start(k_.hid.at[rows], k_.hid.at[rows], (b, i), x_peer(j))

    for i, j in enumerate(ORDER):
        links.toks.arrived(k_.tok.at[rows_t], (0, i))
    local_tok.wait()
    for b in range(NB):
        norm_block(0, b, k_.tok)
    reset_forward(0)
    k_.sq_tile[...] = jnp.zeros((2, NB, 8, 128), F32)
    gather_twin(0)
    gather_done(0)
    gather_first(1)

    def first_forward(b, carry):
        pl.when(b == 1)(lambda: gather_second(1))
        pl.when(b >= 2)(lambda: hidden_block(b - 2))
        forward_block(0, b)
        spread_tile(links.sq0, 0, b)
        output_rows(0, span(b * L, L), k_.pa)
        spread_slices(links.p0, k_.pa, k_.ra, b)
        return carry

    lax.fori_loop(0, NB, first_forward, 0)

    gather_twin(1)
    for i, j in enumerate(ORDER):
        links.toks.arrived(k_.gb1.at[rows_t], (1, i))
    local_cot.wait()
    reset_forward(1)
    gather_done(1)

    def second_forward(b, carry):
        pl.when(b < 2)(lambda: hidden_block(b + 2))
        for i, j in enumerate(ORDER):
            links.hids.arrived(k_.hid.at[slice_of(b, 0)], (b, i))
        norm_block(1, b, k_.hid)
        forward_block(1, b)
        spread_tile(links.sq1, 1, b)
        return carry

    lax.fori_loop(0, NB, second_forward, 0)
    output_rows(1, pl.ds(0, T), k_.pb)

    upper_low = (iota((L, L), 1) >= iota((L, L), 0)).astype(BF16)
    strict = (iota((L, L), 1) < iota((L, L), 0)).astype(F32)
    strict_low = strict.astype(BF16)

    def reset_backward():
        k_.state[...] = jnp.zeros((NST, CH), F32)
        k_.ggo[...] = jnp.zeros((8, CH), F32)
        k_.gsk[...] = jnp.zeros((8, CH), F32)
        k_.gdt[...] = jnp.zeros((8, 128), F32)
        k_.gdl[...] = jnp.zeros((8, 128), F32)
        k_.tapx[...] = jnp.zeros((5, 8, CH), F32)
        k_.tapbc[...] = jnp.zeros((5, 8, 256), F32)
        k_.dcx[...] = jnp.zeros((L + 8, CH), F32)
        k_.dcbc[...] = jnp.zeros((L + 8, 256), F32)

    def backward_block(k, b, gb_ref, inner, dn_ref):
        par, keep = make_par(k), saved[k]
        rows = span(b * L, L)
        spread, collect = head_spread(), head_collect()
        rate = -jnp.exp(par(8, 128, 128))
        skip = mm_exact(jnp.broadcast_to(par(8, 256, 128), (8, 128)), spread.astype(F32))[0:1, :]
        gain_out = par(5, 0, CH)
        v = keep.v[rows, :]
        st = softplus(v)
        cu = mm_exact(tri, st * rate)
        cut = cu.T
        ea = jnp.exp(cu)
        tail = jnp.exp(cu[L - 1 : L, :] - cu)
        st_e = mm_split(st, spread)
        ea_e = mm_split(ea, spread)
        tail_e = mm_split(tail, spread)
        cx = keep.cx[rows, :]
        sx = jax.nn.sigmoid(cx)
        xs = cx * sx
        cbc = keep.cbc[rows, :]
        sbc = jax.nn.sigmoid(cbc)
        bc = (cbc * sbc).astype(BF16)
        bb, cc = bc[:, :NST], bc[:, NST:]
        xd = xs * st_e
        factor = factor_column(k, b)
        if k == 1:
            dno = k_.dno[rows, :]
        else:
            gb = gb_ref[rows, :]
            dno = jnp.concatenate([mm(gb, weight(k, O0, 256)), mm(gb, weight(k, O0 + 256, 256))], axis=1)
        out = keep.y[rows, :] + xs * skip
        zz = keep.pz[rows, :]
        sz = jax.nn.sigmoid(zz)
        silu_z = zz * sz
        gated = out * silu_z
        scaled = gated * factor
        k_.gate[rows, :] = (scaled * gain_out).astype(BF16)
        k_.ggo[...] += fold(dno * scaled)
        dgated = factor * (dno * gain_out) - gated * (factor * factor * factor * (1.0 / INNER) * inner)
        dy = dgated * silu_z
        k_.dproj[rows, Z0 : Z0 + CH] = (dgated * out * (sz * (1.0 + zz - silu_z))).astype(BF16)
        k_.gsk[...] += fold(dy * xs)
        h_in = keep.h[b]
        h_back = k_.state[...]
        hb_low = h_back.astype(BF16)
        gram = mm(cc, bb, NT)
        xdt = (xd * tail_e).astype(BF16)
        dye = (dy * ea_e).astype(BF16)
        y_in = mm(cc, h_in) * ea_e
        dxd_in = mm(bb, hb_low) * tail_e
        dcc = mm(dye, h_in, NT)
        dbb = mm(xdt, hb_low, NT)
        dgram = jnp.zeros((L, L), F32)
        inside = []
        crossing = jnp.zeros((L, 128), F32)
        for pair in range(4):
            sl = slice(128 * pair, 128 * pair + 128)
            xp = xd[:, sl].astype(BF16)
            dyp = dy[:, sl]
            decs, mixes, parts = [], [], []
            for part in range(2):
                h = 2 * pair + part
                dec = jnp.exp(cu[:, h : h + 1] - cut[h : h + 1, :] + off)
                decs.append(dec)
                mixes.append(gram * dec)
                parts.append(jnp.where(first_half == (part == 0), dyp, 0.0).astype(BF16))
            dy2 = jnp.concatenate(parts, axis=0)
            dmix = mm(dy2, xp, NT)
            dm0, dm1 = dmix[:L, :], dmix[L:, :]
            dgram = dgram + dm0 * decs[0] + dm1 * decs[1]
            inside.append(mm(jnp.concatenate([mixes[0].astype(BF16), mixes[1].astype(BF16)], axis=0), dy2, TN))
            both = jnp.concatenate([(mixes[0] * dm0).astype(BF16), (mixes[1] * dm1).astype(BF16)], axis=1)
            cross = mm(upper_low, both)
            c0 = (cross[:, :L] * strict).astype(BF16)
            c1 = (cross[:, L:] * strict).astype(BF16)
            pick = jnp.concatenate(
                [(lanes == 2 * pair).astype(BF16), (lanes == 2 * pair + 1).astype(BF16)], axis=0
            )
            crossing = crossing + mm(jnp.concatenate([c0, c1], axis=1), pick)
        dgl = dgram.astype(BF16)
        dcc = dcc + mm(dgl, bb)
        dbb = dbb + mm(dgl, cc, TN)
        dxd = jnp.concatenate(inside, axis=1) + dxd_in
        kept = mm_split(jnp.broadcast_to(jnp.sum(h_in.astype(F32) * h_back, axis=0, keepdims=True), (8, CH)), collect)
        kept = kept[0:1, :] * ea[L - 1 : L, :]
        p_in = mm_split(dy * y_in, collect)
        q_in = mm_split(xd * dxd_in, collect)
        dls = crossing + mm_split_right(upper_low, p_in) + mm_split_right(strict_low, q_in) + kept
        k_.state[...] = h_back * ea_e[L - 1 : L, :] + mm(cc, dye, TN)
        dst = dls * rate + mm_split(dxd * xs, collect)
        dv = jnp.where(lanes < 8, dst * jax.nn.sigmoid(v), 0.0)
        k_.dproj[rows, S0 - 512 : S0 - 384] = dv.astype(BF16)
        k_.gdt[...] += fold(dv)
        k_.gdl[...] += fold(dls * st)
        dxs = dy * skip + dxd * st_e
        k_.dcx[L : L + 8, :] = k_.dcx[0:8, :]
        k_.dcbc[L : L + 8, :] = k_.dcbc[0:8, :]
        k_.dcx[0:L, :] = dxs * (sx * (1.0 + cx - xs))
        k_.dcbc[0:L, :] = jnp.concatenate([dbb, dcc], axis=1) * (sbc * (1.0 + cbc - cbc * sbc))
        window = pl.ds(pl.multiple_of(b * L, 8), L + 8)
        k_.blkx[...] = keep.px[window, :]
        k_.blkbc[...] = keep.pbc[window, :]

        def conv_back(width, first_row, dc, blk, taps, start):
            for j in range(width // 128):
                cols = slice(128 * j, 128 * j + 128)
                d = dc[0:L, cols]
                taps[4, :, cols] += fold(d)
                total = jnp.zeros((L, 128), F32)
                for tap in range(4):
                    taps[tap, :, cols] += fold(d * blk[5 + tap : 5 + tap + L, cols])
                    total = total + par(first_row + tap, 128 * j, 128) * dc[3 - tap : 3 - tap + L, cols]
                k_.dproj[rows, start + 128 * j : start + 128 * j + 128] = total.astype(BF16)

        conv_back(CH, 0, k_.dcx, k_.blkx, k_.tapx, X0)
        conv_back(256, 9, k_.dcbc, k_.blkbc, k_.tapbc, B0 - 512)
        for j in range(4):
            wr = slice(4 * j, 4 * j + 4)
            d = mm(k_.dproj[rows, 0:1024], walls[k][wr, :, 0:1024].reshape(256, 1024), NT)
            d = d + mm(k_.dproj[rows, 1024:1408], walls[k][wr, :, B0:COLS].reshape(256, 384), NT)
            dn_ref[rows, 256 * j : 256 * j + 256] = d.astype(BF16)

    def small_grads(k):
        par = make_par(k)
        rate = -jnp.exp(par(8, 128, 128))
        k_.pack[k] = jnp.zeros((16, CH), F32)
        for tap in range(5):
            k_.pack[k, tap : tap + 1, :] = jnp.sum(k_.tapx[tap], axis=0, keepdims=True)
            k_.pack[k, 9 + tap : 10 + tap, 0:256] = jnp.sum(k_.tapbc[tap], axis=0, keepdims=True)
        k_.pack[k, 5:6, :] = jnp.sum(k_.ggo[...], axis=0, keepdims=True)
        k_.pack[k, 8:9, 0:128] = jnp.sum(k_.gdt[...], axis=0, keepdims=True)
        k_.pack[k, 8:9, 128:256] = jnp.sum(k_.gdl[...], axis=0, keepdims=True) * rate
        gs = mm_split(jnp.broadcast_to(jnp.sum(k_.gsk[...], axis=0, keepdims=True), (8, CH)), head_collect())
        k_.pack[k, 8:9, 256:384] = gs[0:1, :]

    def weight_grads(k, gb_ref, dst):
        for j in range(4):
            nt = saved[k].n[:, 256 * j : 256 * j + 256].T
            gt = gb_ref[:, 256 * j : 256 * j + 256].T
            wr = slice(4 * j, 4 * j + 4)

            def put(start, size, value):
                dst[wr, :, start : start + size] = value.astype(BF16).reshape(4, 64, size)

            for c in range(4):
                put(256 * c, 256, mm(nt, k_.dproj[:, 256 * c : 256 * c + 256]))
            put(B0, 256, mm(nt, k_.dproj[:, B0 - 512 : S0 - 512]))
            put(S0, 128, mm(nt, k_.dproj[:, S0 - 512 : COLS - 512]))
            for c in range(2):
                put(O0 + 256 * c, 256, mm(gt, k_.gate[:, 256 * c : 256 * c + 256]))
            links.d_twin.start(dst.at[wr, twin_half], k_.theirs.at[k, wr], (k, j), twin())

    def input_grad(k, total, u, upstream):
        par = make_par(k)
        gain = jnp.concatenate([par(6, 0, CH), par(7, 0, CH)], axis=1)
        r = lax.rsqrt(jnp.mean(u * u, axis=-1, keepdims=True) + EPS)
        c = total * gain
        back = upstream + r * c - u * (r * r * r * (1.0 / D)) * jnp.sum(c * u, axis=-1, keepdims=True)
        return back, fold(total * (u * r))

    def turn_block(b):
        for i, j in enumerate(ORDER):
            links.dn1.arrived(k_.rb.at[b, j - 1], (b, i))
        rows = slice_of(b, t)
        u = k_.hid[rows, :].astype(F32)
        back, gain_grad = input_grad(1, slice_sum(k_.pc, k_.rb, b), u, k_.gb1[rows, :].astype(F32))
        k_.gi1[...] += gain_grad
        low = (row_mask(b * L + t * HALF, HALF) * back).astype(BF16)
        k_.gb0[rows, :] = low
        inner = jnp.sum(low.astype(F32) * k_.ptot0[b], axis=-1, keepdims=True)
        k_.inner0[rows, :] = jnp.broadcast_to(inner, (HALF, 128))
        for i, j in enumerate(ORDER):
            links.gbs.start(k_.gb0.at[rows], k_.gb0.at[rows], (b, i), x_peer(j))
            links.in0.start(k_.inner0.at[rows], k_.inner0.at[rows], (b, i), x_peer(j))

    def owner_slices(link, buf, into):
        for i, j in enumerate(ORDER):
            link.start(buf.at[span(x_of(j) * ROWS, ROWS)], into.at[j - 1], i, x_peer(j))

    def reduce_first(k, dst):
        for j in range(4):
            links.d_twin.arrived(k_.theirs.at[k, 0:4], (k, j))

        def add(i, carry):
            dst[i, my_half, :] = (dst[i, my_half, :].astype(F32) + k_.theirs[k, i].astype(F32)).astype(BF16)
            return carry

        lax.fori_loop(0, 16, add, 0)
        for i, j in enumerate(ORDER):
            for r in range(4):
                piece = dst.at[index(lax.rem(a1 + j, 4), r), my_half]
                links.d_first.start(piece, k_.first_in.at[k, j - 1, r], (k, r, i), first_peer(j))

    def reduce_second(k, dst):
        for i, j in enumerate(ORDER):
            for r in range(4):
                links.d_first.arrived(k_.first_in.at[k, j - 1, r], (k, r, i))

        def add(r, carry):
            total = dst[index(a1, r), my_half, :].astype(F32)
            for j in (1, 2, 3):
                total = total + k_.first_in[k, j - 1, r].astype(F32)
            k_.mid[k, r] = total.astype(BF16)
            return carry

        lax.fori_loop(0, 4, add, 0)
        for i, j in enumerate(ORDER):
            links.d_second.start(k_.mid.at[k, lax.rem(a2 + j, 4)], k_.last_in.at[k, j], (k, i), second_peer(j))

    def reduce_last(k):
        for i, j in enumerate(ORDER):
            links.d_second.arrived(k_.last_in.at[k, j], (k, i))
        total = k_.mid[k, a2].astype(F32)
        for j in (1, 2, 3):
            total = total + k_.last_in[k, j].astype(F32)
        k_.half[k] = total

    reset_backward()
    k_.gi1[...] = jnp.zeros((8, D), F32)

    def second_backward(i, carry):
        b = NB - 1 - i
        tile_sum(links.sq1, 1, b)
        backward_block(1, b, k_.gb1, as_column(k_.sums[1, b, 1:2, :]), k_.pc)
        spread_slices(links.dn1, k_.pc, k_.rb, b)
        pl.when(i >= 2)(lambda: turn_block(b + 2))
        return carry

    lax.fori_loop(0, NB, second_backward, 0)
    small_grads(1)
    weight_grads(1, k_.gb1, k_.dw1)

    reset_backward()
    for b in range(NB):
        for i in range(3):
            links.p0.sent(k_.ra.at[0, 0], (b, i))

    def first_backward(i, carry):
        b = NB - 1 - i
        pl.when(i < 2)(lambda: turn_block(1 - i))
        pl.when(i == 1)(lambda: reduce_first(1, k_.dw1))
        pl.when(i == 3)(lambda: owner_slices(links.p1, k_.pb, k_.pb_in))
        for q in range(3):
            links.gbs.arrived(k_.gb0.at[slice_of(b, 0)], (b, q))
            links.in0.arrived(k_.inner0.at[slice_of(b, 0)], (b, q))
        inner = k_.inner0[span(b * L, L), :][:, 0:1]
        backward_block(0, b, k_.gb0, inner, k_.pa)
        return carry

    lax.fori_loop(0, NB, first_backward, 0)
    owner_slices(links.dn0, k_.pa, k_.pc_in)
    small_grads(0)
    gather_sent(1)
    weight_grads(0, k_.gb0, k_.wall1)

    reduce_second(1, k_.dw1)
    reduce_first(0, k_.wall1)
    for i, j in enumerate(ORDER):
        links.dn0.arrived(k_.pc_in.at[j - 1], i)
    total = k_.pa[rows_t, :].astype(F32)
    for j in (1, 2, 3):
        total = total + k_.pc_in[j - 1].astype(F32)
    grad, gain_grad = input_grad(0, total, k_.tok[rows_t, :].astype(F32), k_.gb0[rows_t, :].astype(F32))
    k_.igs[0] = grad
    k_.igs[1] = k_.gb0[rows_t, :].astype(F32)
    for k, part in ((0, gain_grad), (1, k_.gi1[...])):
        part = jnp.sum(part, axis=0, keepdims=True)
        k_.pack[k, 6:7, :] = part[:, 0:CH]
        k_.pack[k, 7:8, :] = part[:, CH:D]
    links.small.start(k_.pack.at[1 - s], k_.pack_in.at[0], 0, twin())
    for i, j in enumerate(ORDER):
        links.p1.arrived(k_.pb_in.at[j - 1], i)
    total = k_.pb[rows_t, :].astype(F32)
    for j in (1, 2, 3):
        total = total + k_.pb_in[j - 1].astype(F32)
    mask = row_mask(t * ROWS, ROWS)
    factor = factor_column(1, t)
    k_.los[0] = k_.hid[rows_t, :]
    k_.los[1] = (mask * (k_.hid[rows_t, :].astype(F32) + factor * total)).astype(BF16)
    links.outs.start(k_.los.at[1 - s], k_.lo.at[s], 0, twin())
    links.outs.start(k_.igs.at[1 - s], k_.ig.at[s], 1, twin())
    keep_lo = pltpu.make_async_copy(k_.los.at[s], k_.lo.at[s], lsem.at[2])
    keep_ig = pltpu.make_async_copy(k_.igs.at[s], k_.ig.at[s], lsem.at[3])
    keep_lo.start()
    keep_ig.start()
    reduce_last(1)
    links.small.arrived(k_.pack_in.at[0], 0)
    k_.par_in[0] = k_.pack[s] + k_.pack_in[0]
    for i, j in enumerate(ORDER):
        links.small.start(k_.par_in.at[0], k_.pack_in.at[j], 1 + i, first_peer(j))
    reduce_second(0, k_.wall1)

    def small_step(src, dst, first, peers):
        for i, j in enumerate(ORDER):
            links.small.arrived(k_.pack_in.at[j], first + i)
        k_.par_in[dst] = (
            k_.par_in[src] + k_.pack_in[first] + k_.pack_in[first + 1] + k_.pack_in[first + 2]
        )
        if peers is not None:
            for i, j in enumerate(ORDER):
                links.small.start(k_.par_in.at[dst], k_.pack_in.at[first + 2 + j], first + 3 + i, peers(j))

    small_step(0, 1, 1, second_peer)
    reduce_last(0)
    links.shard.start(k_.half.at[1 - s], k_.other_half, 0, twin())
    small_step(1, 2, 4, x_peer)
    links.shard.arrived(k_.other_half, 0)
    mine, others = k_.half[s], k_.other_half[...]
    k_.shard_out[my_half, :] = mine
    k_.shard_out[twin_half, :] = others
    for i in range(2):
        k_.bcs[i, my_half, :] = mine[:, B0 + 128 * i : B0 + 128 * i + 128]
        k_.bcs[i, twin_half, :] = others[:, B0 + 128 * i : B0 + 128 * i + 128]
    for i, j in enumerate(ORDER):
        links.bcx.start(k_.bcs.at[x_of(j) // 2], k_.bcs_in.at[j], i, x_peer(j))
    for i, j in enumerate(ORDER):
        links.small.arrived(k_.pack_in.at[j], 7 + i)
    over_x = k_.par_in[2] + k_.pack_in[7] + k_.pack_in[8] + k_.pack_in[9]
    row = iota((16, CH), 0)
    shared = (row == 6) | (row == 7) | (row >= 9)
    over_x = jnp.where(shared, over_x, k_.par_in[2])
    k_.small_out[...] = over_x
    chosen = over_x[8:16, 0:64]
    for i in range(1, 4):
        chosen = jnp.where(t == i, over_x[8:16, 64 * i : 64 * i + 64], chosen)
    k_.small_out[9:14, 0:64] = chosen[1:6, :]
    for i, j in enumerate(ORDER):
        links.bcx.arrived(k_.bcs_in.at[j], i)
    block = k_.bcs[t // 2] + k_.bcs_in[1] + k_.bcs_in[2] + k_.bcs_in[3]
    k_.shard_out[:, B0 : B0 + 64] = jnp.where(lax.rem(t, 2) == 0, block[:, 0:64], block[:, 64:128])

    keep_lo.wait()
    keep_ig.wait()
    links.outs.arrived(k_.los.at[0], 0)
    links.outs.arrived(k_.igs.at[0], 1)
    links.outs.sent(k_.los.at[0], 0)
    links.outs.sent(k_.igs.at[0], 1)
    links.halves.sent(k_.src.at[0], 0)
    links.params.sent(k_.par_all.at[0], 0)
    links.shard.sent(k_.other_half, 0)
    for i in range(10):
        links.small.sent(k_.par_in.at[0], i)
    for i in range(3):
        links.early.sent(k_.bc_in.at[0], (0, i))
        links.early.sent(k_.par_own, (1, i))
        links.toks.sent(k_.tok.at[rows_t], (0, i))
        links.toks.sent(k_.tok.at[rows_t], (1, i))
        links.p1.sent(k_.pb_in.at[0], i)
        links.dn0.sent(k_.pc_in.at[0], i)
        links.bcx.sent(k_.bcs.at[0], i)
        for k in range(2):
            links.g_first.sent(k_.src.at[0], (k, i))
            links.d_second.sent(k_.src.at[0], (k, i))
            for r in range(4):
                links.d_first.sent(k_.src.at[0], (k, r, i))
        for b in range(NB):
            links.sq0.sent(k_.sq_tile.at[0, 0], (b, i))
            links.sq1.sent(k_.sq_tile.at[0, 0], (b, i))
            links.hids.sent(k_.ra.at[0, 0], (b, i))
            links.dn1.sent(k_.ra.at[0, 0], (b, i))
            links.gbs.sent(k_.ra.at[0, 0], (b, i))
            links.in0.sent(k_.inner0.at[pl.ds(0, HALF)], (b, i))
    for k in range(2):
        for r in range(4):
            links.d_twin.sent(k_.theirs.at[0, 0:4], (k, r))
    gather_sent(0)


def unpack_kernel(
    shard, small, lo, ig,
    o_lo, o_ig, o_gi, o_wx, o_wz, o_bc, o_dt, o_cx, o_cb, o_bx, o_bb, o_db, o_dl, o_sk, o_go, o_wo,
):
    o_lo[...] = lo[...]
    o_ig[...] = ig[...]
    o_gi[:, 0:CH] = small[6:7, :]
    o_gi[:, CH:D] = small[7:8, :]
    o_wx[...] = shard[:, X0:Z0]
    o_wz[...] = shard[:, Z0:O0]
    o_bc[...] = shard[:, B0 : B0 + 64]
    o_dt[...] = shard[:, S0 : S0 + 8]
    part = shard[:, O0:B0]
    o_wo[...] = jnp.concatenate([part, part], axis=0).T[:, 0:64]
    o_cx[...] = small[0:4, :]
    o_bx[...] = small[4:5, :]
    o_go[...] = small[5:6, :]
    o_db[...] = small[8:9, 0:8]
    o_dl[...] = small[8:9, 128:136]
    o_sk[...] = small[8:9, 256:264]
    o_cb[...] = small[9:13, 0:64]
    o_bb[...] = small[13:14, 0:64]


def sds(shape, dtype):
    return jax.ShapeDtypeStruct(shape, dtype)


VM = pl.BlockSpec(memory_space=pltpu.VMEM)
ANY = pl.BlockSpec(memory_space=pl.ANY)


def body(
    tokens_in, cotangent, seq_lengths, gain_in, weight_x, weight_z, weight_bc, weight_dt, conv_x, conv_bc,
    bias_x, bias_bc, dt_bias, decay_log, skip_gain, gain_out, weight_out,
):
    ins = [
        gain_in, weight_x, weight_z, weight_bc, weight_dt, conv_x, conv_bc, bias_x, bias_bc, dt_bias, decay_log,
        skip_gain, gain_out, weight_out, seq_lengths, tokens_in, cotangent,
    ]
    scratch = [pltpu.VMEM(*a) for a in SCRATCH.values()]
    scratch += [pltpu.VMEM(*a) for _ in range(2) for a in SAVED.values()]
    scratch += [pltpu.SemaphoreType.DMA((4,))]
    for shape in LINKS.values():
        scratch += [pltpu.SemaphoreType.DMA(shape)] * 2
    lo, ig, shard, small = pl.pallas_call(
        layer_kernel,
        out_shape=[
            sds((2, ROWS, D), BF16),
            sds((2, ROWS, D), F32),
            sds((64, COLS), F32),
            sds((16, CH), F32),
        ],
        in_specs=[VM] * 15 + [ANY] * 2,
        out_specs=[ANY, ANY, VM, VM],
        scratch_shapes=scratch,
        compiler_params=pltpu.CompilerParams(collective_id=0, has_side_effects=True, vmem_limit_bytes=VMEM_LIMIT),
    )(*ins)
    shapes = [
        (2, ROWS, D), (2, ROWS, D), (1, D), (64, CH), (64, CH), (64, 64), (64, 8), (4, CH), (4, 64), (1, CH), (1, 64),
        (1, 8), (1, 8), (1, 8), (1, CH), (CH, 64),
    ]
    found = pl.pallas_call(
        unpack_kernel,
        out_shape=[sds(a, BF16 if i == 0 else F32) for i, a in enumerate(shapes)],
        in_specs=[VM] * 4,
        out_specs=[VM] * 16,
        compiler_params=pltpu.CompilerParams(vmem_limit_bytes=VMEM_LIMIT),
    )(shard, small, lo, ig)
    return tuple(a if i in (2, 9, 10, 11, 12, 13, 14) else a[None] for i, a in enumerate(found))


def solution(mesh):
    in_specs = (
        P(None, ("dp", "tensor"), None),
        P(None, ("dp", "tensor"), None),
        P(None, "dp"),
        P("section", None),
        P("section", "dp", "tensor"),
        P("section", "dp", "tensor"),
        P("section", "dp", "tensor"),
        P("section", "dp", "tensor"),
        P("section", None, "tensor"),
        P("section", None, "tensor"),
        P("section", "tensor"),
        P("section", "tensor"),
        P("section", "tensor"),
        P("section", "tensor"),
        P("section", "tensor"),
        P("section", "tensor"),
        P("section", "tensor", "dp"),
    )
    out_specs = (
        P("section", None, ("dp", "tensor"), None),
        P("section", None, ("dp", "tensor"), None),
        P("section", None),
        P("section", "dp", "tensor"),
        P("section", "dp", "tensor"),
        P("section", "dp", "tensor"),
        P("section", "dp", "tensor"),
        P("section", None, "tensor"),
        P("section", None, "tensor"),
        P("section", "tensor"),
        P("section", "tensor"),
        P("section", "tensor"),
        P("section", "tensor"),
        P("section", "tensor"),
        P("section", "tensor"),
        P("section", "tensor", "dp"),
    )
    return jax.shard_map(body, mesh=mesh, in_specs=in_specs, out_specs=out_specs, check_vma=False)
```

```python
import jax
import jax.numpy as jnp
from jax import lax
from jax.experimental import pallas as pl
from jax.experimental.pallas import tpu as pltpu
from jax.sharding import PartitionSpec as P

F32 = jnp.float32
BF16 = jnp.bfloat16
T = 512
L = 128
NB = T // L
D = 1024
CH = 512
INNER = 2048
NST = 128
EPS = 1e-05
B0, S0, X0, Z0, O0, COLS = 0, 256, 384, 896, 1408, 1920
VMEM_LIMIT = 60 * 2**20
MESH = pl.DeviceIdType.MESH
ROWS = 128
HALF = 32
ORDER = (1, 3, 2)

NN = (((1,), (0,)), ((), ()))
NT = (((1,), (1,)), ((), ()))
TN = (((0,), (0,)), ((), ()))


def mm(a, b, dims=NN):
    return lax.dot_general(a, b, dims, preferred_element_type=F32)


def mm_exact(a, b):
    return lax.dot_general(a, b, NN, precision=lax.Precision.HIGHEST, preferred_element_type=F32)


def mm_split(a, b):
    hi = a.astype(BF16)
    lo = (a - hi.astype(F32)).astype(BF16)
    return mm(hi, b) + mm(lo, b)


def mm_split_right(a, b):
    hi = b.astype(BF16)
    lo = (b - hi.astype(F32)).astype(BF16)
    return mm(a, hi) + mm(a, lo)


def iota(shape, dim):
    return lax.broadcasted_iota(jnp.int32, shape, dim)


def as_row(column):
    return jnp.broadcast_to(column, (L, 128)).T[0:1, :]


def as_column(row):
    return jnp.broadcast_to(row, (128, L)).T[:, 0:1]


def softplus(v):
    return jnp.maximum(v, 0.0) + jnp.log1p(jnp.exp(-jnp.abs(v)))


def head_spread():
    return (iota((128, CH), 1) // 64 == iota((128, CH), 0)).astype(BF16)


def head_collect():
    return (iota((CH, 128), 0) // 64 == iota((CH, 128), 1)).astype(BF16)


def fold(a):
    return jnp.sum(a.reshape(a.shape[0] // 8, 8, a.shape[1]), axis=0)


def span(start, size):
    return pl.ds(pl.multiple_of(start, size), size)


def places():
    group = lax.axis_index("dp")
    return lax.axis_index("section"), group // 4, lax.rem(group, 4), lax.axis_index("tensor")


def x_peer(j):
    return {"tensor": lax.rem(lax.axis_index("tensor") + j, 4)}


def twin():
    return {"section": 1 - lax.axis_index("section")}


def greet(peers):
    for peer in peers:
        pl.semaphore_signal(pltpu.get_barrier_semaphore(), inc=1, device_id=peer, device_id_type=MESH)


def greeted(peers):
    pl.semaphore_wait(pltpu.get_barrier_semaphore(), len(peers))


class Link:
    def __init__(self, send_sems, recv_sems):
        self.send_sems, self.recv_sems = send_sems, recv_sems

    def copy(self, src, dst, at, peer):
        return pltpu.make_async_remote_copy(
            src_ref=src,
            dst_ref=dst,
            send_sem=self.send_sems.at[at],
            recv_sem=self.recv_sems.at[at],
            device_id=peer,
            device_id_type=MESH,
        )

    def start(self, src, dst, at, peer):
        self.copy(src, dst, at, peer).start()

    def arrived(self, like, at):
        self.copy(like, like, at, twin()).wait_recv()

    def sent(self, like, at):
        self.copy(like, like, at, twin()).wait_send()


SCRATCH = dict(
    wall0=((16, 64, COLS), BF16),
    wall1=((16, 64, COLS), BF16),
    dw1=((16, 64, COLS), BF16),
    theirs=((2, 16, HALF, COLS), BF16),
    first_in=((2, 3, 4, HALF, COLS), BF16),
    mid=((2, 4, HALF, COLS), BF16),
    last_in=((2, 4, HALF, COLS), BF16),
    half=((2, HALF, COLS), F32),
    other_half=((HALF, COLS), F32),
    own=((64, COLS), BF16),
    bc_in=((4, 64, 128), BF16),
    par_own=((16, CH), F32),
    par_x=((8, 128), F32),
    par_in=((4, 8, 128), F32),
    run=((3, 16, CH), F32),
    square=((128, 128), F32),
    par_all=((2, 16, CH), F32),
    tok=((T, D), BF16),
    hid=((T, D), BF16),
    gb1=((T, D), BF16),
    gb0=((T, D), BF16),
    pa=((T, D), BF16),
    pb=((T, D), BF16),
    pc=((T, D), BF16),
    ra=((NB, 3, HALF, D), BF16),
    rb=((NB, 3, HALF, D), BF16),
    pb_in=((3, ROWS, D), BF16),
    pc_in=((3, ROWS, D), BF16),
    ptot0=((NB, HALF, D), F32),
    sq_tile=((2, NB, 8, 128), F32),
    sq_in=((2, NB, 4, 8, 128), F32),
    sums=((2, NB, 8, 128), F32),
    inner0=((T, 128), F32),
    factors=((ROWS, 128), F32),
    dno=((T, CH), F32),
    blkx=((L + 8, CH), F32),
    blkbc=((L + 8, 256), F32),
    dcx=((L + 8, CH), F32),
    dcbc=((L + 8, 256), F32),
    gate=((T, CH), BF16),
    dproj=((T, 1408), BF16),
    state=((NST, CH), F32),
    ggo=((8, CH), F32),
    gsk=((8, CH), F32),
    gdt=((8, 128), F32),
    gdl=((8, 128), F32),
    tapx=((5, 8, CH), F32),
    tapbc=((5, 8, 256), F32),
    gi1=((8, D), F32),
    pack=((2, 16, CH), F32),
    pack_in=((10, 16, CH), F32),
    bcs=((2, 64, 128), F32),
    bcs_in=((4, 64, 128), F32),
    los=((2, ROWS, D), BF16),
    igs=((2, ROWS, D), F32),
)
SAVED = dict(
    n=((T, D), BF16),
    px=((T + 8, CH), F32),
    cx=((T, CH), F32),
    pz=((T, CH), F32),
    pbc=((T + 8, 256), F32),
    cbc=((T, 256), F32),
    v=((T, 128), F32),
    y=((T, CH), F32),
    h=((NB, NST, CH), BF16),
)
LINKS = dict(
    early=(2,),
    toks=(2,),
    params=(1,),
    g_first=(2, 4),
    g_second=(2, 3),
    g_twin=(2,),
    p0=(NB,),
    sq0=(NB,),
    hids=(NB,),
    sq1=(NB,),
    dn1=(NB,),
    gbs=(NB,),
    in0=(NB,),
    p1=(1,),
    dn0=(1,),
    d_twin=(2,),
    d_first=(2,),
    d_second=(2,),
    shard=(1,),
    small=(4,),
    bcx=(1,),
    outs=(2,),
)
INPUTS = (
    "gain_in", "weight_x", "weight_z", "weight_bc", "weight_dt", "conv_x", "conv_bc", "bias_x", "bias_bc", "dt_bias",
    "decay_log", "skip_gain", "gain_out", "weight_out", "lens", "tokens", "cot",
)
OUTPUTS = ("lo", "ig", "shard_out", "small_out")


class Names:
    def __init__(self, **kw):
        self.__dict__.update(kw)


def layer_kernel(*refs):
    names = list(INPUTS) + list(OUTPUTS) + list(SCRATCH)
    names += [f"{n}{k}" for k in range(2) for n in SAVED]
    k_ = Names(**dict(zip(names, refs)))
    rest = refs[len(names) :]
    lsem = rest[0]
    links = Names(**{n: Link(rest[1 + 2 * i], rest[2 + 2 * i]) for i, n in enumerate(LINKS)})
    saved = [Names(**{n: getattr(k_, f"{n}{k}") for n in SAVED}) for k in range(2)]
    walls = (k_.wall0, k_.wall1)
    s, z, y, t = places()
    own_d = z * 4 + y
    a1 = (1 - s) * y + s * z
    a2 = (1 - s) * z + s * y

    def index(first, second):
        return (1 - s) * (4 * second + first) + s * (4 * first + second)

    def first_peer(j):
        return {"dp": index(lax.rem(a1 + j, 4), a2)}

    def second_peer(j):
        return {"dp": index(a1, lax.rem(a2 + j, 4))}

    def x_of(j):
        return lax.rem(t + j, 4)

    my_half = span(HALF * s, HALF)
    twin_half = span(HALF * (1 - s), HALF)

    def y_peer(j, section):
        return {"section": section, "dp": z * 4 + lax.rem(y + j, 4)}

    def z_peer(j, section):
        return {"section": section, "dp": lax.rem(z + j, 4) * 4 + y}

    everyone = [x_peer(j) for j in ORDER] + [twin()]
    everyone += [peer(j, section) for peer in (y_peer, z_peer) for section in range(2) for j in ORDER]
    greet(everyone)

    k_.par_own[...] = jnp.zeros((16, CH), F32)
    k_.par_own[0:4, :] = k_.conv_x[0]
    k_.par_own[4:5, :] = k_.bias_x[...]
    k_.par_own[5:6, :] = k_.gain_out[...]
    k_.par_own[6:7, :] = k_.gain_in[:, 0:CH]
    k_.par_own[7:8, :] = k_.gain_in[:, CH:D]
    k_.par_own[8:9, 0:8] = k_.dt_bias[...]
    k_.par_own[8:9, 128:136] = k_.decay_log[...]
    k_.par_own[8:9, 256:264] = k_.skip_gain[...]
    k_.par_x[...] = jnp.zeros((8, 128), F32)
    k_.par_x[0:4, 0:64] = k_.conv_bc[0]
    k_.par_x[4:5, 0:64] = k_.bias_bc[...]
    k_.par_in[0] = k_.par_x[...]
    k_.bc_in[0] = jnp.zeros((64, 128), BF16)
    k_.bc_in[0, :, 0:64] = k_.weight_bc[0]
    k_.own[:, X0:Z0] = k_.weight_x[0]
    k_.own[:, Z0:O0] = k_.weight_z[0]
    k_.own[:, O0:COLS] = k_.weight_out[0]
    k_.square[...] = jnp.zeros((128, 128), F32)
    k_.square[0:8, 0:64] = k_.weight_dt[0].astype(F32)
    k_.own[:, S0:X0] = k_.square[...].T[0:64, :].astype(BF16)
    rows_t = span(t * ROWS, ROWS)
    local_tok = pltpu.make_async_copy(k_.tokens.at[s], k_.tok.at[rows_t], lsem.at[0])
    local_cot = pltpu.make_async_copy(k_.cot.at[s], k_.gb1.at[rows_t], lsem.at[1])
    local_tok.start()
    local_cot.start()
    greeted(everyone)
    for j in ORDER:
        links.early.start(k_.bc_in.at[0], k_.bc_in.at[j], 0, x_peer(j))
        links.early.start(k_.par_x, k_.par_in.at[j], 1, x_peer(j))

    def shard_to_all(k, start, size):
        def part(half):
            rows = pl.ds(half * HALF, HALF)
            return k_.own.at[rows, pl.ds(start, size)], walls[k].at[own_d, rows, pl.ds(start, size)]

        for half, peer in enumerate((y_peer, z_peer)):
            for i, j in enumerate(ORDER):
                links.g_first.start(*part(half), (k, i), peer(j, half))
        links.g_first.start(*part(1 - k), (k, 3), twin())
        rows = pl.ds(k * HALF, HALF)
        walls[k][own_d, rows, pl.ds(start, size)] = k_.own[rows, pl.ds(start, size)]

    pl.when(s == 0)(lambda: shard_to_all(0, X0, COLS - X0))
    links.early.arrived(k_.bc_in.at[pl.ds(1, 3)], 0)
    links.early.arrived(k_.par_in.at[pl.ds(1, 3)], 1)
    left = iota((64, 128), 1) < 64
    left8 = iota((8, 128), 1) < 64
    slots = [lax.rem(t - i + 4, 4) for i in range(4)]
    for i in range(2):
        cols = slice(128 * i, 128 * i + 128)
        right = pltpu.roll(k_.bc_in[slots[2 * i + 1]].astype(F32), 64, 1)
        k_.own[:, cols] = jnp.where(left, k_.bc_in[slots[2 * i]].astype(F32), right).astype(BF16)
        right = pltpu.roll(k_.par_in[slots[2 * i + 1]], 64, 1)
        k_.par_own[9:14, cols] = jnp.where(left8, k_.par_in[slots[2 * i]], right)[0:5, :]
    pl.when(s == 0)(lambda: shard_to_all(0, B0, X0))
    k_.par_all[s] = k_.par_own[...]
    links.params.start(k_.par_own, k_.par_all.at[s], 0, twin())
    for j in ORDER:
        links.toks.start(k_.tokens.at[s], k_.tok.at[rows_t], 0, x_peer(j))

    def gather_first(k):
        pl.when(s == k)(lambda: shard_to_all(k, 0, COLS))

    def gather_second(k):
        for r in (0,) + ORDER:
            piece = walls[k].at[index(lax.rem(a1 - r + 4, 4), a2), my_half]
            if r:
                links.g_first.arrived(piece, (k, ORDER.index(r)))
            else:
                pl.when(s != k)(lambda: links.g_first.arrived(piece, (k, 3)))
            for i, j in enumerate(ORDER):
                links.g_second.start(piece, piece, (k, i), second_peer(j))
            links.g_twin.start(piece, piece, k, twin())

    def gather_twin(k, between=None):
        for i, j in enumerate(ORDER):
            links.g_second.arrived(k_.mid.at[0], (k, i))
            for r in (0,) + ORDER:
                piece = walls[k].at[index(lax.rem(a1 - r + 4, 4), lax.rem(a2 - j + 4, 4)), my_half]
                links.g_twin.start(piece, piece, k, twin())
            if i == 1 and between is not None:
                between()

    def gather_done(k):
        links.g_twin.arrived(k_.theirs.at[0], k)

    def gather_sent(k):
        for i in range(3):
            links.g_second.sent(k_.mid.at[0], (k, i))
        links.g_twin.sent(k_.theirs.at[0], k)

    links.params.arrived(k_.par_own, 0)
    gather_second(0)
    for j in ORDER:
        links.toks.start(k_.cot.at[s], k_.gb1.at[rows_t], 1, x_peer(j))

    length = jnp.where(s == 0, k_.lens[:, 0:1], k_.lens[:, 1:2])

    def row_mask(start, rows):
        return (iota((rows, 1), 0) + start < length).astype(F32)

    lower = iota((L, L), 0) >= iota((L, L), 1)
    tri = lower.astype(F32)
    off = jnp.where(lower, 0.0, -1e30)
    first_half = iota((L, 128), 1) < 64
    lanes = iota((L, 128), 1)

    def make_par(k):
        def par(row, start, size):
            return k_.par_all[k, row : row + 1, start : start + size]

        return par

    def weight(k, start, size):
        return walls[k][:, :, start : start + size].reshape(D, size)

    def forward_block(k, b):
        par, keep = make_par(k), saved[k]
        rows = span(b * L, L)
        spread = head_spread()
        rate = -jnp.exp(par(8, 128, 128))
        skip = mm_exact(jnp.broadcast_to(par(8, 256, 128), (8, 128)), spread.astype(F32))[0:1, :]
        n = keep.n[rows, :]
        k_.blkbc[0:8, :] = k_.blkbc[L : L + 8, :]
        k_.blkx[0:8, :] = k_.blkx[L : L + 8, :]
        k_.blkbc[8 : 8 + L, :] = mm(n, weight(k, B0, 256))
        v = mm(n, weight(k, S0, 128)) + par(8, 0, 128)
        keep.v[rows, :] = v
        for j in range(2):
            k_.blkx[8 : 8 + L, 256 * j : 256 * j + 256] = mm(n, weight(k, X0 + 256 * j, 256))
        for j in range(2):
            keep.pz[rows, 256 * j : 256 * j + 256] = mm(n, weight(k, Z0 + 256 * j, 256))
        shifted = pl.ds(pl.multiple_of(b * L + 8, 8), L)
        keep.px[shifted, :] = k_.blkx[8 : 8 + L, :]
        keep.pbc[shifted, :] = k_.blkbc[8 : 8 + L, :]
        for j in range(4):
            cols = slice(128 * j, 128 * j + 128)
            c = par(4, 128 * j, 128)
            for tap in range(4):
                c = c + par(tap, 128 * j, 128) * k_.blkx[5 + tap : 5 + tap + L, cols]
            keep.cx[rows, cols] = c
        for j in range(2):
            cols = slice(128 * j, 128 * j + 128)
            c = par(13, 128 * j, 128)
            for tap in range(4):
                c = c + par(9 + tap, 128 * j, 128) * k_.blkbc[5 + tap : 5 + tap + L, cols]
            keep.cbc[rows, cols] = c
        st = softplus(v)
        cu = mm_exact(tri, st * rate)
        cut = cu.T
        ea = jnp.exp(cu)
        tail = jnp.exp(cu[L - 1 : L, :] - cu)
        st_e = mm_split(st, spread)
        ea_e = mm_split(ea, spread)
        tail_e = mm_split(tail, spread)
        cx = keep.cx[rows, :]
        xs = cx * jax.nn.sigmoid(cx)
        cbc = keep.cbc[rows, :]
        bc = (cbc * jax.nn.sigmoid(cbc)).astype(BF16)
        bb, cc = bc[:, :NST], bc[:, NST:]
        xd = xs * st_e
        h_in = k_.state[...].astype(BF16)
        keep.h[b] = h_in
        gram = mm(cc, bb, NT)
        yy = mm(cc, h_in) * ea_e
        k_.state[...] = k_.state[...] * ea_e[L - 1 : L, :] + mm(bb, (xd * tail_e).astype(BF16), TN)
        inside = []
        for pair in range(4):
            xp = xd[:, 128 * pair : 128 * pair + 128]
            parts, mixes = [], []
            for part in range(2):
                h = 2 * pair + part
                mixes.append((gram * jnp.exp(cu[:, h : h + 1] - cut[h : h + 1, :] + off)).astype(BF16))
                parts.append(jnp.where(first_half == (part == 0), xp, 0.0).astype(BF16))
            inside.append(mm(jnp.concatenate(mixes, axis=1), jnp.concatenate(parts, axis=0)))
        yy = yy + jnp.concatenate(inside, axis=1)
        keep.y[rows, :] = yy
        zz = keep.pz[rows, :]
        gated = (yy + xs * skip) * (zz * jax.nn.sigmoid(zz))
        k_.sq_tile[k, b, 0:1, :] = as_row(jnp.sum(gated * gated, axis=-1, keepdims=True))
        weighted = gated * par(5, 0, CH)
        k_.gate[rows, :] = weighted.astype(BF16)
        if k == 1:
            gb = (k_.gb1[rows, :].astype(F32) * row_mask(b * L, L)).astype(BF16)
            k_.gb1[rows, :] = gb
            dno = jnp.concatenate([mm(gb, weight(k, O0, 256)), mm(gb, weight(k, O0 + 256, 256))], axis=1)
            k_.dno[rows, :] = dno
            k_.sq_tile[k, b, 1:2, :] = as_row(jnp.sum(dno * weighted, axis=-1, keepdims=True))

    def norm_block(k, b, u):
        par = make_par(k)
        gain = jnp.concatenate([par(6, 0, CH), par(7, 0, CH)], axis=1)
        for i in range(4):
            part = span(b * L + 32 * i, 32)
            a = u[part, :].astype(F32)
            r = lax.rsqrt(jnp.mean(a * a, axis=-1, keepdims=True) + EPS)
            saved[k].n[part, :] = (a * r * gain).astype(BF16)

    def reset_forward(k):
        k_.blkx[...] = jnp.zeros((L + 8, CH), F32)
        k_.blkbc[...] = jnp.zeros((L + 8, 256), F32)
        saved[k].px[0:8, :] = jnp.zeros((8, CH), F32)
        saved[k].pbc[0:8, :] = jnp.zeros((8, 256), F32)
        k_.state[...] = jnp.zeros((NST, CH), F32)

    def output_rows(k, rows, dst):
        for j in range(4):
            wo = walls[k][4 * j : 4 * j + 4, :, O0 : O0 + CH].reshape(256, CH)
            dst[rows, 256 * j : 256 * j + 256] = mm(k_.gate[rows, :], wo, NT).astype(BF16)

    def slice_of(b, place):
        return span(b * L + place * HALF, HALF)

    def spread_slices(link, buf, into, b):
        for j in ORDER:
            link.start(buf.at[slice_of(b, x_of(j))], into.at[b, j - 1], b, x_peer(j))

    def spread_tile(link, k, b):
        for j in ORDER:
            link.start(k_.sq_tile.at[k, b], k_.sq_in.at[k, b, j], b, x_peer(j))

    def slice_sum(buf, into, b):
        total = buf[slice_of(b, t), :].astype(F32)
        for j in (1, 2, 3):
            total = total + into[b, j - 1].astype(F32)
        return total

    def tile_sum(link, k, b):
        link.arrived(k_.sq_in.at[k, b, pl.ds(1, 3)], b)
        k_.sums[k, b] = (
            k_.sq_tile[k, b] + k_.sq_in[k, b, 1] + k_.sq_in[k, b, 2] + k_.sq_in[k, b, 3]
        )

    def factor_column(k, b):
        return as_column(lax.rsqrt(k_.sums[k, b, 0:1, :] / INNER + EPS))

    def hidden_block(b):
        tile_sum(links.sq0, 0, b)
        links.p0.arrived(k_.ra.at[b], b)
        k_.factors[...] = jnp.broadcast_to(factor_column(0, b), (ROWS, 128))
        factor = k_.factors[span(t * HALF, HALF), :][:, 0:1]
        total = slice_sum(k_.pa, k_.ra, b)
        k_.ptot0[b] = total
        rows = slice_of(b, t)
        mask = row_mask(b * L + t * HALF, HALF)
        k_.hid[rows, :] = (mask * (k_.tok[rows, :].astype(F32) + factor * total)).astype(BF16)
        for j in ORDER:
            links.hids.start(k_.hid.at[rows], k_.hid.at[rows], b, x_peer(j))

    links.toks.arrived(k_.tok.at[pl.ds(0, 3 * ROWS)], 0)
    local_tok.wait()
    for b in range(NB):
        norm_block(0, b, k_.tok)
    reset_forward(0)
    k_.sq_tile[...] = jnp.zeros((2, NB, 8, 128), F32)
    gather_twin(0, lambda: gather_first(1))
    gather_done(0)

    def first_forward(b, carry):
        pl.when(b == 1)(lambda: gather_second(1))
        pl.when(b >= 2)(lambda: hidden_block(b - 2))
        forward_block(0, b)
        spread_tile(links.sq0, 0, b)
        output_rows(0, span(b * L, L), k_.pa)
        spread_slices(links.p0, k_.pa, k_.ra, b)
        return carry

    lax.fori_loop(0, NB, first_forward, 0)

    gather_twin(1)
    links.toks.arrived(k_.tok.at[pl.ds(0, 3 * ROWS)], 1)
    local_cot.wait()
    reset_forward(1)
    gather_done(1)

    def second_forward(b, carry):
        pl.when(b < 2)(lambda: hidden_block(b + 2))
        links.hids.arrived(k_.ra.at[b], b)
        norm_block(1, b, k_.hid)
        forward_block(1, b)
        spread_tile(links.sq1, 1, b)
        return carry

    lax.fori_loop(0, NB, second_forward, 0)
    output_rows(1, pl.ds(0, T), k_.pb)

    upper_low = (iota((L, L), 1) >= iota((L, L), 0)).astype(BF16)
    strict = (iota((L, L), 1) < iota((L, L), 0)).astype(F32)
    strict_low = strict.astype(BF16)

    def reset_backward():
        k_.state[...] = jnp.zeros((NST, CH), F32)
        k_.ggo[...] = jnp.zeros((8, CH), F32)
        k_.gsk[...] = jnp.zeros((8, CH), F32)
        k_.gdt[...] = jnp.zeros((8, 128), F32)
        k_.gdl[...] = jnp.zeros((8, 128), F32)
        k_.tapx[...] = jnp.zeros((5, 8, CH), F32)
        k_.tapbc[...] = jnp.zeros((5, 8, 256), F32)
        k_.dcx[...] = jnp.zeros((L + 8, CH), F32)
        k_.dcbc[...] = jnp.zeros((L + 8, 256), F32)

    def backward_block(k, b, gb_ref, inner, dn_ref):
        par, keep = make_par(k), saved[k]
        rows = span(b * L, L)
        spread, collect = head_spread(), head_collect()
        rate = -jnp.exp(par(8, 128, 128))
        skip = mm_exact(jnp.broadcast_to(par(8, 256, 128), (8, 128)), spread.astype(F32))[0:1, :]
        gain_out = par(5, 0, CH)
        v = keep.v[rows, :]
        st = softplus(v)
        cu = mm_exact(tri, st * rate)
        cut = cu.T
        ea = jnp.exp(cu)
        tail = jnp.exp(cu[L - 1 : L, :] - cu)
        st_e = mm_split(st, spread)
        ea_e = mm_split(ea, spread)
        tail_e = mm_split(tail, spread)
        cx = keep.cx[rows, :]
        sx = jax.nn.sigmoid(cx)
        xs = cx * sx
        cbc = keep.cbc[rows, :]
        sbc = jax.nn.sigmoid(cbc)
        bc = (cbc * sbc).astype(BF16)
        bb, cc = bc[:, :NST], bc[:, NST:]
        xd = xs * st_e
        factor = factor_column(k, b)
        if k == 1:
            dno = k_.dno[rows, :]
        else:
            gb = gb_ref[rows, :]
            dno = jnp.concatenate([mm(gb, weight(k, O0, 256)), mm(gb, weight(k, O0 + 256, 256))], axis=1)
        out = keep.y[rows, :] + xs * skip
        zz = keep.pz[rows, :]
        sz = jax.nn.sigmoid(zz)
        silu_z = zz * sz
        gated = out * silu_z
        scaled = gated * factor
        k_.gate[rows, :] = (scaled * gain_out).astype(BF16)
        k_.ggo[...] += fold(dno * scaled)
        dgated = factor * (dno * gain_out) - gated * (factor * factor * factor * (1.0 / INNER) * inner)
        dy = dgated * silu_z
        k_.dproj[rows, Z0 : Z0 + CH] = (dgated * out * (sz * (1.0 + zz - silu_z))).astype(BF16)
        k_.gsk[...] += fold(dy * xs)
        h_in = keep.h[b]
        h_back = k_.state[...]
        hb_low = h_back.astype(BF16)
        gram = mm(cc, bb, NT)
        xdt = (xd * tail_e).astype(BF16)
        dye = (dy * ea_e).astype(BF16)
        y_in = mm(cc, h_in) * ea_e
        dxd_in = mm(bb, hb_low) * tail_e
        dcc = mm(dye, h_in, NT)
        dbb = mm(xdt, hb_low, NT)
        dgram = jnp.zeros((L, L), F32)
        inside = []
        crossing = jnp.zeros((L, 128), F32)
        for pair in range(4):
            sl = slice(128 * pair, 128 * pair + 128)
            xp = xd[:, sl].astype(BF16)
            dyp = dy[:, sl]
            decs, mixes, parts = [], [], []
            for part in range(2):
                h = 2 * pair + part
                dec = jnp.exp(cu[:, h : h + 1] - cut[h : h + 1, :] + off)
                decs.append(dec)
                mixes.append(gram * dec)
                parts.append(jnp.where(first_half == (part == 0), dyp, 0.0).astype(BF16))
            dy2 = jnp.concatenate(parts, axis=0)
            dmix = mm(dy2, xp, NT)
            dm0, dm1 = dmix[:L, :], dmix[L:, :]
            dgram = dgram + dm0 * decs[0] + dm1 * decs[1]
            inside.append(mm(jnp.concatenate([mixes[0].astype(BF16), mixes[1].astype(BF16)], axis=0), dy2, TN))
            both = jnp.concatenate([(mixes[0] * dm0).astype(BF16), (mixes[1] * dm1).astype(BF16)], axis=1)
            cross = mm(upper_low, both)
            c0 = (cross[:, :L] * strict).astype(BF16)
            c1 = (cross[:, L:] * strict).astype(BF16)
            pick = jnp.concatenate(
                [(lanes == 2 * pair).astype(BF16), (lanes == 2 * pair + 1).astype(BF16)], axis=0
            )
            crossing = crossing + mm(jnp.concatenate([c0, c1], axis=1), pick)
        dgl = dgram.astype(BF16)
        dcc = dcc + mm(dgl, bb)
        dbb = dbb + mm(dgl, cc, TN)
        dxd = jnp.concatenate(inside, axis=1) + dxd_in
        kept = mm_split(jnp.broadcast_to(jnp.sum(h_in.astype(F32) * h_back, axis=0, keepdims=True), (8, CH)), collect)
        kept = kept[0:1, :] * ea[L - 1 : L, :]
        p_in = mm_split(dy * y_in, collect)
        q_in = mm_split(xd * dxd_in, collect)
        dls = crossing + mm_split_right(upper_low, p_in) + mm_split_right(strict_low, q_in) + kept
        k_.state[...] = h_back * ea_e[L - 1 : L, :] + mm(cc, dye, TN)
        dst = dls * rate + mm_split(dxd * xs, collect)
        dv = jnp.where(lanes < 8, dst * jax.nn.sigmoid(v), 0.0)
        k_.dproj[rows, S0:X0] = dv.astype(BF16)
        k_.gdt[...] += fold(dv)
        k_.gdl[...] += fold(dls * st)
        dxs = dy * skip + dxd * st_e
        k_.dcx[L : L + 8, :] = k_.dcx[0:8, :]
        k_.dcbc[L : L + 8, :] = k_.dcbc[0:8, :]
        k_.dcx[0:L, :] = dxs * (sx * (1.0 + cx - xs))
        k_.dcbc[0:L, :] = jnp.concatenate([dbb, dcc], axis=1) * (sbc * (1.0 + cbc - cbc * sbc))
        window = pl.ds(pl.multiple_of(b * L, 8), L + 8)
        k_.blkx[...] = keep.px[window, :]
        k_.blkbc[...] = keep.pbc[window, :]

        def conv_back(width, first_row, dc, blk, taps, start):
            for j in range(width // 128):
                cols = slice(128 * j, 128 * j + 128)
                d = dc[0:L, cols]
                taps[4, :, cols] += fold(d)
                total = jnp.zeros((L, 128), F32)
                for tap in range(4):
                    taps[tap, :, cols] += fold(d * blk[5 + tap : 5 + tap + L, cols])
                    total = total + par(first_row + tap, 128 * j, 128) * dc[3 - tap : 3 - tap + L, cols]
                k_.dproj[rows, start + 128 * j : start + 128 * j + 128] = total.astype(BF16)

        conv_back(CH, 0, k_.dcx, k_.blkx, k_.tapx, X0)
        conv_back(256, 9, k_.dcbc, k_.blkbc, k_.tapbc, B0)
        for j in range(4):
            wr = slice(4 * j, 4 * j + 4)
            d = mm(k_.dproj[rows, :], walls[k][wr, :, 0:O0].reshape(256, O0), NT)
            dn_ref[rows, 256 * j : 256 * j + 256] = d.astype(BF16)

    def small_grads(k):
        par = make_par(k)
        rate = -jnp.exp(par(8, 128, 128))
        k_.pack[k] = jnp.zeros((16, CH), F32)
        for tap in range(5):
            k_.pack[k, tap : tap + 1, :] = jnp.sum(k_.tapx[tap], axis=0, keepdims=True)
            k_.pack[k, 9 + tap : 10 + tap, 0:256] = jnp.sum(k_.tapbc[tap], axis=0, keepdims=True)
        k_.pack[k, 5:6, :] = jnp.sum(k_.ggo[...], axis=0, keepdims=True)
        k_.pack[k, 8:9, 0:128] = jnp.sum(k_.gdt[...], axis=0, keepdims=True)
        k_.pack[k, 8:9, 128:256] = jnp.sum(k_.gdl[...], axis=0, keepdims=True) * rate
        gs = mm_split(jnp.broadcast_to(jnp.sum(k_.gsk[...], axis=0, keepdims=True), (8, CH)), head_collect())
        k_.pack[k, 8:9, 256:384] = gs[0:1, :]

    def weight_grads(k, gb_ref, dst):
        for j in range(4):
            nt = saved[k].n[:, 256 * j : 256 * j + 256].T
            gt = gb_ref[:, 256 * j : 256 * j + 256].T
            wr = slice(4 * j, 4 * j + 4)

            def put(start, size, value):
                dst[wr, :, start : start + size] = value.astype(BF16).reshape(4, 64, size)

            for c in range(0, O0, 256):
                size = min(256, O0 - c)
                put(c, size, mm(nt, k_.dproj[:, c : c + size]))
            for c in range(2):
                put(O0 + 256 * c, 256, mm(gt, k_.gate[:, 256 * c : 256 * c + 256]))
            links.d_twin.start(dst.at[wr, twin_half], k_.theirs.at[k, wr], k, twin())

    def input_grad(k, total, u, upstream):
        par = make_par(k)
        gain = jnp.concatenate([par(6, 0, CH), par(7, 0, CH)], axis=1)
        r = lax.rsqrt(jnp.mean(u * u, axis=-1, keepdims=True) + EPS)
        c = total * gain
        back = upstream + r * c - u * (r * r * r * (1.0 / D)) * jnp.sum(c * u, axis=-1, keepdims=True)
        return back, fold(total * (u * r))

    def turn_block(b):
        links.dn1.arrived(k_.rb.at[b], b)
        rows = slice_of(b, t)
        u = k_.hid[rows, :].astype(F32)
        back, gain_grad = input_grad(1, slice_sum(k_.pc, k_.rb, b), u, k_.gb1[rows, :].astype(F32))
        k_.gi1[...] += gain_grad
        low = (row_mask(b * L + t * HALF, HALF) * back).astype(BF16)
        k_.gb0[rows, :] = low
        inner = jnp.sum(low.astype(F32) * k_.ptot0[b], axis=-1, keepdims=True)
        k_.inner0[rows, :] = jnp.broadcast_to(inner, (HALF, 128))
        for j in ORDER:
            links.gbs.start(k_.gb0.at[rows], k_.gb0.at[rows], b, x_peer(j))
            links.in0.start(k_.inner0.at[rows], k_.inner0.at[rows], b, x_peer(j))

    def owner_slices(link, buf, into):
        for j in ORDER:
            link.start(buf.at[span(x_of(j) * ROWS, ROWS)], into.at[j - 1], 0, x_peer(j))

    def reduce_first(k, dst):
        links.d_twin.arrived(k_.theirs.at[k], k)

        def add(i, carry):
            dst[i, my_half, :] = (dst[i, my_half, :].astype(F32) + k_.theirs[k, i].astype(F32)).astype(BF16)
            return carry

        lax.fori_loop(0, 16, add, 0)
        for j in ORDER:
            for r in range(4):
                piece = dst.at[index(lax.rem(a1 + j, 4), r), my_half]
                links.d_first.start(piece, k_.first_in.at[k, j - 1, r], k, first_peer(j))

    def reduce_second(k, dst):
        links.d_first.arrived(k_.first_in.at[k], k)

        def add(r, carry):
            total = dst[index(a1, r), my_half, :].astype(F32)
            for j in (1, 2, 3):
                total = total + k_.first_in[k, j - 1, r].astype(F32)
            k_.mid[k, r] = total.astype(BF16)
            return carry

        lax.fori_loop(0, 4, add, 0)
        for j in ORDER:
            links.d_second.start(k_.mid.at[k, lax.rem(a2 + j, 4)], k_.last_in.at[k, j], k, second_peer(j))

    def reduce_last(k):
        links.d_second.arrived(k_.last_in.at[k, pl.ds(1, 3)], k)
        total = k_.mid[k, a2].astype(F32)
        for j in (1, 2, 3):
            total = total + k_.last_in[k, j].astype(F32)
        k_.half[k] = total

    reset_backward()
    k_.gi1[...] = jnp.zeros((8, D), F32)

    def second_backward(i, carry):
        b = NB - 1 - i
        tile_sum(links.sq1, 1, b)
        backward_block(1, b, k_.gb1, as_column(k_.sums[1, b, 1:2, :]), k_.pc)
        spread_slices(links.dn1, k_.pc, k_.rb, b)
        pl.when(i >= 2)(lambda: turn_block(b + 2))
        return carry

    lax.fori_loop(0, NB, second_backward, 0)
    small_grads(1)
    weight_grads(1, k_.gb1, k_.dw1)

    reset_backward()
    for b in range(NB):
        links.p0.sent(k_.ra.at[b], b)

    def first_backward(i, carry):
        b = NB - 1 - i
        pl.when(i < 2)(lambda: turn_block(1 - i))
        pl.when(i == 1)(lambda: reduce_first(1, k_.dw1))
        pl.when(i == 3)(lambda: owner_slices(links.p1, k_.pb, k_.pb_in))
        links.gbs.arrived(k_.ra.at[b], b)
        links.in0.arrived(k_.inner0.at[pl.ds(0, 3 * HALF)], b)
        inner = k_.inner0[span(b * L, L), :][:, 0:1]
        backward_block(0, b, k_.gb0, inner, k_.pa)
        return carry

    lax.fori_loop(0, NB, first_backward, 0)
    owner_slices(links.dn0, k_.pa, k_.pc_in)
    small_grads(0)
    gather_sent(1)
    weight_grads(0, k_.gb0, k_.wall1)

    reduce_second(1, k_.dw1)
    reduce_first(0, k_.wall1)
    links.dn0.arrived(k_.pc_in, 0)
    total = k_.pa[rows_t, :].astype(F32)
    for j in (1, 2, 3):
        total = total + k_.pc_in[j - 1].astype(F32)
    grad, gain_grad = input_grad(0, total, k_.tok[rows_t, :].astype(F32), k_.gb0[rows_t, :].astype(F32))
    k_.igs[0] = grad
    k_.igs[1] = k_.gb0[rows_t, :].astype(F32)
    for k, part in ((0, gain_grad), (1, k_.gi1[...])):
        part = jnp.sum(part, axis=0, keepdims=True)
        k_.pack[k, 6:7, :] = part[:, 0:CH]
        k_.pack[k, 7:8, :] = part[:, CH:D]
    links.small.start(k_.pack.at[1 - s], k_.pack_in.at[0], 0, twin())
    links.p1.arrived(k_.pb_in, 0)
    total = k_.pb[rows_t, :].astype(F32)
    for j in (1, 2, 3):
        total = total + k_.pb_in[j - 1].astype(F32)
    mask = row_mask(t * ROWS, ROWS)
    factor = factor_column(1, t)
    k_.los[0] = k_.hid[rows_t, :]
    k_.los[1] = (mask * (k_.hid[rows_t, :].astype(F32) + factor * total)).astype(BF16)
    links.outs.start(k_.los.at[1 - s], k_.lo.at[s], 0, twin())
    links.outs.start(k_.igs.at[1 - s], k_.ig.at[s], 1, twin())
    keep_lo = pltpu.make_async_copy(k_.los.at[s], k_.lo.at[s], lsem.at[2])
    keep_ig = pltpu.make_async_copy(k_.igs.at[s], k_.ig.at[s], lsem.at[3])
    keep_lo.start()
    keep_ig.start()
    reduce_last(1)
    links.small.arrived(k_.pack_in.at[0], 0)
    k_.run[0] = k_.pack[s] + k_.pack_in[0]
    for j in ORDER:
        links.small.start(k_.run.at[0], k_.pack_in.at[j], 1, first_peer(j))
    reduce_second(0, k_.wall1)

    def small_step(stage, peers):
        first = 3 * stage - 2
        links.small.arrived(k_.pack_in.at[pl.ds(first, 3)], stage)
        k_.run[stage] = (
            k_.run[stage - 1] + k_.pack_in[first] + k_.pack_in[first + 1] + k_.pack_in[first + 2]
        )
        for j in ORDER:
            links.small.start(k_.run.at[stage], k_.pack_in.at[first + 2 + j], stage + 1, peers(j))

    small_step(1, second_peer)
    reduce_last(0)
    links.shard.start(k_.half.at[1 - s], k_.other_half, 0, twin())
    small_step(2, x_peer)
    links.shard.arrived(k_.other_half, 0)
    mine, others = k_.half[s], k_.other_half[...]
    k_.shard_out[my_half, :] = mine
    k_.shard_out[twin_half, :] = others
    for i in range(2):
        k_.bcs[i, my_half, :] = mine[:, B0 + 128 * i : B0 + 128 * i + 128]
        k_.bcs[i, twin_half, :] = others[:, B0 + 128 * i : B0 + 128 * i + 128]
    for j in ORDER:
        links.bcx.start(k_.bcs.at[x_of(j) // 2], k_.bcs_in.at[j], 0, x_peer(j))
    links.small.arrived(k_.pack_in.at[pl.ds(7, 3)], 3)
    over_x = k_.run[2] + k_.pack_in[7] + k_.pack_in[8] + k_.pack_in[9]
    row = iota((16, CH), 0)
    shared = (row == 6) | (row == 7) | (row >= 9)
    over_x = jnp.where(shared, over_x, k_.run[2])
    k_.small_out[...] = over_x
    chosen = over_x[8:16, 0:64]
    for i in range(1, 4):
        chosen = jnp.where(t == i, over_x[8:16, 64 * i : 64 * i + 64], chosen)
    k_.small_out[9:14, 0:64] = chosen[1:6, :]
    links.bcx.arrived(k_.bcs_in.at[pl.ds(1, 3)], 0)
    block = k_.bcs[t // 2] + k_.bcs_in[1] + k_.bcs_in[2] + k_.bcs_in[3]
    k_.shard_out[:, B0 : B0 + 64] = jnp.where(lax.rem(t, 2) == 0, block[:, 0:64], block[:, 64:128])

    keep_lo.wait()
    keep_ig.wait()
    links.outs.arrived(k_.los.at[0], 0)
    links.outs.arrived(k_.igs.at[0], 1)
    links.outs.sent(k_.los.at[0], 0)
    links.outs.sent(k_.igs.at[0], 1)
    links.params.sent(k_.par_own, 0)
    links.shard.sent(k_.other_half, 0)
    links.small.sent(k_.run.at[0], 0)
    for i in range(1, 4):
        links.small.sent(k_.run, i)
    links.early.sent(k_.bc_in.at[pl.ds(1, 3)], 0)
    links.early.sent(k_.par_in.at[pl.ds(1, 3)], 1)
    links.toks.sent(k_.tok.at[pl.ds(0, 3 * ROWS)], 0)
    links.toks.sent(k_.tok.at[pl.ds(0, 3 * ROWS)], 1)
    links.p1.sent(k_.pb_in, 0)
    links.dn0.sent(k_.pc_in, 0)
    links.bcx.sent(k_.bcs_in.at[pl.ds(1, 3)], 0)
    gather_sent(0)

    def shard_sent(k):
        for i in range(3):
            links.g_first.sent(k_.mid.at[0, pl.ds(0, 2)], (k, i))
        links.g_first.sent(k_.mid.at[0, 0], (k, 3))

    for k in range(2):
        pl.when(s == k)(lambda: shard_sent(k))
        links.d_twin.sent(k_.theirs.at[k], k)
        links.d_first.sent(k_.first_in.at[k], k)
        links.d_second.sent(k_.last_in.at[k, pl.ds(1, 3)], k)
    for b in range(NB):
        links.sq0.sent(k_.sq_in.at[0, b, pl.ds(1, 3)], b)
        links.sq1.sent(k_.sq_in.at[1, b, pl.ds(1, 3)], b)
        links.hids.sent(k_.ra.at[b], b)
        links.dn1.sent(k_.rb.at[b], b)
        links.gbs.sent(k_.ra.at[b], b)
        links.in0.sent(k_.inner0.at[pl.ds(0, 3 * HALF)], b)


def unpack_kernel(
    shard, small, lo, ig,
    o_lo, o_ig, o_gi, o_wx, o_wz, o_bc, o_dt, o_cx, o_cb, o_bx, o_bb, o_db, o_dl, o_sk, o_go, o_wo,
):
    o_lo[...] = lo[...]
    o_ig[...] = ig[...]
    o_gi[:, 0:CH] = small[6:7, :]
    o_gi[:, CH:D] = small[7:8, :]
    o_wx[...] = shard[:, X0:Z0]
    o_wz[...] = shard[:, Z0:O0]
    o_bc[...] = shard[:, B0 : B0 + 64]
    steps = shard[:, S0:X0]
    o_dt[...] = jnp.concatenate([steps, steps], axis=0).T[0:8, 0:64]
    o_wo[...] = shard[:, O0:COLS]
    o_cx[...] = small[0:4, :]
    o_bx[...] = small[4:5, :]
    o_go[...] = small[5:6, :]
    o_db[...] = small[8:9, 0:8]
    o_dl[...] = small[8:9, 128:136]
    o_sk[...] = small[8:9, 256:264]
    o_cb[...] = small[9:13, 0:64]
    o_bb[...] = small[13:14, 0:64]


def sds(shape, dtype):
    return jax.ShapeDtypeStruct(shape, dtype)


VM = pl.BlockSpec(memory_space=pltpu.VMEM)
ANY = pl.BlockSpec(memory_space=pl.ANY)


def body(
    tokens_in, cotangent, seq_lengths, gain_in, weight_x, weight_z, weight_bc, weight_dt, conv_x, conv_bc,
    bias_x, bias_bc, dt_bias, decay_log, skip_gain, gain_out, weight_out,
):
    ins = [
        gain_in, weight_x, weight_z, weight_bc, weight_dt.swapaxes(1, 2), conv_x, conv_bc, bias_x, bias_bc, dt_bias,
        decay_log, skip_gain, gain_out, weight_out.swapaxes(1, 2), seq_lengths.T, tokens_in, cotangent,
    ]
    scratch = [pltpu.VMEM(*a) for a in SCRATCH.values()]
    scratch += [pltpu.VMEM(*a) for _ in range(2) for a in SAVED.values()]
    scratch += [pltpu.SemaphoreType.DMA((4,))]
    for shape in LINKS.values():
        scratch += [pltpu.SemaphoreType.DMA(shape)] * 2
    lo, ig, shard, small = pl.pallas_call(
        layer_kernel,
        out_shape=[
            sds((2, ROWS, D), BF16),
            sds((2, ROWS, D), F32),
            sds((64, COLS), F32),
            sds((16, CH), F32),
        ],
        in_specs=[VM] * 15 + [ANY] * 2,
        out_specs=[ANY, ANY, VM, VM],
        scratch_shapes=scratch,
        compiler_params=pltpu.CompilerParams(collective_id=0, has_side_effects=True, vmem_limit_bytes=VMEM_LIMIT),
    )(*ins)
    shapes = [
        (2, ROWS, D), (2, ROWS, D), (1, D), (64, CH), (64, CH), (64, 64), (8, 64), (4, CH), (4, 64), (1, CH), (1, 64),
        (1, 8), (1, 8), (1, 8), (1, CH), (64, CH),
    ]
    found = pl.pallas_call(
        unpack_kernel,
        out_shape=[sds(a, BF16 if i == 0 else F32) for i, a in enumerate(shapes)],
        in_specs=[VM] * 4,
        out_specs=[VM] * 16,
        compiler_params=pltpu.CompilerParams(vmem_limit_bytes=VMEM_LIMIT),
    )(shard, small, lo, ig)
    found = list(found)
    found[6] = found[6].T
    found[15] = found[15].T
    return tuple(a if i in (2, 9, 10, 11, 12, 13, 14) else a[None] for i, a in enumerate(found))


def solution(mesh):
    in_specs = (
        P(None, ("dp", "tensor"), None),
        P(None, ("dp", "tensor"), None),
        P(None, "dp"),
        P("section", None),
        P("section", "dp", "tensor"),
        P("section", "dp", "tensor"),
        P("section", "dp", "tensor"),
        P("section", "dp", "tensor"),
        P("section", None, "tensor"),
        P("section", None, "tensor"),
        P("section", "tensor"),
        P("section", "tensor"),
        P("section", "tensor"),
        P("section", "tensor"),
        P("section", "tensor"),
        P("section", "tensor"),
        P("section", "tensor", "dp"),
    )
    out_specs = (
        P("section", None, ("dp", "tensor"), None),
        P("section", None, ("dp", "tensor"), None),
        P("section", None),
        P("section", "dp", "tensor"),
        P("section", "dp", "tensor"),
        P("section", "dp", "tensor"),
        P("section", "dp", "tensor"),
        P("section", None, "tensor"),
        P("section", None, "tensor"),
        P("section", "tensor"),
        P("section", "tensor"),
        P("section", "tensor"),
        P("section", "tensor"),
        P("section", "tensor"),
        P("section", "tensor"),
        P("section", "tensor", "dp"),
    )
    return jax.shard_map(body, mesh=mesh, in_specs=in_specs, out_specs=out_specs, check_vma=False)
```

```python
import jax
import jax.numpy as jnp
from jax import lax
from jax.experimental import pallas as pl
from jax.experimental.pallas import tpu as pltpu
from jax.sharding import PartitionSpec as P

F32 = jnp.float32
BF16 = jnp.bfloat16
T = 512
L = 128
NB = T // L
D = 1024
CH = 512
INNER = 2048
NST = 128
EPS = 1e-05
B0, S0, X0, Z0, O0, COLS = 0, 256, 384, 896, 1408, 1920
VMEM_LIMIT = 60 * 2**20
MESH = pl.DeviceIdType.MESH
ROWS = 128
HALF = 32
ORDER = (1, 3, 2)

NN = (((1,), (0,)), ((), ()))
NT = (((1,), (1,)), ((), ()))
TN = (((0,), (0,)), ((), ()))


def mm(a, b, dims=NN):
    return lax.dot_general(a, b, dims, preferred_element_type=F32)


def mm_exact(a, b):
    return lax.dot_general(a, b, NN, precision=lax.Precision.HIGHEST, preferred_element_type=F32)


def mm_split(a, b):
    hi = a.astype(BF16)
    lo = (a - hi.astype(F32)).astype(BF16)
    return mm(hi, b) + mm(lo, b)


def mm_split_right(a, b):
    hi = b.astype(BF16)
    lo = (b - hi.astype(F32)).astype(BF16)
    return mm(a, hi) + mm(a, lo)


def iota(shape, dim):
    return lax.broadcasted_iota(jnp.int32, shape, dim)


def as_row(column):
    return jnp.broadcast_to(column, (L, 128)).T[0:1, :]


def as_column(row):
    return jnp.broadcast_to(row, (128, L)).T[:, 0:1]


def softplus(v):
    return jnp.maximum(v, 0.0) + jnp.log1p(jnp.exp(-jnp.abs(v)))


def head_spread():
    return (iota((128, CH), 1) // 64 == iota((128, CH), 0)).astype(BF16)


def head_collect():
    return (iota((CH, 128), 0) // 64 == iota((CH, 128), 1)).astype(BF16)


def fold(a):
    return jnp.sum(a.reshape(a.shape[0] // 8, 8, a.shape[1]), axis=0)


def span(start, size):
    return pl.ds(pl.multiple_of(start, size), size)


def places():
    group = lax.axis_index("dp")
    return lax.axis_index("section"), group // 4, lax.rem(group, 4), lax.axis_index("tensor")


def x_peer(j):
    return {"tensor": lax.rem(lax.axis_index("tensor") + j, 4)}


def twin():
    return {"section": 1 - lax.axis_index("section")}


def greet(peers):
    for peer in peers:
        pl.semaphore_signal(pltpu.get_barrier_semaphore(), inc=1, device_id=peer, device_id_type=MESH)


def greeted(peers):
    pl.semaphore_wait(pltpu.get_barrier_semaphore(), len(peers))


class Link:
    def __init__(self, send_sems, recv_sems):
        self.send_sems, self.recv_sems = send_sems, recv_sems

    def copy(self, src, dst, at, peer):
        return pltpu.make_async_remote_copy(
            src_ref=src,
            dst_ref=dst,
            send_sem=self.send_sems.at[at],
            recv_sem=self.recv_sems.at[at],
            device_id=peer,
            device_id_type=MESH,
        )

    def start(self, src, dst, at, peer):
        self.copy(src, dst, at, peer).start()

    def arrived(self, like, at):
        self.copy(like, like, at, twin()).wait_recv()

    def sent(self, like, at):
        self.copy(like, like, at, twin()).wait_send()


SCRATCH = dict(
    wall0=((16, 64, COLS), BF16),
    wall1=((16, 64, COLS), BF16),
    dw1=((16, 64, COLS), BF16),
    theirs=((2, 16, HALF, COLS), BF16),
    first_in=((2, 3, 4, HALF, COLS), BF16),
    mid=((2, 4, HALF, COLS), BF16),
    last_in=((2, 4, HALF, COLS), BF16),
    half=((2, HALF, COLS), F32),
    other_half=((HALF, COLS), F32),
    own=((64, COLS), BF16),
    bc_in=((4, 64, 128), BF16),
    par_own=((16, CH), F32),
    par_x=((8, 128), F32),
    par_in=((4, 8, 128), F32),
    run=((3, 16, CH), F32),
    square=((128, 128), F32),
    par_all=((2, 16, CH), F32),
    tok=((T, D), BF16),
    hid=((T, D), BF16),
    gb1=((T, D), BF16),
    gb0=((T, D), BF16),
    pa=((T, D), BF16),
    pb=((T, D), BF16),
    pc=((T, D), BF16),
    ra=((NB, 3, HALF, D), BF16),
    rb=((NB, 3, HALF, D), BF16),
    p1_in=((3, ROWS, D), BF16),
    dn0_in=((3, ROWS, D), BF16),
    ptot0=((NB, HALF, D), F32),
    sq_tile=((2, NB, 8, 128), F32),
    sq_in=((2, NB, 4, 8, 128), F32),
    sums=((2, NB, 8, 128), F32),
    inner_in=((NB, 4, 8, 128), F32),
    factors=((ROWS, 128), F32),
    dno=((T, CH), F32),
    blkx=((L + 8, CH), F32),
    blkbc=((L + 8, 256), F32),
    dcx=((L + 8, CH), F32),
    dcbc=((L + 8, 256), F32),
    gate=((T, CH), BF16),
    dproj=((T, 1408), BF16),
    state=((NST, CH), F32),
    ggo=((8, CH), F32),
    gsk=((8, CH), F32),
    gdt=((8, 128), F32),
    gdl=((8, 128), F32),
    tapx=((5, 8, CH), F32),
    tapbc=((5, 8, 256), F32),
    gi=((2, 8, D), F32),
    pack=((2, 16, CH), F32),
    pack_in=((10, 16, CH), F32),
    bc_last=((2, 4, 4, HALF, 128), BF16),
    los=((2, ROWS, D), BF16),
    igs=((2, ROWS, D), F32),
)
SAVED = dict(
    n=((T, D), BF16),
    px=((T + 8, CH), F32),
    cx=((T, CH), F32),
    pz=((T, CH), F32),
    pbc=((T + 8, 256), F32),
    cbc=((T, 256), F32),
    v=((T, 128), F32),
    y=((T, CH), F32),
    h=((NB, NST, CH), BF16),
)
LINKS = dict(
    early=(2,),
    rows1=(2, 2),
    rows2=(2,),
    params=(1,),
    g_first=(4, 4),
    g_second=(4, 3),
    g_twin=(4,),
    p0=(NB,),
    sq0=(NB,),
    hids=(NB,),
    sq1=(NB,),
    dn1=(NB,),
    gbs=(NB,),
    in0=(NB,),
    p1=(1,),
    dn0=(1,),
    d_twin=(2, 2),
    d_first=(2, 2),
    d_second=(2, 2),
    shard=(1,),
    small=(4,),
    bcx=(2,),
    outs=(2,),
)
GROUPS = ((0, X0, O0 - X0), (0, B0, X0), (0, O0, COLS - O0), (1, 0, COLS))
PARTS = (((Z0, COLS - Z0), (0, Z0)), ((0, COLS),))
INPUTS = (
    "gain_in", "weight_x", "weight_z", "weight_bc", "weight_dt", "conv_x", "conv_bc", "bias_x", "bias_bc", "dt_bias",
    "decay_log", "skip_gain", "gain_out", "weight_out", "lens", "tokens", "cot",
)
OUTPUTS = ("lo", "ig", "shard_out", "small_out")


class Names:
    def __init__(self, **kw):
        self.__dict__.update(kw)


def layer_kernel(*refs):
    names = list(INPUTS) + list(OUTPUTS) + list(SCRATCH)
    names += [f"{n}{k}" for k in range(2) for n in SAVED]
    k_ = Names(**dict(zip(names, refs)))
    rest = refs[len(names) :]
    lsem = rest[0]
    links = Names(**{n: Link(rest[1 + 2 * i], rest[2 + 2 * i]) for i, n in enumerate(LINKS)})
    saved = [Names(**{n: getattr(k_, f"{n}{k}") for n in SAVED}) for k in range(2)]
    walls = (k_.wall0, k_.wall1)
    s, z, y, t = places()
    own_d = z * 4 + y
    a1 = (1 - s) * y + s * z
    a2 = (1 - s) * z + s * y

    def index(first, second):
        return (1 - s) * (4 * second + first) + s * (4 * first + second)

    def first_peer(j):
        return {"dp": index(lax.rem(a1 + j, 4), a2)}

    def second_peer(j):
        return {"dp": index(a1, lax.rem(a2 + j, 4))}

    def x_of(j):
        return lax.rem(t + j, 4)

    my_half = span(HALF * s, HALF)
    twin_half = span(HALF * (1 - s), HALF)

    def y_peer(j, section):
        return {"section": section, "dp": z * 4 + lax.rem(y + j, 4)}

    def z_peer(j, section):
        return {"section": section, "dp": lax.rem(z + j, 4) * 4 + y}

    everyone = [x_peer(j) for j in ORDER] + [twin()]
    everyone += [peer(j, section) for peer in (y_peer, z_peer) for section in range(2) for j in ORDER]
    everyone += [{"dp": index(a1, lax.rem(a2 + j, 4)), "tensor": x_of(i)} for j in ORDER for i in ORDER]
    greet(everyone)

    k_.par_own[...] = jnp.zeros((16, CH), F32)
    k_.par_own[0:4, :] = k_.conv_x[0]
    k_.par_own[4:5, :] = k_.bias_x[...]
    k_.par_own[5:6, :] = k_.gain_out[...]
    k_.par_own[6:7, :] = k_.gain_in[:, 0:CH]
    k_.par_own[7:8, :] = k_.gain_in[:, CH:D]
    k_.par_own[8:9, 0:8] = k_.dt_bias[...]
    k_.par_own[8:9, 128:136] = k_.decay_log[...]
    k_.par_own[8:9, 256:264] = k_.skip_gain[...]
    k_.par_x[...] = jnp.zeros((8, 128), F32)
    k_.par_x[0:4, 0:64] = k_.conv_bc[0]
    k_.par_x[4:5, 0:64] = k_.bias_bc[...]
    k_.par_in[0] = k_.par_x[...]
    k_.bc_in[0] = jnp.zeros((64, 128), BF16)
    k_.bc_in[0, :, 0:64] = k_.weight_bc[0]
    k_.own[:, X0:Z0] = k_.weight_x[0]
    k_.own[:, Z0:O0] = k_.weight_z[0]
    k_.own[:, O0:COLS] = k_.weight_out[0]
    k_.square[...] = jnp.zeros((128, 128), F32)
    k_.square[0:8, 0:64] = k_.weight_dt[0].astype(F32)
    k_.own[:, S0:X0] = k_.square[...].T[0:64, :].astype(BF16)
    rows_t = span(t * ROWS, ROWS)
    local_tok = pltpu.make_async_copy(k_.tokens.at[s], k_.tok.at[rows_t], lsem.at[0])
    local_cot = pltpu.make_async_copy(k_.cot.at[s], k_.gb1.at[rows_t], lsem.at[1])
    local_tok.start()
    local_cot.start()
    greeted(everyone)
    for j in ORDER:
        links.early.start(k_.bc_in.at[0], k_.bc_in.at[j], 0, x_peer(j))
        links.early.start(k_.par_x, k_.par_in.at[j], 1, x_peer(j))

    def shard_to_all(group):
        k, start, size = GROUPS[group]
        cols = pl.ds(start, size)

        def part(half):
            rows = pl.ds(half * HALF, HALF)
            return k_.own.at[rows, cols], walls[k].at[own_d, rows, cols]

        for half, peer in enumerate((y_peer, z_peer)):
            for i, j in enumerate(ORDER):
                links.g_first.start(*part(half), (group, i), peer(j, half))
        links.g_first.start(*part(1 - k), (group, 3), twin())
        rows = pl.ds(k * HALF, HALF)
        walls[k][own_d, rows, cols] = k_.own[rows, cols]

    def gather_first(group):
        pl.when(s == GROUPS[group][0])(lambda: shard_to_all(group))

    def gather_second(group):
        k, start, size = GROUPS[group]
        for r in (0,) + ORDER:
            piece = walls[k].at[index(lax.rem(a1 - r + 4, 4), a2), my_half, pl.ds(start, size)]
            if r:
                links.g_first.arrived(piece, (group, ORDER.index(r)))
            else:
                pl.when(s != k)(lambda: links.g_first.arrived(piece, (group, 3)))
            for i, j in enumerate(ORDER):
                links.g_second.start(piece, piece, (group, i), second_peer(j))
            links.g_twin.start(piece, piece, group, twin())

    def gather_twin(group):
        k, start, size = GROUPS[group]
        for i, j in enumerate(ORDER):
            links.g_second.arrived(k_.mid.at[0, :, :, pl.ds(start, size)], (group, i))
            for r in (0,) + ORDER:
                place = index(lax.rem(a1 - r + 4, 4), lax.rem(a2 - j + 4, 4))
                piece = walls[k].at[place, my_half, pl.ds(start, size)]
                links.g_twin.start(piece, piece, group, twin())

    def gather_done(group):
        links.g_twin.arrived(k_.theirs.at[0, :, :, pl.ds(*GROUPS[group][1:])], group)

    def gather_sent(group):
        cols = pl.ds(*GROUPS[group][1:])
        for i in range(3):
            links.g_second.sent(k_.mid.at[0, :, :, cols], (group, i))
        links.g_twin.sent(k_.theirs.at[0, :, :, cols], group)

    def rows_first(a, src, dst):
        links.rows1.start(src.at[s], dst.at[rows_t], (a, 0), x_peer(1))
        links.rows1.start(src.at[s], dst.at[rows_t], (a, 1), x_peer(3))

    def rows_second(a, dst):
        links.rows1.arrived(dst.at[rows_t], (a, 0))
        upper = dst.at[span(x_of(3) * ROWS, ROWS // 2)]
        links.rows2.start(upper, upper, a, x_peer(1))
        links.rows1.arrived(dst.at[rows_t], (a, 1))
        lower_rows = dst.at[span(x_of(1) * ROWS + ROWS // 2, ROWS // 2)]
        links.rows2.start(lower_rows, lower_rows, a, x_peer(3))

    gather_first(0)
    rows_first(0, k_.tokens, k_.tok)
    gather_second(0)
    links.early.arrived(k_.bc_in.at[pl.ds(1, 3)], 0)
    links.early.arrived(k_.par_in.at[pl.ds(1, 3)], 1)
    left = iota((64, 128), 1) < 64
    left8 = iota((8, 128), 1) < 64
    slots = [lax.rem(t - i + 4, 4) for i in range(4)]
    for i in range(2):
        cols = slice(128 * i, 128 * i + 128)
        right = pltpu.roll(k_.bc_in[slots[2 * i + 1]].astype(F32), 64, 1)
        k_.own[:, cols] = jnp.where(left, k_.bc_in[slots[2 * i]].astype(F32), right).astype(BF16)
        right = pltpu.roll(k_.par_in[slots[2 * i + 1]], 64, 1)
        k_.par_own[9:14, cols] = jnp.where(left8, k_.par_in[slots[2 * i]], right)[0:5, :]
    gather_first(1)
    gather_first(2)
    k_.par_all[s] = k_.par_own[...]
    links.params.start(k_.par_own, k_.par_all.at[s], 0, twin())
    rows_second(0, k_.tok)
    gather_second(1)
    gather_second(2)
    links.params.arrived(k_.par_own, 0)

    length = jnp.where(s == 0, k_.lens[:, 0:1], k_.lens[:, 1:2])

    def row_mask(start, rows):
        return (iota((rows, 1), 0) + start < length).astype(F32)

    lower = iota((L, L), 0) >= iota((L, L), 1)
    tri = lower.astype(F32)
    off = jnp.where(lower, 0.0, -1e30)
    first_half = iota((L, 128), 1) < 64
    lanes = iota((L, 128), 1)

    def make_par(k):
        def par(row, start, size):
            return k_.par_all[k, row : row + 1, start : start + size]

        return par

    def weight(k, start, size):
        return walls[k][:, :, start : start + size].reshape(D, size)

    def project_block(k, b):
        par, keep = make_par(k), saved[k]
        rows = span(b * L, L)
        n = keep.n[rows, :]
        k_.blkbc[0:8, :] = k_.blkbc[L : L + 8, :]
        k_.blkx[0:8, :] = k_.blkx[L : L + 8, :]
        k_.blkbc[8 : 8 + L, :] = mm(n, weight(k, B0, 256))
        v = mm(n, weight(k, S0, 128)) + par(8, 0, 128)
        keep.v[rows, :] = v
        for j in range(2):
            k_.blkx[8 : 8 + L, 256 * j : 256 * j + 256] = mm(n, weight(k, X0 + 256 * j, 256))
        for j in range(2):
            keep.pz[rows, 256 * j : 256 * j + 256] = mm(n, weight(k, Z0 + 256 * j, 256))
        shifted = pl.ds(pl.multiple_of(b * L + 8, 8), L)
        keep.px[shifted, :] = k_.blkx[8 : 8 + L, :]
        keep.pbc[shifted, :] = k_.blkbc[8 : 8 + L, :]
        for j in range(4):
            cols = slice(128 * j, 128 * j + 128)
            c = par(4, 128 * j, 128)
            for tap in range(4):
                c = c + par(tap, 128 * j, 128) * k_.blkx[5 + tap : 5 + tap + L, cols]
            keep.cx[rows, cols] = c
        for j in range(2):
            cols = slice(128 * j, 128 * j + 128)
            c = par(13, 128 * j, 128)
            for tap in range(4):
                c = c + par(9 + tap, 128 * j, 128) * k_.blkbc[5 + tap : 5 + tap + L, cols]
            keep.cbc[rows, cols] = c

    def forward_block(k, b):
        par, keep = make_par(k), saved[k]
        rows = span(b * L, L)
        spread = head_spread()
        rate = -jnp.exp(par(8, 128, 128))
        skip = mm_exact(jnp.broadcast_to(par(8, 256, 128), (8, 128)), spread.astype(F32))[0:1, :]
        st = softplus(keep.v[rows, :])
        cu = mm_exact(tri, st * rate)
        cut = cu.T
        ea = jnp.exp(cu)
        tail = jnp.exp(cu[L - 1 : L, :] - cu)
        st_e = mm_split(st, spread)
        ea_e = mm_split(ea, spread)
        tail_e = mm_split(tail, spread)
        cx = keep.cx[rows, :]
        xs = cx * jax.nn.sigmoid(cx)
        cbc = keep.cbc[rows, :]
        bc = (cbc * jax.nn.sigmoid(cbc)).astype(BF16)
        bb, cc = bc[:, :NST], bc[:, NST:]
        xd = xs * st_e
        h_in = k_.state[...].astype(BF16)
        keep.h[b] = h_in
        gram = mm(cc, bb, NT)
        yy = mm(cc, h_in) * ea_e
        k_.state[...] = k_.state[...] * ea_e[L - 1 : L, :] + mm(bb, (xd * tail_e).astype(BF16), TN)
        inside = []
        for pair in range(4):
            xp = xd[:, 128 * pair : 128 * pair + 128]
            parts, mixes = [], []
            for part in range(2):
                h = 2 * pair + part
                mixes.append((gram * jnp.exp(cu[:, h : h + 1] - cut[h : h + 1, :] + off)).astype(BF16))
                parts.append(jnp.where(first_half == (part == 0), xp, 0.0).astype(BF16))
            inside.append(mm(jnp.concatenate(mixes, axis=1), jnp.concatenate(parts, axis=0)))
        yy = yy + jnp.concatenate(inside, axis=1)
        keep.y[rows, :] = yy
        zz = keep.pz[rows, :]
        gated = (yy + xs * skip) * (zz * jax.nn.sigmoid(zz))
        k_.sq_tile[k, b, 0:1, :] = as_row(jnp.sum(gated * gated, axis=-1, keepdims=True))
        weighted = gated * par(5, 0, CH)
        k_.gate[rows, :] = weighted.astype(BF16)
        if k == 1:
            gb = (k_.gb1[rows, :].astype(F32) * row_mask(b * L, L)).astype(BF16)
            k_.gb1[rows, :] = gb
            dno = jnp.concatenate([mm(gb, weight(k, O0, 256)), mm(gb, weight(k, O0 + 256, 256))], axis=1)
            k_.dno[rows, :] = dno
            k_.sq_tile[k, b, 1:2, :] = as_row(jnp.sum(dno * weighted, axis=-1, keepdims=True))

    def norm_block(k, b, u):
        par = make_par(k)
        gain = jnp.concatenate([par(6, 0, CH), par(7, 0, CH)], axis=1)
        for i in range(4):
            part = span(b * L + 32 * i, 32)
            a = u[part, :].astype(F32)
            r = lax.rsqrt(jnp.mean(a * a, axis=-1, keepdims=True) + EPS)
            saved[k].n[part, :] = (a * r * gain).astype(BF16)

    def reset_forward(k):
        k_.blkx[...] = jnp.zeros((L + 8, CH), F32)
        k_.blkbc[...] = jnp.zeros((L + 8, 256), F32)
        saved[k].px[0:8, :] = jnp.zeros((8, CH), F32)
        saved[k].pbc[0:8, :] = jnp.zeros((8, 256), F32)
        k_.state[...] = jnp.zeros((NST, CH), F32)

    def output_rows(k, rows, dst):
        for j in range(4):
            wo = walls[k][4 * j : 4 * j + 4, :, O0 : O0 + CH].reshape(256, CH)
            dst[rows, 256 * j : 256 * j + 256] = mm(k_.gate[rows, :], wo, NT).astype(BF16)

    def slice_of(b, place):
        return span(b * L + place * HALF, HALF)

    def spread_slices(link, buf, into, b):
        for j in ORDER:
            link.start(buf.at[slice_of(b, x_of(j))], into.at[b, j - 1], b, x_peer(j))

    def slice_sum(link, buf, into, b):
        link.arrived(into.at[b], b)
        total = buf[slice_of(b, t), :].astype(F32)
        for j in (1, 2, 3):
            total = total + into[b, j - 1].astype(F32)
        return total

    def share_slice(link, buf, b):
        rows = buf.at[slice_of(b, t)]
        for j in ORDER:
            link.start(rows, rows, b, x_peer(j))

    def spread_tile(link, k, b):
        for j in ORDER:
            link.start(k_.sq_tile.at[k, b], k_.sq_in.at[k, b, j], b, x_peer(j))

    def tile_sum(link, k, b):
        link.arrived(k_.sq_in.at[k, b, pl.ds(1, 3)], b)
        k_.sums[k, b] = (
            k_.sq_tile[k, b] + k_.sq_in[k, b, 1] + k_.sq_in[k, b, 2] + k_.sq_in[k, b, 3]
        )

    def factor_column(k, b):
        return as_column(lax.rsqrt(k_.sums[k, b, 0:1, :] / INNER + EPS))

    def hidden_block(b):
        tile_sum(links.sq0, 0, b)
        k_.factors[...] = jnp.broadcast_to(factor_column(0, b), (ROWS, 128))
        factor = k_.factors[span(t * HALF, HALF), :][:, 0:1]
        total = slice_sum(links.p0, k_.pa, k_.ra, b)
        k_.ptot0[b] = total
        rows = slice_of(b, t)
        mask = row_mask(b * L + t * HALF, HALF)
        k_.hid[rows, :] = (mask * (k_.tok[rows, :].astype(F32) + factor * total)).astype(BF16)
        share_slice(links.hids, k_.hid, b)

    links.rows2.arrived(k_.tok.at[pl.ds(0, ROWS)], 0)
    local_tok.wait()
    rows_first(1, k_.cot, k_.gb1)
    for b in range(NB):
        norm_block(0, b, k_.tok)
    reset_forward(0)
    k_.sq_tile[...] = jnp.zeros((2, NB, 8, 128), F32)
    gather_first(3)
    gather_twin(0)
    gather_twin(1)
    gather_done(0)
    gather_done(1)

    def first_forward(b, carry):
        project_block(0, b)
        pl.when(b == 0)(lambda: gather_second(3))
        pl.when(b == 0)(lambda: rows_second(1, k_.gb1))
        pl.when(b >= 2)(lambda: hidden_block(b - 2))
        pl.when(b == 3)(lambda: gather_twin(3))
        forward_block(0, b)
        pl.when(b == 0)(lambda: gather_twin(2))
        spread_tile(links.sq0, 0, b)
        pl.when(b == 0)(lambda: gather_done(2))
        output_rows(0, span(b * L, L), k_.pa)
        spread_slices(links.p0, k_.pa, k_.ra, b)
        return carry

    lax.fori_loop(0, NB, first_forward, 0)

    links.rows2.arrived(k_.tok.at[pl.ds(0, ROWS)], 1)
    links.rows2.sent(k_.tok.at[pl.ds(0, ROWS)], 1)
    local_cot.wait()
    reset_forward(1)
    gather_done(3)

    def second_forward(b, carry):
        pl.when(b < 2)(lambda: hidden_block(b + 2))
        links.hids.arrived(k_.ra.at[b], b)
        norm_block(1, b, k_.hid)
        project_block(1, b)
        forward_block(1, b)
        spread_tile(links.sq1, 1, b)
        return carry

    lax.fori_loop(0, NB, second_forward, 0)
    output_rows(1, pl.ds(0, T), k_.pb)

    upper_low = (iota((L, L), 1) >= iota((L, L), 0)).astype(BF16)
    strict = (iota((L, L), 1) < iota((L, L), 0)).astype(F32)
    strict_low = strict.astype(BF16)

    def reset_backward():
        k_.state[...] = jnp.zeros((NST, CH), F32)
        k_.ggo[...] = jnp.zeros((8, CH), F32)
        k_.gsk[...] = jnp.zeros((8, CH), F32)
        k_.gdt[...] = jnp.zeros((8, 128), F32)
        k_.gdl[...] = jnp.zeros((8, 128), F32)
        k_.tapx[...] = jnp.zeros((5, 8, CH), F32)
        k_.tapbc[...] = jnp.zeros((5, 8, 256), F32)
        k_.dcx[...] = jnp.zeros((L + 8, CH), F32)
        k_.dcbc[...] = jnp.zeros((L + 8, 256), F32)

    def gate_back(k, b, inner, xs, skip):
        par, keep = make_par(k), saved[k]
        rows = span(b * L, L)
        gain_out = par(5, 0, CH)
        factor = factor_column(k, b)
        if k == 1:
            dno = k_.dno[rows, :]
        else:
            gb = k_.gb0[rows, :]
            dno = jnp.concatenate([mm(gb, weight(k, O0, 256)), mm(gb, weight(k, O0 + 256, 256))], axis=1)
        out = keep.y[rows, :] + xs * skip
        zz = keep.pz[rows, :]
        sz = jax.nn.sigmoid(zz)
        silu_z = zz * sz
        gated = out * silu_z
        scaled = gated * factor
        k_.gate[rows, :] = (scaled * gain_out).astype(BF16)
        k_.ggo[...] += fold(dno * scaled)
        dgated = factor * (dno * gain_out) - gated * (factor * factor * factor * (1.0 / INNER) * inner)
        dy = dgated * silu_z
        k_.dproj[rows, Z0 : Z0 + CH] = (dgated * out * (sz * (1.0 + zz - silu_z))).astype(BF16)
        k_.gsk[...] += fold(dy * xs)
        return dy

    def skip_row(k):
        skip = jnp.broadcast_to(make_par(k)(8, 256, 128), (8, 128))
        return mm_exact(skip, head_spread().astype(F32))[0:1, :]

    def gate_block(k, b, inner):
        rows = span(b * L, L)
        cx = saved[k].cx[rows, :]
        k_.dno[rows, :] = gate_back(k, b, inner, cx * jax.nn.sigmoid(cx), skip_row(k))

    def backward_block(k, b, inner, dn_ref, between):
        par, keep = make_par(k), saved[k]
        rows = span(b * L, L)
        spread, collect = head_spread(), head_collect()
        rate = -jnp.exp(par(8, 128, 128))
        skip = skip_row(k)
        v = keep.v[rows, :]
        st = softplus(v)
        cu = mm_exact(tri, st * rate)
        cut = cu.T
        ea = jnp.exp(cu)
        tail = jnp.exp(cu[L - 1 : L, :] - cu)
        st_e = mm_split(st, spread)
        ea_e = mm_split(ea, spread)
        tail_e = mm_split(tail, spread)
        cx = keep.cx[rows, :]
        sx = jax.nn.sigmoid(cx)
        xs = cx * sx
        cbc = keep.cbc[rows, :]
        sbc = jax.nn.sigmoid(cbc)
        bc = (cbc * sbc).astype(BF16)
        bb, cc = bc[:, :NST], bc[:, NST:]
        xd = xs * st_e
        dy = k_.dno[rows, :] if inner is None else gate_back(k, b, inner, xs, skip)
        h_in = keep.h[b]
        h_back = k_.state[...]
        hb_low = h_back.astype(BF16)
        gram = mm(cc, bb, NT)
        xdt = (xd * tail_e).astype(BF16)
        dye = (dy * ea_e).astype(BF16)
        y_in = mm(cc, h_in) * ea_e
        dxd_in = mm(bb, hb_low) * tail_e
        dcc = mm(dye, h_in, NT)
        dbb = mm(xdt, hb_low, NT)
        dgram = jnp.zeros((L, L), F32)
        inside = []
        crossing = jnp.zeros((L, 128), F32)
        for pair in range(4):
            sl = slice(128 * pair, 128 * pair + 128)
            xp = xd[:, sl].astype(BF16)
            dyp = dy[:, sl]
            decs, mixes, parts = [], [], []
            for part in range(2):
                h = 2 * pair + part
                dec = jnp.exp(cu[:, h : h + 1] - cut[h : h + 1, :] + off)
                decs.append(dec)
                mixes.append(gram * dec)
                parts.append(jnp.where(first_half == (part == 0), dyp, 0.0).astype(BF16))
            dy2 = jnp.concatenate(parts, axis=0)
            dmix = mm(dy2, xp, NT)
            dm0, dm1 = dmix[:L, :], dmix[L:, :]
            dgram = dgram + dm0 * decs[0] + dm1 * decs[1]
            inside.append(mm(jnp.concatenate([mixes[0].astype(BF16), mixes[1].astype(BF16)], axis=0), dy2, TN))
            both = jnp.concatenate([(mixes[0] * dm0).astype(BF16), (mixes[1] * dm1).astype(BF16)], axis=1)
            cross = mm(upper_low, both)
            c0 = (cross[:, :L] * strict).astype(BF16)
            c1 = (cross[:, L:] * strict).astype(BF16)
            pick = jnp.concatenate(
                [(lanes == 2 * pair).astype(BF16), (lanes == 2 * pair + 1).astype(BF16)], axis=0
            )
            crossing = crossing + mm(jnp.concatenate([c0, c1], axis=1), pick)
        dgl = dgram.astype(BF16)
        dcc = dcc + mm(dgl, bb)
        dbb = dbb + mm(dgl, cc, TN)
        dxd = jnp.concatenate(inside, axis=1) + dxd_in
        kept = mm_split(jnp.broadcast_to(jnp.sum(h_in.astype(F32) * h_back, axis=0, keepdims=True), (8, CH)), collect)
        kept = kept[0:1, :] * ea[L - 1 : L, :]
        p_in = mm_split(dy * y_in, collect)
        q_in = mm_split(xd * dxd_in, collect)
        dls = crossing + mm_split_right(upper_low, p_in) + mm_split_right(strict_low, q_in) + kept
        k_.state[...] = h_back * ea_e[L - 1 : L, :] + mm(cc, dye, TN)
        dst = dls * rate + mm_split(dxd * xs, collect)
        dv = jnp.where(lanes < 8, dst * jax.nn.sigmoid(v), 0.0)
        k_.dproj[rows, S0:X0] = dv.astype(BF16)
        k_.gdt[...] += fold(dv)
        k_.gdl[...] += fold(dls * st)
        dxs = dy * skip + dxd * st_e
        between()
        k_.dcx[L : L + 8, :] = k_.dcx[0:8, :]
        k_.dcbc[L : L + 8, :] = k_.dcbc[0:8, :]
        k_.dcx[0:L, :] = dxs * (sx * (1.0 + cx - xs))
        k_.dcbc[0:L, :] = jnp.concatenate([dbb, dcc], axis=1) * (sbc * (1.0 + cbc - cbc * sbc))
        window = pl.ds(pl.multiple_of(b * L, 8), L + 8)
        k_.blkx[...] = keep.px[window, :]
        k_.blkbc[...] = keep.pbc[window, :]

        def conv_back(width, first_row, dc, blk, taps, start):
            for j in range(width // 128):
                cols = slice(128 * j, 128 * j + 128)
                d = dc[0:L, cols]
                taps[4, :, cols] += fold(d)
                total = jnp.zeros((L, 128), F32)
                for tap in range(4):
                    taps[tap, :, cols] += fold(d * blk[5 + tap : 5 + tap + L, cols])
                    total = total + par(first_row + tap, 128 * j, 128) * dc[3 - tap : 3 - tap + L, cols]
                k_.dproj[rows, start + 128 * j : start + 128 * j + 128] = total.astype(BF16)

        conv_back(CH, 0, k_.dcx, k_.blkx, k_.tapx, X0)
        conv_back(256, 9, k_.dcbc, k_.blkbc, k_.tapbc, B0)
        for j in range(4):
            wr = slice(4 * j, 4 * j + 4)
            d = mm(k_.dproj[rows, :], walls[k][wr, :, 0:O0].reshape(256, O0), NT)
            cols = slice(256 * j, 256 * j + 256)
            dn_ref[rows, cols] = d.astype(BF16)
            k_.gi[k, :, cols] += fold(d * keep.n[rows, cols].astype(F32))

    def small_grads(k):
        par = make_par(k)
        rate = -jnp.exp(par(8, 128, 128))
        k_.pack[k] = jnp.zeros((16, CH), F32)
        for tap in range(5):
            k_.pack[k, tap : tap + 1, :] = jnp.sum(k_.tapx[tap], axis=0, keepdims=True)
            k_.pack[k, 9 + tap : 10 + tap, 0:256] = jnp.sum(k_.tapbc[tap], axis=0, keepdims=True)
        k_.pack[k, 5:6, :] = jnp.sum(k_.ggo[...], axis=0, keepdims=True)
        k_.pack[k, 8:9, 0:128] = jnp.sum(k_.gdt[...], axis=0, keepdims=True)
        k_.pack[k, 8:9, 128:256] = jnp.sum(k_.gdl[...], axis=0, keepdims=True) * rate
        gs = mm_split(jnp.broadcast_to(jnp.sum(k_.gsk[...], axis=0, keepdims=True), (8, CH)), head_collect())
        k_.pack[k, 8:9, 256:384] = gs[0:1, :]
        gi = jnp.sum(k_.gi[k], axis=0, keepdims=True)
        k_.pack[k, 6:7, :] = gi[:, 0:CH] / par(6, 0, CH)
        k_.pack[k, 7:8, :] = gi[:, CH:D] / par(7, 0, CH)

    def weight_grads(k, part, gb_ref, dst):
        start, size = PARTS[k][part]
        for j in range(4):
            nt = saved[k].n[:, 256 * j : 256 * j + 256].T
            wr = slice(4 * j, 4 * j + 4)

            def put(c, value):
                width = value.shape[1]
                dst[wr, :, c : c + width] = value.astype(BF16).reshape(4, 64, width)

            for c in range(start, min(start + size, O0), 256):
                put(c, mm(nt, k_.dproj[:, c : min(c + 256, start + size, O0)]))
            if start + size > O0:
                gt = gb_ref[:, 256 * j : 256 * j + 256].T
                for c in range(2):
                    put(O0 + 256 * c, mm(gt, k_.gate[:, 256 * c : 256 * c + 256]))
            cols = pl.ds(start, size)
            links.d_twin.start(dst.at[wr, twin_half, cols], k_.theirs.at[k, wr, :, cols], (k, part), twin())

    def input_grad(k, total, u, upstream):
        par = make_par(k)
        gain = jnp.concatenate([par(6, 0, CH), par(7, 0, CH)], axis=1)
        r = lax.rsqrt(jnp.mean(u * u, axis=-1, keepdims=True) + EPS)
        c = total * gain
        back = upstream + r * c - u * (r * r * r * (1.0 / D)) * jnp.sum(c * u, axis=-1, keepdims=True)
        return back

    def turn_block(b):
        rows = slice_of(b, t)
        u = k_.hid[rows, :].astype(F32)
        total = slice_sum(links.dn1, k_.pc, k_.rb, b)
        back = input_grad(1, total, u, k_.gb1[rows, :].astype(F32))
        low = (row_mask(b * L + t * HALF, HALF) * back).astype(BF16)
        k_.gb0[rows, :] = low
        share_slice(links.gbs, k_.gb0, b)
        inner = jnp.sum(low.astype(F32) * k_.ptot0[b], axis=-1, keepdims=True)
        inner = jnp.broadcast_to(inner, (HALF, 128)).T[0:8, :]
        k_.inner_in[b, t] = jnp.concatenate([inner, jnp.zeros((8, 128 - HALF), F32)], axis=1)
        for j in ORDER:
            links.in0.start(k_.inner_in.at[b, t], k_.inner_in.at[b, t], b, x_peer(j))

    def to_owner(b):
        j = lax.rem(b - t + 4, 4)

        def go():
            links.dn0.start(k_.pa.at[span(b * L, L)], k_.dn0_in.at[j - 1], 0, {"tensor": b})

        pl.when(j != 0)(go)

    def reduce_first(k, part, dst):
        cols = pl.ds(*PARTS[k][part])
        links.d_twin.arrived(k_.theirs.at[k, :, :, cols], (k, part))

        def add(i, carry):
            dst[i, my_half, cols] = (
                dst[i, my_half, cols].astype(F32) + k_.theirs[k, i, :, cols].astype(F32)
            ).astype(BF16)
            return carry

        lax.fori_loop(0, 16, add, 0)
        for j in ORDER:
            for r in range(4):
                piece = dst.at[index(lax.rem(a1 + j, 4), r), my_half, cols]
                links.d_first.start(piece, k_.first_in.at[k, j - 1, r, :, cols], (k, part), first_peer(j))

    def bc_direct(k):
        for j in (0,) + ORDER:
            for i in (0,) + ORDER:
                place = lax.rem(a2 + j, 4)
                block = k_.mid.at[k, place, :, span((x_of(i) // 2) * 128, 128)]
                if (j, i) == (0, 0):
                    k_.bc_last[k, 0, 0] = k_.mid[k, place, :, span((t // 2) * 128, 128)]
                else:
                    peer = {"dp": index(a1, place), "tensor": x_of(i)}
                    links.bcx.start(block, k_.bc_last.at[k, j, i], k, peer)

    def bc_sum(k):
        links.bcx.arrived(k_.first_in.at[0, 0, 0, :, pl.ds(0, 15 * 128)], k)
        total = jnp.zeros((HALF, 128), F32)
        for j in range(4):
            for i in range(4):
                total = total + k_.bc_last[k, j, i].astype(F32)
        k_.half[k, :, B0 : B0 + 64] = jnp.where(lax.rem(t, 2) == 0, total[:, 0:64], total[:, 64:128])

    def reduce_second(k, part, dst):
        cols = pl.ds(*PARTS[k][part])
        links.d_first.arrived(k_.first_in.at[k, :, :, :, cols], (k, part))

        def add(r, carry):
            total = dst[index(a1, r), my_half, cols].astype(F32)
            for j in (1, 2, 3):
                total = total + k_.first_in[k, j - 1, r, :, cols].astype(F32)
            k_.mid[k, r, :, cols] = total.astype(BF16)
            return carry

        lax.fori_loop(0, 4, add, 0)
        for j in ORDER:
            piece = k_.mid.at[k, lax.rem(a2 + j, 4), :, cols]
            links.d_second.start(piece, k_.last_in.at[k, j, :, cols], (k, part), second_peer(j))
        if PARTS[k][part][0] == 0:
            bc_direct(k)

    def reduce_last(k, part):
        cols = pl.ds(*PARTS[k][part])
        links.d_second.arrived(k_.last_in.at[k, pl.ds(1, 3), :, cols], (k, part))
        total = k_.mid[k, a2, :, cols].astype(F32)
        for j in (1, 2, 3):
            total = total + k_.last_in[k, j, :, cols].astype(F32)
        k_.half[k, :, cols] = total
        if PARTS[k][part][0] == 0:
            bc_sum(k)

    reset_backward()
    k_.gi[...] = jnp.zeros((2, 8, D), F32)
    for b in range(NB):
        tile_sum(links.sq1, 1, b)

    def second_backward(i, carry):
        b = NB - 1 - i
        inner = as_column(k_.sums[1, b, 1:2, :])
        backward_block(1, b, inner, k_.pc, lambda: pl.when(i >= 2)(lambda: turn_block(b + 2)))
        spread_slices(links.dn1, k_.pc, k_.rb, b)
        return carry

    lax.fori_loop(0, NB, second_backward, 0)
    small_grads(1)
    weight_grads(1, 0, k_.gb1, k_.dw1)
    turn_block(1)

    reset_backward()
    for b in range(NB):
        links.p0.sent(k_.ra.at[b], b)
    gather_sent(3)

    def first_inner(b):
        links.gbs.arrived(k_.ra.at[b], b)
        links.in0.arrived(k_.inner_in.at[b, pl.ds(1, 3)], b)
        row = k_.inner_in[b, 0, 0:1, :]
        for place in range(1, 4):
            row = row + pltpu.roll(k_.inner_in[b, place], HALF * place, 1)[0:1, :]
        return as_column(row)

    def first_backward(i, carry):
        b = NB - 1 - i

        def between():
            def at0():
                reduce_first(1, 0, k_.dw1)
                turn_block(0)

            def at1():
                for j in ORDER:
                    links.p1.start(k_.pb.at[span(x_of(j) * ROWS, ROWS)], k_.p1_in.at[j - 1], 0, x_peer(j))

            pl.when(i == 0)(at0)
            pl.when(i == 1)(at1)

        backward_block(0, b, first_inner(b), k_.pa, between)
        return carry

    lax.fori_loop(0, 2, first_backward, 0)
    gate_block(0, 1, first_inner(1))
    gate_block(0, 0, first_inner(0))
    to_owner(3)
    to_owner(2)
    weight_grads(0, 0, k_.gb0, k_.wall1)

    def last_backward(i, carry):
        b = 1 - i

        def between():
            pl.when(i == 0)(lambda: reduce_first(0, 0, k_.wall1))
            pl.when(i == 1)(lambda: reduce_second(1, 0, k_.dw1))

        backward_block(0, b, None, k_.pa, between)
        to_owner(b)
        return carry

    lax.fori_loop(0, 2, last_backward, 0)
    small_grads(0)
    links.small.start(k_.pack.at[1 - s], k_.pack_in.at[0], 0, twin())
    weight_grads(0, 1, k_.gb0, k_.wall1)

    links.small.arrived(k_.pack_in.at[0], 0)
    k_.run[0] = k_.pack[s] + k_.pack_in[0]
    for j in ORDER:
        links.small.start(k_.run.at[0], k_.pack_in.at[j], 1, first_peer(j))
    reduce_first(0, 1, k_.wall1)
    reduce_second(0, 0, k_.wall1)

    def small_step(stage, peers):
        first = 3 * stage - 2
        links.small.arrived(k_.pack_in.at[pl.ds(first, 3)], stage)
        k_.run[stage] = (
            k_.run[stage - 1] + k_.pack_in[first] + k_.pack_in[first + 1] + k_.pack_in[first + 2]
        )
        for j in ORDER:
            links.small.start(k_.run.at[stage], k_.pack_in.at[first + 2 + j], stage + 1, peers(j))

    small_step(1, second_peer)
    reduce_second(0, 1, k_.wall1)
    small_step(2, x_peer)
    reduce_last(1, 0)
    reduce_last(0, 0)
    links.p1.arrived(k_.p1_in, 0)
    total = k_.pb[rows_t, :].astype(F32)
    for j in range(3):
        total = total + k_.p1_in[j].astype(F32)
    mask = row_mask(t * ROWS, ROWS)
    factor = factor_column(1, t)
    k_.los[0] = k_.hid[rows_t, :]
    k_.los[1] = (mask * (k_.hid[rows_t, :].astype(F32) + factor * total)).astype(BF16)
    links.outs.start(k_.los.at[1 - s], k_.lo.at[s], 0, twin())
    keep_lo = pltpu.make_async_copy(k_.los.at[s], k_.lo.at[s], lsem.at[2])
    keep_lo.start()
    links.dn0.arrived(k_.dn0_in, 0)
    total = k_.pa[rows_t, :].astype(F32)
    for j in range(3):
        total = total + k_.dn0_in[j].astype(F32)
    k_.igs[0] = input_grad(0, total, k_.tok[rows_t, :].astype(F32), k_.gb0[rows_t, :].astype(F32))
    k_.igs[1] = k_.gb0[rows_t, :].astype(F32)
    links.outs.start(k_.igs.at[1 - s], k_.ig.at[s], 1, twin())
    keep_ig = pltpu.make_async_copy(k_.igs.at[s], k_.ig.at[s], lsem.at[3])
    keep_ig.start()
    reduce_last(0, 1)
    links.shard.start(k_.half.at[1 - s], k_.other_half, 0, twin())
    links.shard.arrived(k_.other_half, 0)
    mine, others = k_.half[s], k_.other_half[...]
    k_.shard_out[my_half, :] = mine
    k_.shard_out[twin_half, :] = others
    links.small.arrived(k_.pack_in.at[pl.ds(7, 3)], 3)
    over_x = k_.run[2] + k_.pack_in[7] + k_.pack_in[8] + k_.pack_in[9]
    row = iota((16, CH), 0)
    shared = (row == 6) | (row == 7) | (row >= 9)
    over_x = jnp.where(shared, over_x, k_.run[2])
    k_.small_out[...] = over_x
    chosen = over_x[8:16, 0:64]
    for i in range(1, 4):
        chosen = jnp.where(t == i, over_x[8:16, 64 * i : 64 * i + 64], chosen)
    k_.small_out[9:14, 0:64] = chosen[1:6, :]

    keep_lo.wait()
    keep_ig.wait()
    links.outs.arrived(k_.los.at[0], 0)
    links.outs.arrived(k_.igs.at[0], 1)
    links.outs.sent(k_.los.at[0], 0)
    links.outs.sent(k_.igs.at[0], 1)
    links.params.sent(k_.par_own, 0)
    links.shard.sent(k_.other_half, 0)
    links.small.sent(k_.run.at[0], 0)
    for i in range(1, 4):
        links.small.sent(k_.run, i)
    links.early.sent(k_.bc_in.at[pl.ds(1, 3)], 0)
    links.early.sent(k_.par_in.at[pl.ds(1, 3)], 1)
    for a in range(2):
        links.rows1.sent(k_.tok.at[rows_t], (a, 0))
        links.rows1.sent(k_.tok.at[rows_t], (a, 1))
    links.rows2.sent(k_.tok.at[pl.ds(0, ROWS)], 0)
    links.p1.sent(k_.p1_in, 0)
    links.dn0.sent(k_.dn0_in, 0)
    for k in range(2):
        links.bcx.sent(k_.first_in.at[0, 0, 0, :, pl.ds(0, 15 * 128)], k)
    for group in range(3):
        gather_sent(group)

    def shard_sent(group):
        cols = pl.ds(*GROUPS[group][1:])
        for i in range(3):
            links.g_first.sent(k_.mid.at[0, pl.ds(0, 2), :, cols], (group, i))
        links.g_first.sent(k_.mid.at[0, 0, :, cols], (group, 3))

    for group in range(4):
        pl.when(s == GROUPS[group][0])(lambda: shard_sent(group))
    for k in range(2):
        for part in range(len(PARTS[k])):
            cols = pl.ds(*PARTS[k][part])
            links.d_twin.sent(k_.theirs.at[k, :, :, cols], (k, part))
            links.d_first.sent(k_.first_in.at[k, :, :, :, cols], (k, part))
            links.d_second.sent(k_.last_in.at[k, pl.ds(1, 3), :, cols], (k, part))
    for b in range(NB):
        links.sq0.sent(k_.sq_in.at[0, b, pl.ds(1, 3)], b)
        links.sq1.sent(k_.sq_in.at[1, b, pl.ds(1, 3)], b)
        links.in0.sent(k_.inner_in.at[b, pl.ds(1, 3)], b)
        for link in (links.hids, links.gbs, links.dn1):
            link.sent(k_.ra.at[b], b)


def unpack_kernel(
    shard, small, lo, ig,
    o_lo, o_ig, o_gi, o_wx, o_wz, o_bc, o_dt, o_cx, o_cb, o_bx, o_bb, o_db, o_dl, o_sk, o_go, o_wo,
):
    o_lo[...] = lo[...]
    o_ig[...] = ig[...]
    o_gi[:, 0:CH] = small[6:7, :]
    o_gi[:, CH:D] = small[7:8, :]
    o_wx[...] = shard[:, X0:Z0]
    o_wz[...] = shard[:, Z0:O0]
    o_bc[...] = shard[:, B0 : B0 + 64]
    steps = shard[:, S0:X0]
    o_dt[...] = jnp.concatenate([steps, steps], axis=0).T[0:8, 0:64]
    o_wo[...] = shard[:, O0:COLS]
    o_cx[...] = small[0:4, :]
    o_bx[...] = small[4:5, :]
    o_go[...] = small[5:6, :]
    o_db[...] = small[8:9, 0:8]
    o_dl[...] = small[8:9, 128:136]
    o_sk[...] = small[8:9, 256:264]
    o_cb[...] = small[9:13, 0:64]
    o_bb[...] = small[13:14, 0:64]


def sds(shape, dtype):
    return jax.ShapeDtypeStruct(shape, dtype)


VM = pl.BlockSpec(memory_space=pltpu.VMEM)
ANY = pl.BlockSpec(memory_space=pl.ANY)


def body(
    tokens_in, cotangent, seq_lengths, gain_in, weight_x, weight_z, weight_bc, weight_dt, conv_x, conv_bc,
    bias_x, bias_bc, dt_bias, decay_log, skip_gain, gain_out, weight_out,
):
    ins = [
        gain_in, weight_x, weight_z, weight_bc, weight_dt.swapaxes(1, 2), conv_x, conv_bc, bias_x, bias_bc, dt_bias,
        decay_log, skip_gain, gain_out, weight_out.swapaxes(1, 2), seq_lengths.T, tokens_in, cotangent,
    ]
    scratch = [pltpu.VMEM(*a) for a in SCRATCH.values()]
    scratch += [pltpu.VMEM(*a) for _ in range(2) for a in SAVED.values()]
    scratch += [pltpu.SemaphoreType.DMA((4,))]
    for shape in LINKS.values():
        scratch += [pltpu.SemaphoreType.DMA(shape)] * 2
    lo, ig, shard, small = pl.pallas_call(
        layer_kernel,
        out_shape=[
            sds((2, ROWS, D), BF16),
            sds((2, ROWS, D), F32),
            sds((64, COLS), F32),
            sds((16, CH), F32),
        ],
        in_specs=[VM] * 15 + [ANY] * 2,
        out_specs=[ANY, ANY, VM, VM],
        scratch_shapes=scratch,
        compiler_params=pltpu.CompilerParams(collective_id=0, has_side_effects=True, vmem_limit_bytes=VMEM_LIMIT),
    )(*ins)
    shapes = [
        (2, ROWS, D), (2, ROWS, D), (1, D), (64, CH), (64, CH), (64, 64), (8, 64), (4, CH), (4, 64), (1, CH), (1, 64),
        (1, 8), (1, 8), (1, 8), (1, CH), (64, CH),
    ]
    found = pl.pallas_call(
        unpack_kernel,
        out_shape=[sds(a, BF16 if i == 0 else F32) for i, a in enumerate(shapes)],
        in_specs=[VM] * 4,
        out_specs=[VM] * 16,
        compiler_params=pltpu.CompilerParams(vmem_limit_bytes=VMEM_LIMIT),
    )(shard, small, lo, ig)
    found = list(found)
    found[6] = found[6].T
    found[15] = found[15].T
    return tuple(a if i in (2, 9, 10, 11, 12, 13, 14) else a[None] for i, a in enumerate(found))


def solution(mesh):
    in_specs = (
        P(None, ("dp", "tensor"), None),
        P(None, ("dp", "tensor"), None),
        P(None, "dp"),
        P("section", None),
        P("section", "dp", "tensor"),
        P("section", "dp", "tensor"),
        P("section", "dp", "tensor"),
        P("section", "dp", "tensor"),
        P("section", None, "tensor"),
        P("section", None, "tensor"),
        P("section", "tensor"),
        P("section", "tensor"),
        P("section", "tensor"),
        P("section", "tensor"),
        P("section", "tensor"),
        P("section", "tensor"),
        P("section", "tensor", "dp"),
    )
    out_specs = (
        P("section", None, ("dp", "tensor"), None),
        P("section", None, ("dp", "tensor"), None),
        P("section", None),
        P("section", "dp", "tensor"),
        P("section", "dp", "tensor"),
        P("section", "dp", "tensor"),
        P("section", "dp", "tensor"),
        P("section", None, "tensor"),
        P("section", None, "tensor"),
        P("section", "tensor"),
        P("section", "tensor"),
        P("section", "tensor"),
        P("section", "tensor"),
        P("section", "tensor"),
        P("section", "tensor"),
        P("section", "tensor", "dp"),
    )
    return jax.shard_map(body, mesh=mesh, in_specs=in_specs, out_specs=out_specs, check_vma=False)
```

```python
import jax
import jax.numpy as jnp
from jax import lax
from jax.experimental import pallas as pl
from jax.experimental.pallas import tpu as pltpu
from jax.sharding import PartitionSpec as P

F32 = jnp.float32
BF16 = jnp.bfloat16
T = 512
L = 128
NB = T // L
D = 1024
CH = 512
INNER = 2048
NST = 128
EPS = 1e-05
B0, S0, X0, Z0, O0, COLS = 0, 256, 384, 896, 1408, 1920
VMEM_LIMIT = 60 * 2**20
MESH = pl.DeviceIdType.MESH
ROWS = 128
HALF = 32
ORDER = (1, 3, 2)

NN = (((1,), (0,)), ((), ()))
NT = (((1,), (1,)), ((), ()))
TN = (((0,), (0,)), ((), ()))


def mm(a, b, dims=NN):
    return lax.dot_general(a, b, dims, preferred_element_type=F32)


def mm_exact(a, b):
    return lax.dot_general(a, b, NN, precision=lax.Precision.HIGHEST, preferred_element_type=F32)


def mm_split(a, b):
    hi = a.astype(BF16)
    lo = (a - hi.astype(F32)).astype(BF16)
    return mm(hi, b) + mm(lo, b)


def mm_split_right(a, b):
    hi = b.astype(BF16)
    lo = (b - hi.astype(F32)).astype(BF16)
    return mm(a, hi) + mm(a, lo)


def iota(shape, dim):
    return lax.broadcasted_iota(jnp.int32, shape, dim)


def as_row(column):
    return jnp.broadcast_to(column, (L, 128)).T[0:1, :]


def as_column(row):
    return jnp.broadcast_to(row, (128, L)).T[:, 0:1]


def softplus(v):
    return jnp.maximum(v, 0.0) + jnp.log1p(jnp.exp(-jnp.abs(v)))


def head_spread():
    return (iota((128, CH), 1) // 64 == iota((128, CH), 0)).astype(BF16)


def head_collect():
    return (iota((CH, 128), 0) // 64 == iota((CH, 128), 1)).astype(BF16)


def fold(a):
    return jnp.sum(a.reshape(a.shape[0] // 8, 8, a.shape[1]), axis=0)


def span(start, size):
    return pl.ds(pl.multiple_of(start, size), size)


def places():
    group = lax.axis_index("dp")
    return lax.axis_index("section"), group // 4, lax.rem(group, 4), lax.axis_index("tensor")


def x_peer(j):
    return {"tensor": lax.rem(lax.axis_index("tensor") + j, 4)}


def twin():
    return {"section": 1 - lax.axis_index("section")}


def greet(peers):
    for peer in peers:
        pl.semaphore_signal(pltpu.get_barrier_semaphore(), inc=1, device_id=peer, device_id_type=MESH)


def greeted(peers):
    pl.semaphore_wait(pltpu.get_barrier_semaphore(), len(peers))


class Link:
    def __init__(self, send_sems, recv_sems):
        self.send_sems, self.recv_sems = send_sems, recv_sems

    def copy(self, src, dst, at, peer):
        return pltpu.make_async_remote_copy(
            src_ref=src,
            dst_ref=dst,
            send_sem=self.send_sems.at[at],
            recv_sem=self.recv_sems.at[at],
            device_id=peer,
            device_id_type=MESH,
        )

    def start(self, src, dst, at, peer):
        self.copy(src, dst, at, peer).start()

    def arrived(self, like, at):
        self.copy(like, like, at, twin()).wait_recv()

    def sent(self, like, at):
        self.copy(like, like, at, twin()).wait_send()


SCRATCH = dict(
    wall0=((16, 64, COLS), BF16),
    wall1=((16, 64, COLS), BF16),
    dw1=((16, 64, COLS), BF16),
    theirs=((2, 16, HALF, COLS), BF16),
    first_in=((2, 3, 4, HALF, COLS), BF16),
    mid=((2, 4, HALF, COLS), BF16),
    last_in=((2, 4, HALF, COLS), BF16),
    half=((2, HALF, COLS), F32),
    other_half=((HALF, COLS), F32),
    own=((64, COLS), BF16),
    bc_in=((4, 64, 128), BF16),
    par_own=((16, CH), F32),
    par_x=((8, 128), F32),
    par_in=((4, 8, 128), F32),
    run=((3, 16, CH), F32),
    square=((128, 128), F32),
    par_all=((2, 16, CH), F32),
    tok=((T, D), BF16),
    hid=((T, D), BF16),
    gb1=((T, D), BF16),
    gb0=((T, D), BF16),
    pa=((T, D), BF16),
    pb=((T, D), BF16),
    pc=((T, D), BF16),
    ra=((NB, 3, HALF, D), BF16),
    rb=((NB, 3, HALF, D), BF16),
    p1_in=((3, ROWS, D), BF16),
    dn0_in=((3, ROWS, D), BF16),
    ptot0=((NB, HALF, D), F32),
    sq_tile=((2, NB, 8, 128), F32),
    sq_in=((2, NB, 4, 8, 128), F32),
    sums=((2, NB, 8, 128), F32),
    inner_in=((NB, 4, 8, 128), F32),
    factors=((ROWS, 128), F32),
    dno=((T, CH), F32),
    blkx=((L + 8, CH), F32),
    blkbc=((L + 8, 256), F32),
    dcx=((L + 8, CH), F32),
    dcbc=((L + 8, 256), F32),
    gate=((T, CH), BF16),
    dproj=((T, 1408), BF16),
    state=((NST, CH), F32),
    ggo=((8, CH), F32),
    gsk=((8, CH), F32),
    gdt=((8, 128), F32),
    gdl=((8, 128), F32),
    tapx=((5, 8, CH), F32),
    tapbc=((5, 8, 256), F32),
    gi=((2, 8, D), F32),
    pack=((2, 16, CH), F32),
    pack_in=((10, 16, CH), F32),
    bc_last=((2, 4, 4, HALF, 128), BF16),
    los=((2, ROWS, D), BF16),
    igs=((2, ROWS, D), F32),
)
SAVED = dict(
    n=((T, D), BF16),
    px=((T + 8, CH), F32),
    cx=((T, CH), F32),
    pz=((T, CH), F32),
    pbc=((T + 8, 256), F32),
    cbc=((T, 256), F32),
    v=((T, 128), F32),
    y=((T, CH), F32),
    h=((NB, NST, CH), BF16),
)
LINKS = dict(
    early=(2,),
    rows1=(2, 2),
    rows2=(2,),
    params=(1,),
    g_first=(4, 4),
    g_second=(4, 3),
    g_twin=(4,),
    p0=(NB,),
    sq0=(NB,),
    hids=(NB,),
    sq1=(NB,),
    dn1=(NB,),
    gbs=(NB,),
    in0=(NB,),
    p1=(1,),
    dn0=(1,),
    d_twin=(2, 2),
    d_first=(2, 2),
    d_second=(2, 2),
    shard=(1,),
    small=(4,),
    bcx=(2,),
    outs=(2,),
)
GROUPS = ((0, X0, O0 - X0), (0, B0, X0), (0, O0, COLS - O0), (1, 0, COLS))
PARTS = (((Z0, COLS - Z0), (0, Z0)), ((0, COLS),))
INPUTS = (
    "gain_in", "weight_x", "weight_z", "weight_bc", "weight_dt", "conv_x", "conv_bc", "bias_x", "bias_bc", "dt_bias",
    "decay_log", "skip_gain", "gain_out", "weight_out", "lens", "tokens", "cot",
)
OUTPUTS = ("lo", "ig", "shard_out", "small_out")


class Names:
    def __init__(self, **kw):
        self.__dict__.update(kw)


def layer_kernel(*refs):
    names = list(INPUTS) + list(OUTPUTS) + list(SCRATCH)
    names += [f"{n}{k}" for k in range(2) for n in SAVED]
    k_ = Names(**dict(zip(names, refs)))
    rest = refs[len(names) :]
    lsem = rest[0]
    links = Names(**{n: Link(rest[1 + 2 * i], rest[2 + 2 * i]) for i, n in enumerate(LINKS)})
    saved = [Names(**{n: getattr(k_, f"{n}{k}") for n in SAVED}) for k in range(2)]
    walls = (k_.wall0, k_.wall1)
    s, z, y, t = places()
    own_d = z * 4 + y
    a1 = (1 - s) * y + s * z
    a2 = (1 - s) * z + s * y

    def index(first, second):
        return (1 - s) * (4 * second + first) + s * (4 * first + second)

    def first_peer(j):
        return {"dp": index(lax.rem(a1 + j, 4), a2)}

    def second_peer(j):
        return {"dp": index(a1, lax.rem(a2 + j, 4))}

    def x_of(j):
        return lax.rem(t + j, 4)

    my_half = span(HALF * s, HALF)
    twin_half = span(HALF * (1 - s), HALF)

    def y_peer(j, section):
        return {"section": section, "dp": z * 4 + lax.rem(y + j, 4)}

    def z_peer(j, section):
        return {"section": section, "dp": lax.rem(z + j, 4) * 4 + y}

    everyone = [x_peer(j) for j in ORDER] + [twin()]
    everyone += [peer(j, section) for peer in (y_peer, z_peer) for section in range(2) for j in ORDER]
    everyone += [{"dp": index(a1, lax.rem(a2 + j, 4)), "tensor": x_of(i)} for j in ORDER for i in ORDER]
    greet(everyone)

    k_.par_own[...] = jnp.zeros((16, CH), F32)
    k_.par_own[0:4, :] = k_.conv_x[0]
    k_.par_own[4:5, :] = k_.bias_x[...]
    k_.par_own[5:6, :] = k_.gain_out[...]
    k_.par_own[6:7, :] = k_.gain_in[:, 0:CH]
    k_.par_own[7:8, :] = k_.gain_in[:, CH:D]
    k_.par_own[8:9, 0:8] = k_.dt_bias[...]
    k_.par_own[8:9, 128:136] = k_.decay_log[...]
    k_.par_own[8:9, 256:264] = k_.skip_gain[...]
    k_.par_x[...] = jnp.zeros((8, 128), F32)
    k_.par_x[0:4, 0:64] = k_.conv_bc[0]
    k_.par_x[4:5, 0:64] = k_.bias_bc[...]
    k_.par_in[0] = k_.par_x[...]
    k_.bc_in[0] = jnp.zeros((64, 128), BF16)
    k_.bc_in[0, :, 0:64] = k_.weight_bc[0]
    k_.own[:, X0:Z0] = k_.weight_x[0]
    k_.own[:, Z0:O0] = k_.weight_z[0]
    k_.own[:, O0:COLS] = k_.weight_out[0]
    k_.square[...] = jnp.zeros((128, 128), F32)
    k_.square[0:8, 0:64] = k_.weight_dt[0].astype(F32)
    k_.own[:, S0:X0] = k_.square[...].T[0:64, :].astype(BF16)
    rows_t = span(t * ROWS, ROWS)
    local_tok = pltpu.make_async_copy(k_.tokens.at[s], k_.tok.at[rows_t], lsem.at[0])
    local_cot = pltpu.make_async_copy(k_.cot.at[s], k_.gb1.at[rows_t], lsem.at[1])
    local_tok.start()
    local_cot.start()
    greeted(everyone)
    for j in ORDER:
        links.early.start(k_.bc_in.at[0], k_.bc_in.at[j], 0, x_peer(j))
        links.early.start(k_.par_x, k_.par_in.at[j], 1, x_peer(j))

    def shard_to_all(group):
        k, start, size = GROUPS[group]
        cols = pl.ds(start, size)

        def part(half):
            rows = pl.ds(half * HALF, HALF)
            return k_.own.at[rows, cols], walls[k].at[own_d, rows, cols]

        for half, peer in enumerate((y_peer, z_peer)):
            for i, j in enumerate(ORDER):
                links.g_first.start(*part(half), (group, i), peer(j, half))
        links.g_first.start(*part(1 - k), (group, 3), twin())
        rows = pl.ds(k * HALF, HALF)
        walls[k][own_d, rows, cols] = k_.own[rows, cols]

    def gather_first(group):
        pl.when(s == GROUPS[group][0])(lambda: shard_to_all(group))

    def gather_second(group):
        k, start, size = GROUPS[group]
        for r in (0,) + ORDER:
            piece = walls[k].at[index(lax.rem(a1 - r + 4, 4), a2), my_half, pl.ds(start, size)]
            if r:
                links.g_first.arrived(piece, (group, ORDER.index(r)))
            else:
                pl.when(s != k)(lambda: links.g_first.arrived(piece, (group, 3)))
            for i, j in enumerate(ORDER):
                links.g_second.start(piece, piece, (group, i), second_peer(j))
            links.g_twin.start(piece, piece, group, twin())

    def gather_twin(group):
        k, start, size = GROUPS[group]
        for i, j in enumerate(ORDER):
            links.g_second.arrived(k_.mid.at[0, :, :, pl.ds(start, size)], (group, i))
            for r in (0,) + ORDER:
                place = index(lax.rem(a1 - r + 4, 4), lax.rem(a2 - j + 4, 4))
                piece = walls[k].at[place, my_half, pl.ds(start, size)]
                links.g_twin.start(piece, piece, group, twin())

    def gather_done(group):
        links.g_twin.arrived(k_.theirs.at[0, :, :, pl.ds(*GROUPS[group][1:])], group)

    def gather_sent(group):
        cols = pl.ds(*GROUPS[group][1:])
        for i in range(3):
            links.g_second.sent(k_.mid.at[0, :, :, cols], (group, i))
        links.g_twin.sent(k_.theirs.at[0, :, :, cols], group)

    def rows_first(a, src, dst):
        links.rows1.start(src.at[s], dst.at[rows_t], (a, 0), x_peer(1))
        links.rows1.start(src.at[s], dst.at[rows_t], (a, 1), x_peer(3))

    def rows_second(a, dst):
        links.rows1.arrived(dst.at[rows_t], (a, 0))
        upper = dst.at[span(x_of(3) * ROWS, ROWS // 2)]
        links.rows2.start(upper, upper, a, x_peer(1))
        links.rows1.arrived(dst.at[rows_t], (a, 1))
        lower_rows = dst.at[span(x_of(1) * ROWS + ROWS // 2, ROWS // 2)]
        links.rows2.start(lower_rows, lower_rows, a, x_peer(3))

    gather_first(0)
    rows_first(0, k_.tokens, k_.tok)
    gather_second(0)
    links.early.arrived(k_.bc_in.at[pl.ds(1, 3)], 0)
    links.early.arrived(k_.par_in.at[pl.ds(1, 3)], 1)
    left = iota((64, 128), 1) < 64
    left8 = iota((8, 128), 1) < 64
    slots = [lax.rem(t - i + 4, 4) for i in range(4)]
    for i in range(2):
        cols = slice(128 * i, 128 * i + 128)
        right = pltpu.roll(k_.bc_in[slots[2 * i + 1]].astype(F32), 64, 1)
        k_.own[:, cols] = jnp.where(left, k_.bc_in[slots[2 * i]].astype(F32), right).astype(BF16)
        right = pltpu.roll(k_.par_in[slots[2 * i + 1]], 64, 1)
        k_.par_own[9:14, cols] = jnp.where(left8, k_.par_in[slots[2 * i]], right)[0:5, :]
    gather_first(1)
    gather_first(2)
    k_.par_all[s] = k_.par_own[...]
    links.params.start(k_.par_own, k_.par_all.at[s], 0, twin())
    rows_second(0, k_.tok)
    gather_second(1)
    gather_second(2)
    links.params.arrived(k_.par_own, 0)

    length = jnp.where(s == 0, k_.lens[:, 0:1], k_.lens[:, 1:2])

    def row_mask(start, rows):
        return (iota((rows, 1), 0) + start < length).astype(F32)

    lower = iota((L, L), 0) >= iota((L, L), 1)
    tri = lower.astype(F32)
    off = jnp.where(lower, 0.0, -1e30)
    first_half = iota((L, 128), 1) < 64
    lanes = iota((L, 128), 1)

    def make_par(k):
        def par(row, start, size):
            return k_.par_all[k, row : row + 1, start : start + size]

        return par

    def weight(k, start, size):
        return walls[k][:, :, start : start + size].reshape(D, size)

    def project_block(k, b):
        par, keep = make_par(k), saved[k]
        rows = span(b * L, L)
        n = keep.n[rows, :]
        k_.blkbc[0:8, :] = k_.blkbc[L : L + 8, :]
        k_.blkx[0:8, :] = k_.blkx[L : L + 8, :]
        k_.blkbc[8 : 8 + L, :] = mm(n, weight(k, B0, 256))
        v = mm(n, weight(k, S0, 128)) + par(8, 0, 128)
        keep.v[rows, :] = v
        for j in range(2):
            k_.blkx[8 : 8 + L, 256 * j : 256 * j + 256] = mm(n, weight(k, X0 + 256 * j, 256))
        for j in range(2):
            keep.pz[rows, 256 * j : 256 * j + 256] = mm(n, weight(k, Z0 + 256 * j, 256))
        shifted = pl.ds(pl.multiple_of(b * L + 8, 8), L)
        keep.px[shifted, :] = k_.blkx[8 : 8 + L, :]
        keep.pbc[shifted, :] = k_.blkbc[8 : 8 + L, :]
        for j in range(4):
            cols = slice(128 * j, 128 * j + 128)
            c = par(4, 128 * j, 128)
            for tap in range(4):
                c = c + par(tap, 128 * j, 128) * k_.blkx[5 + tap : 5 + tap + L, cols]
            keep.cx[rows, cols] = c
        for j in range(2):
            cols = slice(128 * j, 128 * j + 128)
            c = par(13, 128 * j, 128)
            for tap in range(4):
                c = c + par(9 + tap, 128 * j, 128) * k_.blkbc[5 + tap : 5 + tap + L, cols]
            keep.cbc[rows, cols] = c

    def forward_block(k, b):
        par, keep = make_par(k), saved[k]
        rows = span(b * L, L)
        spread = head_spread()
        rate = -jnp.exp(par(8, 128, 128))
        skip = mm_exact(jnp.broadcast_to(par(8, 256, 128), (8, 128)), spread.astype(F32))[0:1, :]
        st = softplus(keep.v[rows, :])
        cu = mm_exact(tri, st * rate)
        cut = cu.T
        ea = jnp.exp(cu)
        tail = jnp.exp(cu[L - 1 : L, :] - cu)
        st_e = mm_split(st, spread)
        ea_e = mm_split(ea, spread)
        tail_e = mm_split(tail, spread)
        cx = keep.cx[rows, :]
        xs = cx * jax.nn.sigmoid(cx)
        cbc = keep.cbc[rows, :]
        bc = (cbc * jax.nn.sigmoid(cbc)).astype(BF16)
        bb, cc = bc[:, :NST], bc[:, NST:]
        xd = xs * st_e
        h_in = k_.state[...].astype(BF16)
        keep.h[b] = h_in
        gram = mm(cc, bb, NT)
        yy = mm(cc, h_in) * ea_e
        k_.state[...] = k_.state[...] * ea_e[L - 1 : L, :] + mm(bb, (xd * tail_e).astype(BF16), TN)
        inside = []
        for pair in range(4):
            xp = xd[:, 128 * pair : 128 * pair + 128]
            parts, mixes = [], []
            for part in range(2):
                h = 2 * pair + part
                mixes.append((gram * jnp.exp(cu[:, h : h + 1] - cut[h : h + 1, :] + off)).astype(BF16))
                parts.append(jnp.where(first_half == (part == 0), xp, 0.0).astype(BF16))
            inside.append(mm(jnp.concatenate(mixes, axis=1), jnp.concatenate(parts, axis=0)))
        yy = yy + jnp.concatenate(inside, axis=1)
        keep.y[rows, :] = yy
        zz = keep.pz[rows, :]
        gated = (yy + xs * skip) * (zz * jax.nn.sigmoid(zz))
        k_.sq_tile[k, b, 0:1, :] = as_row(jnp.sum(gated * gated, axis=-1, keepdims=True))
        weighted = gated * par(5, 0, CH)
        k_.gate[rows, :] = weighted.astype(BF16)
        if k == 1:
            gb = (k_.gb1[rows, :].astype(F32) * row_mask(b * L, L)).astype(BF16)
            k_.gb1[rows, :] = gb
            dno = jnp.concatenate([mm(gb, weight(k, O0, 256)), mm(gb, weight(k, O0 + 256, 256))], axis=1)
            k_.dno[rows, :] = dno
            k_.sq_tile[k, b, 1:2, :] = as_row(jnp.sum(dno * weighted, axis=-1, keepdims=True))

    def norm_block(k, b, u):
        par = make_par(k)
        gain = jnp.concatenate([par(6, 0, CH), par(7, 0, CH)], axis=1)
        for i in range(4):
            part = span(b * L + 32 * i, 32)
            a = u[part, :].astype(F32)
            r = lax.rsqrt(jnp.mean(a * a, axis=-1, keepdims=True) + EPS)
            saved[k].n[part, :] = (a * r * gain).astype(BF16)

    def reset_forward(k):
        k_.blkx[...] = jnp.zeros((L + 8, CH), F32)
        k_.blkbc[...] = jnp.zeros((L + 8, 256), F32)
        saved[k].px[0:8, :] = jnp.zeros((8, CH), F32)
        saved[k].pbc[0:8, :] = jnp.zeros((8, 256), F32)
        k_.state[...] = jnp.zeros((NST, CH), F32)

    def output_rows(k, rows, dst):
        for j in range(4):
            wo = walls[k][4 * j : 4 * j + 4, :, O0 : O0 + CH].reshape(256, CH)
            dst[rows, 256 * j : 256 * j + 256] = mm(k_.gate[rows, :], wo, NT).astype(BF16)

    def slice_of(b, place):
        return span(b * L + place * HALF, HALF)

    def spread_slices(link, buf, into, b):
        for j in ORDER:
            link.start(buf.at[slice_of(b, x_of(j))], into.at[b, j - 1], b, x_peer(j))

    def slice_sum(link, buf, into, b):
        link.arrived(into.at[b], b)
        total = buf[slice_of(b, t), :].astype(F32)
        for j in (1, 2, 3):
            total = total + into[b, j - 1].astype(F32)
        return total

    def share_slice(link, buf, b):
        rows = buf.at[slice_of(b, t)]
        for j in ORDER:
            link.start(rows, rows, b, x_peer(j))

    def spread_tile(link, k, b):
        for j in ORDER:
            link.start(k_.sq_tile.at[k, b], k_.sq_in.at[k, b, j], b, x_peer(j))

    def tile_sum(link, k, b):
        link.arrived(k_.sq_in.at[k, b, pl.ds(1, 3)], b)
        k_.sums[k, b] = (
            k_.sq_tile[k, b] + k_.sq_in[k, b, 1] + k_.sq_in[k, b, 2] + k_.sq_in[k, b, 3]
        )

    def factor_column(k, b):
        return as_column(lax.rsqrt(k_.sums[k, b, 0:1, :] / INNER + EPS))

    def hidden_block(b):
        tile_sum(links.sq0, 0, b)
        k_.factors[...] = jnp.broadcast_to(factor_column(0, b), (ROWS, 128))
        factor = k_.factors[span(t * HALF, HALF), :][:, 0:1]
        total = slice_sum(links.p0, k_.pa, k_.ra, b)
        k_.ptot0[b] = total
        rows = slice_of(b, t)
        mask = row_mask(b * L + t * HALF, HALF)
        k_.hid[rows, :] = (mask * (k_.tok[rows, :].astype(F32) + factor * total)).astype(BF16)
        share_slice(links.hids, k_.hid, b)

    links.rows2.arrived(k_.tok.at[pl.ds(0, ROWS)], 0)
    local_tok.wait()
    rows_first(1, k_.cot, k_.gb1)
    for b in range(NB):
        norm_block(0, b, k_.tok)
    reset_forward(0)
    k_.sq_tile[...] = jnp.zeros((2, NB, 8, 128), F32)
    gather_first(3)
    gather_twin(0)
    gather_twin(1)
    gather_done(0)
    gather_done(1)

    def first_forward(b, carry):
        project_block(0, b)
        pl.when(b >= 2)(lambda: hidden_block(b - 2))
        pl.when(b == 3)(lambda: gather_twin(3))
        forward_block(0, b)
        pl.when(b == 0)(lambda: gather_twin(2))
        spread_tile(links.sq0, 0, b)
        pl.when(b == 0)(lambda: gather_done(2))
        output_rows(0, span(b * L, L), k_.pa)
        spread_slices(links.p0, k_.pa, k_.ra, b)
        pl.when(b == 0)(lambda: gather_second(3))
        pl.when(b == 0)(lambda: rows_second(1, k_.gb1))
        return carry

    lax.fori_loop(0, NB, first_forward, 0)

    links.rows2.arrived(k_.tok.at[pl.ds(0, ROWS)], 1)
    links.rows2.sent(k_.tok.at[pl.ds(0, ROWS)], 1)
    local_cot.wait()
    reset_forward(1)
    gather_done(3)

    def second_forward(b, carry):
        pl.when(b < 2)(lambda: hidden_block(b + 2))
        links.hids.arrived(k_.ra.at[b], b)
        norm_block(1, b, k_.hid)
        project_block(1, b)
        forward_block(1, b)
        spread_tile(links.sq1, 1, b)
        return carry

    lax.fori_loop(0, NB, second_forward, 0)
    output_rows(1, pl.ds(0, T), k_.pb)

    upper_low = (iota((L, L), 1) >= iota((L, L), 0)).astype(BF16)
    strict = (iota((L, L), 1) < iota((L, L), 0)).astype(F32)
    strict_low = strict.astype(BF16)

    def reset_backward():
        k_.state[...] = jnp.zeros((NST, CH), F32)
        k_.ggo[...] = jnp.zeros((8, CH), F32)
        k_.gsk[...] = jnp.zeros((8, CH), F32)
        k_.gdt[...] = jnp.zeros((8, 128), F32)
        k_.gdl[...] = jnp.zeros((8, 128), F32)
        k_.tapx[...] = jnp.zeros((5, 8, CH), F32)
        k_.tapbc[...] = jnp.zeros((5, 8, 256), F32)
        k_.dcx[...] = jnp.zeros((L + 8, CH), F32)
        k_.dcbc[...] = jnp.zeros((L + 8, 256), F32)

    def gate_back(k, b, inner, xs, skip):
        par, keep = make_par(k), saved[k]
        rows = span(b * L, L)
        gain_out = par(5, 0, CH)
        factor = factor_column(k, b)
        if k == 1:
            dno = k_.dno[rows, :]
        else:
            gb = k_.gb0[rows, :]
            dno = jnp.concatenate([mm(gb, weight(k, O0, 256)), mm(gb, weight(k, O0 + 256, 256))], axis=1)
        out = keep.y[rows, :] + xs * skip
        zz = keep.pz[rows, :]
        sz = jax.nn.sigmoid(zz)
        silu_z = zz * sz
        gated = out * silu_z
        scaled = gated * factor
        k_.gate[rows, :] = (scaled * gain_out).astype(BF16)
        k_.ggo[...] += fold(dno * scaled)
        dgated = factor * (dno * gain_out) - gated * (factor * factor * factor * (1.0 / INNER) * inner)
        dy = dgated * silu_z
        k_.dproj[rows, Z0 : Z0 + CH] = (dgated * out * (sz * (1.0 + zz - silu_z))).astype(BF16)
        k_.gsk[...] += fold(dy * xs)
        return dy

    def skip_row(k):
        skip = jnp.broadcast_to(make_par(k)(8, 256, 128), (8, 128))
        return mm_exact(skip, head_spread().astype(F32))[0:1, :]

    def gate_block(k, b, inner):
        rows = span(b * L, L)
        cx = saved[k].cx[rows, :]
        k_.dno[rows, :] = gate_back(k, b, inner, cx * jax.nn.sigmoid(cx), skip_row(k))

    def backward_block(k, b, inner, dn_ref, between):
        par, keep = make_par(k), saved[k]
        rows = span(b * L, L)
        spread, collect = head_spread(), head_collect()
        rate = -jnp.exp(par(8, 128, 128))
        skip = skip_row(k)
        v = keep.v[rows, :]
        st = softplus(v)
        cu = mm_exact(tri, st * rate)
        cut = cu.T
        ea = jnp.exp(cu)
        tail = jnp.exp(cu[L - 1 : L, :] - cu)
        st_e = mm_split(st, spread)
        ea_e = mm_split(ea, spread)
        tail_e = mm_split(tail, spread)
        cx = keep.cx[rows, :]
        sx = jax.nn.sigmoid(cx)
        xs = cx * sx
        cbc = keep.cbc[rows, :]
        sbc = jax.nn.sigmoid(cbc)
        bc = (cbc * sbc).astype(BF16)
        bb, cc = bc[:, :NST], bc[:, NST:]
        xd = xs * st_e
        dy = k_.dno[rows, :] if inner is None else gate_back(k, b, inner, xs, skip)
        h_in = keep.h[b]
        h_back = k_.state[...]
        hb_low = h_back.astype(BF16)
        gram = mm(cc, bb, NT)
        xdt = (xd * tail_e).astype(BF16)
        dye = (dy * ea_e).astype(BF16)
        y_in = mm(cc, h_in) * ea_e
        dxd_in = mm(bb, hb_low) * tail_e
        dcc = mm(dye, h_in, NT)
        dbb = mm(xdt, hb_low, NT)
        dgram = jnp.zeros((L, L), F32)
        inside = []
        crossing = jnp.zeros((L, 128), F32)
        for pair in range(4):
            sl = slice(128 * pair, 128 * pair + 128)
            xp = xd[:, sl].astype(BF16)
            dyp = dy[:, sl]
            decs, mixes, parts = [], [], []
            for part in range(2):
                h = 2 * pair + part
                dec = jnp.exp(cu[:, h : h + 1] - cut[h : h + 1, :] + off)
                decs.append(dec)
                mixes.append(gram * dec)
                parts.append(jnp.where(first_half == (part == 0), dyp, 0.0).astype(BF16))
            dy2 = jnp.concatenate(parts, axis=0)
            dmix = mm(dy2, xp, NT)
            dm0, dm1 = dmix[:L, :], dmix[L:, :]
            dgram = dgram + dm0 * decs[0] + dm1 * decs[1]
            inside.append(mm(jnp.concatenate([mixes[0].astype(BF16), mixes[1].astype(BF16)], axis=0), dy2, TN))
            both = jnp.concatenate([(mixes[0] * dm0).astype(BF16), (mixes[1] * dm1).astype(BF16)], axis=1)
            cross = mm(upper_low, both)
            c0 = (cross[:, :L] * strict).astype(BF16)
            c1 = (cross[:, L:] * strict).astype(BF16)
            pick = jnp.concatenate(
                [(lanes == 2 * pair).astype(BF16), (lanes == 2 * pair + 1).astype(BF16)], axis=0
            )
            crossing = crossing + mm(jnp.concatenate([c0, c1], axis=1), pick)
        dgl = dgram.astype(BF16)
        dcc = dcc + mm(dgl, bb)
        dbb = dbb + mm(dgl, cc, TN)
        dxd = jnp.concatenate(inside, axis=1) + dxd_in
        kept = mm_split(jnp.broadcast_to(jnp.sum(h_in.astype(F32) * h_back, axis=0, keepdims=True), (8, CH)), collect)
        kept = kept[0:1, :] * ea[L - 1 : L, :]
        p_in = mm_split(dy * y_in, collect)
        q_in = mm_split(xd * dxd_in, collect)
        dls = crossing + mm_split_right(upper_low, p_in) + mm_split_right(strict_low, q_in) + kept
        k_.state[...] = h_back * ea_e[L - 1 : L, :] + mm(cc, dye, TN)
        dst = dls * rate + mm_split(dxd * xs, collect)
        dv = jnp.where(lanes < 8, dst * jax.nn.sigmoid(v), 0.0)
        k_.dproj[rows, S0:X0] = dv.astype(BF16)
        k_.gdt[...] += fold(dv)
        k_.gdl[...] += fold(dls * st)
        dxs = dy * skip + dxd * st_e
        between()
        k_.dcx[L : L + 8, :] = k_.dcx[0:8, :]
        k_.dcbc[L : L + 8, :] = k_.dcbc[0:8, :]
        k_.dcx[0:L, :] = dxs * (sx * (1.0 + cx - xs))
        k_.dcbc[0:L, :] = jnp.concatenate([dbb, dcc], axis=1) * (sbc * (1.0 + cbc - cbc * sbc))
        window = pl.ds(pl.multiple_of(b * L, 8), L + 8)
        k_.blkx[...] = keep.px[window, :]
        k_.blkbc[...] = keep.pbc[window, :]

        def conv_back(width, first_row, dc, blk, taps, start):
            for j in range(width // 128):
                cols = slice(128 * j, 128 * j + 128)
                d = dc[0:L, cols]
                taps[4, :, cols] += fold(d)
                total = jnp.zeros((L, 128), F32)
                for tap in range(4):
                    taps[tap, :, cols] += fold(d * blk[5 + tap : 5 + tap + L, cols])
                    total = total + par(first_row + tap, 128 * j, 128) * dc[3 - tap : 3 - tap + L, cols]
                k_.dproj[rows, start + 128 * j : start + 128 * j + 128] = total.astype(BF16)

        conv_back(CH, 0, k_.dcx, k_.blkx, k_.tapx, X0)
        conv_back(256, 9, k_.dcbc, k_.blkbc, k_.tapbc, B0)
        for j in range(4):
            wr = slice(4 * j, 4 * j + 4)
            if k == 1:
                d = mm(k_.dproj[rows, 0:D], k_.dw1[:, :, 256 * j : 256 * j + 256].reshape(D, 256))
                rest = k_.dproj[rows, D:O0]
                if j < 3:
                    d = d + mm(rest, k_.dw1[0:6, :, D + 256 * j : D + 256 * j + 256].reshape(O0 - D, 256))
                else:
                    tail_cols = (k_.dw1[0:6, :, COLS - 128 : COLS], k_.dw1[6:12, :, D : D + 128])
                    d = d + jnp.concatenate([mm(rest, a.reshape(O0 - D, 128)) for a in tail_cols], axis=1)
            else:
                d = mm(k_.dproj[rows, :], walls[k][wr, :, 0:O0].reshape(256, O0), NT)
            cols = slice(256 * j, 256 * j + 256)
            dn_ref[rows, cols] = d.astype(BF16)
            k_.gi[k, :, cols] += fold(d * keep.n[rows, cols].astype(F32))

    def small_grads(k):
        par = make_par(k)
        rate = -jnp.exp(par(8, 128, 128))
        k_.pack[k] = jnp.zeros((16, CH), F32)
        for tap in range(5):
            k_.pack[k, tap : tap + 1, :] = jnp.sum(k_.tapx[tap], axis=0, keepdims=True)
            k_.pack[k, 9 + tap : 10 + tap, 0:256] = jnp.sum(k_.tapbc[tap], axis=0, keepdims=True)
        k_.pack[k, 5:6, :] = jnp.sum(k_.ggo[...], axis=0, keepdims=True)
        k_.pack[k, 8:9, 0:128] = jnp.sum(k_.gdt[...], axis=0, keepdims=True)
        k_.pack[k, 8:9, 128:256] = jnp.sum(k_.gdl[...], axis=0, keepdims=True) * rate
        gs = mm_split(jnp.broadcast_to(jnp.sum(k_.gsk[...], axis=0, keepdims=True), (8, CH)), head_collect())
        k_.pack[k, 8:9, 256:384] = gs[0:1, :]
        gi = jnp.sum(k_.gi[k], axis=0, keepdims=True)
        k_.pack[k, 6:7, :] = gi[:, 0:CH] / par(6, 0, CH)
        k_.pack[k, 7:8, :] = gi[:, CH:D] / par(7, 0, CH)

    def weight_grads(k, part, gb_ref, dst):
        start, size = PARTS[k][part]
        for j in range(4):
            nt = saved[k].n[:, 256 * j : 256 * j + 256].T
            wr = slice(4 * j, 4 * j + 4)

            def put(c, value):
                width = value.shape[1]
                dst[wr, :, c : c + width] = value.astype(BF16).reshape(4, 64, width)

            for c in range(start, min(start + size, O0), 256):
                put(c, mm(nt, k_.dproj[:, c : min(c + 256, start + size, O0)]))
            if start + size > O0:
                gt = gb_ref[:, 256 * j : 256 * j + 256].T
                for c in range(2):
                    put(O0 + 256 * c, mm(gt, k_.gate[:, 256 * c : 256 * c + 256]))
            cols = pl.ds(start, size)
            links.d_twin.start(dst.at[wr, twin_half, cols], k_.theirs.at[k, wr, :, cols], (k, part), twin())

    def input_grad(k, total, u, upstream):
        par = make_par(k)
        gain = jnp.concatenate([par(6, 0, CH), par(7, 0, CH)], axis=1)
        r = lax.rsqrt(jnp.mean(u * u, axis=-1, keepdims=True) + EPS)
        c = total * gain
        back = upstream + r * c - u * (r * r * r * (1.0 / D)) * jnp.sum(c * u, axis=-1, keepdims=True)
        return back

    def turn_block(b):
        rows = slice_of(b, t)
        u = k_.hid[rows, :].astype(F32)
        total = slice_sum(links.dn1, k_.pc, k_.rb, b)
        back = input_grad(1, total, u, k_.gb1[rows, :].astype(F32))
        low = (row_mask(b * L + t * HALF, HALF) * back).astype(BF16)
        k_.gb0[rows, :] = low
        share_slice(links.gbs, k_.gb0, b)
        inner = jnp.sum(low.astype(F32) * k_.ptot0[b], axis=-1, keepdims=True)
        inner = jnp.broadcast_to(inner, (HALF, 128)).T[0:8, :]
        k_.inner_in[b, t] = jnp.concatenate([inner, jnp.zeros((8, 128 - HALF), F32)], axis=1)
        for j in ORDER:
            links.in0.start(k_.inner_in.at[b, t], k_.inner_in.at[b, t], b, x_peer(j))

    def to_owner(b):
        j = lax.rem(b - t + 4, 4)

        def go():
            links.dn0.start(k_.pa.at[span(b * L, L)], k_.dn0_in.at[j - 1], 0, {"tensor": b})

        pl.when(j != 0)(go)

    def reduce_first(k, part, dst):
        cols = pl.ds(*PARTS[k][part])
        links.d_twin.arrived(k_.theirs.at[k, :, :, cols], (k, part))

        def add(i, carry):
            dst[i, my_half, cols] = (
                dst[i, my_half, cols].astype(F32) + k_.theirs[k, i, :, cols].astype(F32)
            ).astype(BF16)
            return carry

        lax.fori_loop(0, 16, add, 0)
        for j in ORDER:
            for r in range(4):
                piece = dst.at[index(lax.rem(a1 + j, 4), r), my_half, cols]
                links.d_first.start(piece, k_.first_in.at[k, j - 1, r, :, cols], (k, part), first_peer(j))

    def bc_direct(k):
        for j in (0,) + ORDER:
            for i in (0,) + ORDER:
                place = lax.rem(a2 + j, 4)
                block = k_.mid.at[k, place, :, span((x_of(i) // 2) * 128, 128)]
                if (j, i) == (0, 0):
                    k_.bc_last[k, 0, 0] = k_.mid[k, place, :, span((t // 2) * 128, 128)]
                else:
                    peer = {"dp": index(a1, place), "tensor": x_of(i)}
                    links.bcx.start(block, k_.bc_last.at[k, j, i], k, peer)

    def bc_sum(k):
        links.bcx.arrived(k_.first_in.at[0, 0, 0, :, pl.ds(0, 15 * 128)], k)
        total = jnp.zeros((HALF, 128), F32)
        for j in range(4):
            for i in range(4):
                total = total + k_.bc_last[k, j, i].astype(F32)
        k_.half[k, :, B0 : B0 + 64] = jnp.where(lax.rem(t, 2) == 0, total[:, 0:64], total[:, 64:128])

    def reduce_second(k, part, dst):
        cols = pl.ds(*PARTS[k][part])
        links.d_first.arrived(k_.first_in.at[k, :, :, :, cols], (k, part))

        def add(r, carry):
            total = dst[index(a1, r), my_half, cols].astype(F32)
            for j in (1, 2, 3):
                total = total + k_.first_in[k, j - 1, r, :, cols].astype(F32)
            k_.mid[k, r, :, cols] = total.astype(BF16)
            return carry

        lax.fori_loop(0, 4, add, 0)
        for j in ORDER:
            piece = k_.mid.at[k, lax.rem(a2 + j, 4), :, cols]
            links.d_second.start(piece, k_.last_in.at[k, j, :, cols], (k, part), second_peer(j))
        if PARTS[k][part][0] == 0:
            bc_direct(k)

    def reduce_last(k, part):
        cols = pl.ds(*PARTS[k][part])
        links.d_second.arrived(k_.last_in.at[k, pl.ds(1, 3), :, cols], (k, part))
        total = k_.mid[k, a2, :, cols].astype(F32)
        for j in (1, 2, 3):
            total = total + k_.last_in[k, j, :, cols].astype(F32)
        k_.half[k, :, cols] = total
        if PARTS[k][part][0] == 0:
            bc_sum(k)

    reset_backward()
    k_.gi[...] = jnp.zeros((2, 8, D), F32)
    for c in range(0, O0, 256):
        size = min(256, O0 - c)
        turned = weight(1, c, size).T
        n = size // 64
        if c < D:
            k_.dw1[c // 64 : c // 64 + n, :, 0:D] = turned.reshape(n, 64, D)
        else:
            r = (c - D) // 64
            k_.dw1[r : r + n, :, D:COLS] = turned[:, 0 : COLS - D].reshape(n, 64, COLS - D)
            k_.dw1[6 + r : 6 + r + n, :, D : D + 128] = turned[:, COLS - D : D].reshape(n, 64, 128)
    for b in range(NB):
        tile_sum(links.sq1, 1, b)

    def second_backward(i, carry):
        b = NB - 1 - i
        inner = as_column(k_.sums[1, b, 1:2, :])
        backward_block(1, b, inner, k_.pc, lambda: pl.when(i >= 2)(lambda: turn_block(b + 2)))
        spread_slices(links.dn1, k_.pc, k_.rb, b)
        return carry

    lax.fori_loop(0, NB, second_backward, 0)
    small_grads(1)
    weight_grads(1, 0, k_.gb1, k_.dw1)
    turn_block(1)

    reset_backward()
    for b in range(NB):
        links.p0.sent(k_.ra.at[b], b)
    gather_sent(3)

    def first_inner(b):
        links.gbs.arrived(k_.ra.at[b], b)
        links.in0.arrived(k_.inner_in.at[b, pl.ds(1, 3)], b)
        row = k_.inner_in[b, 0, 0:1, :]
        for place in range(1, 4):
            row = row + pltpu.roll(k_.inner_in[b, place], HALF * place, 1)[0:1, :]
        return as_column(row)

    def first_backward(i, carry):
        b = NB - 1 - i

        def between():
            def at0():
                reduce_first(1, 0, k_.dw1)

            def at1():
                for j in ORDER:
                    links.p1.start(k_.pb.at[span(x_of(j) * ROWS, ROWS)], k_.p1_in.at[j - 1], 0, x_peer(j))

            pl.when(i == 0)(at0)
            pl.when(i == 1)(at1)

        backward_block(0, b, first_inner(b), k_.pa, between)
        pl.when(i == 0)(lambda: turn_block(0))
        return carry

    lax.fori_loop(0, 2, first_backward, 0)
    gate_block(0, 1, first_inner(1))
    gate_block(0, 0, first_inner(0))
    to_owner(3)
    to_owner(2)
    weight_grads(0, 0, k_.gb0, k_.wall1)

    def last_backward(i, carry):
        b = 1 - i

        def between():
            pl.when(i == 0)(lambda: reduce_first(0, 0, k_.wall1))
            pl.when(i == 1)(lambda: reduce_second(1, 0, k_.dw1))

        backward_block(0, b, None, k_.pa, between)
        to_owner(b)
        return carry

    lax.fori_loop(0, 2, last_backward, 0)
    small_grads(0)
    links.small.start(k_.pack.at[1 - s], k_.pack_in.at[0], 0, twin())
    weight_grads(0, 1, k_.gb0, k_.wall1)

    links.small.arrived(k_.pack_in.at[0], 0)
    k_.run[0] = k_.pack[s] + k_.pack_in[0]
    for j in ORDER:
        links.small.start(k_.run.at[0], k_.pack_in.at[j], 1, first_peer(j))
    reduce_first(0, 1, k_.wall1)
    reduce_second(0, 0, k_.wall1)

    def small_step(stage, peers):
        first = 3 * stage - 2
        links.small.arrived(k_.pack_in.at[pl.ds(first, 3)], stage)
        k_.run[stage] = (
            k_.run[stage - 1] + k_.pack_in[first] + k_.pack_in[first + 1] + k_.pack_in[first + 2]
        )
        for j in ORDER:
            links.small.start(k_.run.at[stage], k_.pack_in.at[first + 2 + j], stage + 1, peers(j))

    small_step(1, second_peer)
    reduce_second(0, 1, k_.wall1)
    small_step(2, x_peer)
    reduce_last(1, 0)
    reduce_last(0, 0)
    links.p1.arrived(k_.p1_in, 0)
    total = k_.pb[rows_t, :].astype(F32)
    for j in range(3):
        total = total + k_.p1_in[j].astype(F32)
    mask = row_mask(t * ROWS, ROWS)
    factor = factor_column(1, t)
    k_.los[0] = k_.hid[rows_t, :]
    k_.los[1] = (mask * (k_.hid[rows_t, :].astype(F32) + factor * total)).astype(BF16)
    links.outs.start(k_.los.at[1 - s], k_.lo.at[s], 0, twin())
    keep_lo = pltpu.make_async_copy(k_.los.at[s], k_.lo.at[s], lsem.at[2])
    keep_lo.start()
    links.dn0.arrived(k_.dn0_in, 0)
    total = k_.pa[rows_t, :].astype(F32)
    for j in range(3):
        total = total + k_.dn0_in[j].astype(F32)
    k_.igs[0] = input_grad(0, total, k_.tok[rows_t, :].astype(F32), k_.gb0[rows_t, :].astype(F32))
    k_.igs[1] = k_.gb0[rows_t, :].astype(F32)
    links.outs.start(k_.igs.at[1 - s], k_.ig.at[s], 1, twin())
    keep_ig = pltpu.make_async_copy(k_.igs.at[s], k_.ig.at[s], lsem.at[3])
    keep_ig.start()
    reduce_last(0, 1)
    links.shard.start(k_.half.at[1 - s], k_.other_half, 0, twin())
    links.shard.arrived(k_.other_half, 0)
    mine, others = k_.half[s], k_.other_half[...]
    k_.shard_out[my_half, :] = mine
    k_.shard_out[twin_half, :] = others
    links.small.arrived(k_.pack_in.at[pl.ds(7, 3)], 3)
    over_x = k_.run[2] + k_.pack_in[7] + k_.pack_in[8] + k_.pack_in[9]
    row = iota((16, CH), 0)
    shared = (row == 6) | (row == 7) | (row >= 9)
    over_x = jnp.where(shared, over_x, k_.run[2])
    k_.small_out[...] = over_x
    chosen = over_x[8:16, 0:64]
    for i in range(1, 4):
        chosen = jnp.where(t == i, over_x[8:16, 64 * i : 64 * i + 64], chosen)
    k_.small_out[9:14, 0:64] = chosen[1:6, :]

    keep_lo.wait()
    keep_ig.wait()
    links.outs.arrived(k_.los.at[0], 0)
    links.outs.arrived(k_.igs.at[0], 1)
    links.outs.sent(k_.los.at[0], 0)
    links.outs.sent(k_.igs.at[0], 1)
    links.params.sent(k_.par_own, 0)
    links.shard.sent(k_.other_half, 0)
    links.small.sent(k_.run.at[0], 0)
    for i in range(1, 4):
        links.small.sent(k_.run, i)
    links.early.sent(k_.bc_in.at[pl.ds(1, 3)], 0)
    links.early.sent(k_.par_in.at[pl.ds(1, 3)], 1)
    for a in range(2):
        links.rows1.sent(k_.tok.at[rows_t], (a, 0))
        links.rows1.sent(k_.tok.at[rows_t], (a, 1))
    links.rows2.sent(k_.tok.at[pl.ds(0, ROWS)], 0)
    links.p1.sent(k_.p1_in, 0)
    links.dn0.sent(k_.dn0_in, 0)
    for k in range(2):
        links.bcx.sent(k_.first_in.at[0, 0, 0, :, pl.ds(0, 15 * 128)], k)
    for group in range(3):
        gather_sent(group)

    def shard_sent(group):
        cols = pl.ds(*GROUPS[group][1:])
        for i in range(3):
            links.g_first.sent(k_.mid.at[0, pl.ds(0, 2), :, cols], (group, i))
        links.g_first.sent(k_.mid.at[0, 0, :, cols], (group, 3))

    for group in range(4):
        pl.when(s == GROUPS[group][0])(lambda: shard_sent(group))
    for k in range(2):
        for part in range(len(PARTS[k])):
            cols = pl.ds(*PARTS[k][part])
            links.d_twin.sent(k_.theirs.at[k, :, :, cols], (k, part))
            links.d_first.sent(k_.first_in.at[k, :, :, :, cols], (k, part))
            links.d_second.sent(k_.last_in.at[k, pl.ds(1, 3), :, cols], (k, part))
    for b in range(NB):
        links.sq0.sent(k_.sq_in.at[0, b, pl.ds(1, 3)], b)
        links.sq1.sent(k_.sq_in.at[1, b, pl.ds(1, 3)], b)
        links.in0.sent(k_.inner_in.at[b, pl.ds(1, 3)], b)
        for link in (links.hids, links.gbs, links.dn1):
            link.sent(k_.ra.at[b], b)


def unpack_kernel(
    shard, small, lo, ig,
    o_lo, o_ig, o_gi, o_wx, o_wz, o_bc, o_dt, o_cx, o_cb, o_bx, o_bb, o_db, o_dl, o_sk, o_go, o_wo,
):
    o_lo[...] = lo[...]
    o_ig[...] = ig[...]
    o_gi[:, 0:CH] = small[6:7, :]
    o_gi[:, CH:D] = small[7:8, :]
    o_wx[...] = shard[:, X0:Z0]
    o_wz[...] = shard[:, Z0:O0]
    o_bc[...] = shard[:, B0 : B0 + 64]
    steps = shard[:, S0:X0]
    o_dt[...] = jnp.concatenate([steps, steps], axis=0).T[0:8, 0:64]
    o_wo[...] = shard[:, O0:COLS]
    o_cx[...] = small[0:4, :]
    o_bx[...] = small[4:5, :]
    o_go[...] = small[5:6, :]
    o_db[...] = small[8:9, 0:8]
    o_dl[...] = small[8:9, 128:136]
    o_sk[...] = small[8:9, 256:264]
    o_cb[...] = small[9:13, 0:64]
    o_bb[...] = small[13:14, 0:64]


def sds(shape, dtype):
    return jax.ShapeDtypeStruct(shape, dtype)


VM = pl.BlockSpec(memory_space=pltpu.VMEM)
ANY = pl.BlockSpec(memory_space=pl.ANY)


def body(
    tokens_in, cotangent, seq_lengths, gain_in, weight_x, weight_z, weight_bc, weight_dt, conv_x, conv_bc,
    bias_x, bias_bc, dt_bias, decay_log, skip_gain, gain_out, weight_out,
):
    ins = [
        gain_in, weight_x, weight_z, weight_bc, weight_dt.swapaxes(1, 2), conv_x, conv_bc, bias_x, bias_bc, dt_bias,
        decay_log, skip_gain, gain_out, weight_out.swapaxes(1, 2), seq_lengths.T, tokens_in, cotangent,
    ]
    scratch = [pltpu.VMEM(*a) for a in SCRATCH.values()]
    scratch += [pltpu.VMEM(*a) for _ in range(2) for a in SAVED.values()]
    scratch += [pltpu.SemaphoreType.DMA((4,))]
    for shape in LINKS.values():
        scratch += [pltpu.SemaphoreType.DMA(shape)] * 2
    lo, ig, shard, small = pl.pallas_call(
        layer_kernel,
        out_shape=[
            sds((2, ROWS, D), BF16),
            sds((2, ROWS, D), F32),
            sds((64, COLS), F32),
            sds((16, CH), F32),
        ],
        in_specs=[VM] * 15 + [ANY] * 2,
        out_specs=[ANY, ANY, VM, VM],
        scratch_shapes=scratch,
        compiler_params=pltpu.CompilerParams(collective_id=0, has_side_effects=True, vmem_limit_bytes=VMEM_LIMIT),
    )(*ins)
    shapes = [
        (2, ROWS, D), (2, ROWS, D), (1, D), (64, CH), (64, CH), (64, 64), (8, 64), (4, CH), (4, 64), (1, CH), (1, 64),
        (1, 8), (1, 8), (1, 8), (1, CH), (64, CH),
    ]
    found = pl.pallas_call(
        unpack_kernel,
        out_shape=[sds(a, BF16 if i == 0 else F32) for i, a in enumerate(shapes)],
        in_specs=[VM] * 4,
        out_specs=[VM] * 16,
        compiler_params=pltpu.CompilerParams(vmem_limit_bytes=VMEM_LIMIT),
    )(shard, small, lo, ig)
    found = list(found)
    found[6] = found[6].T
    found[15] = found[15].T
    return tuple(a if i in (2, 9, 10, 11, 12, 13, 14) else a[None] for i, a in enumerate(found))


def solution(mesh):
    in_specs = (
        P(None, ("dp", "tensor"), None),
        P(None, ("dp", "tensor"), None),
        P(None, "dp"),
        P("section", None),
        P("section", "dp", "tensor"),
        P("section", "dp", "tensor"),
        P("section", "dp", "tensor"),
        P("section", "dp", "tensor"),
        P("section", None, "tensor"),
        P("section", None, "tensor"),
        P("section", "tensor"),
        P("section", "tensor"),
        P("section", "tensor"),
        P("section", "tensor"),
        P("section", "tensor"),
        P("section", "tensor"),
        P("section", "tensor", "dp"),
    )
    out_specs = (
        P("section", None, ("dp", "tensor"), None),
        P("section", None, ("dp", "tensor"), None),
        P("section", None),
        P("section", "dp", "tensor"),
        P("section", "dp", "tensor"),
        P("section", "dp", "tensor"),
        P("section", "dp", "tensor"),
        P("section", None, "tensor"),
        P("section", None, "tensor"),
        P("section", "tensor"),
        P("section", "tensor"),
        P("section", "tensor"),
        P("section", "tensor"),
        P("section", "tensor"),
        P("section", "tensor"),
        P("section", "tensor", "dp"),
    )
    return jax.shard_map(body, mesh=mesh, in_specs=in_specs, out_specs=out_specs, check_vma=False)
```

```python
import jax
import jax.numpy as jnp
from jax import lax
from jax.experimental import pallas as pl
from jax.experimental.pallas import tpu as pltpu
from jax.sharding import PartitionSpec as P

F32 = jnp.float32
BF16 = jnp.bfloat16
T = 512
L = 128
NB = T // L
D = 1024
CH = 512
INNER = 2048
NST = 128
EPS = 1e-05
B0, S0, X0, Z0, O0, COLS = 0, 256, 384, 896, 1408, 1920
VMEM_LIMIT = 60 * 2**20
MESH = pl.DeviceIdType.MESH
ROWS = 128
HALF = 32
ORDER = (1, 3, 2)

NN = (((1,), (0,)), ((), ()))
NT = (((1,), (1,)), ((), ()))
TN = (((0,), (0,)), ((), ()))


def mm(a, b, dims=NN):
    return lax.dot_general(a, b, dims, preferred_element_type=F32)


def mm_exact(a, b):
    return lax.dot_general(a, b, NN, precision=lax.Precision.HIGHEST, preferred_element_type=F32)


def mm_split(a, b):
    hi = a.astype(BF16)
    lo = (a - hi.astype(F32)).astype(BF16)
    return mm(hi, b) + mm(lo, b)


def mm_split_right(a, b):
    hi = b.astype(BF16)
    lo = (b - hi.astype(F32)).astype(BF16)
    return mm(a, hi) + mm(a, lo)


def iota(shape, dim):
    return lax.broadcasted_iota(jnp.int32, shape, dim)


def as_row(column):
    return jnp.broadcast_to(column, (L, 128)).T[0:1, :]


def as_column(row):
    return jnp.broadcast_to(row, (128, L)).T[:, 0:1]


def softplus(v):
    return jnp.maximum(v, 0.0) + jnp.log1p(jnp.exp(-jnp.abs(v)))


def head_spread():
    return (iota((128, CH), 1) // 64 == iota((128, CH), 0)).astype(BF16)


def head_collect():
    return (iota((CH, 128), 0) // 64 == iota((CH, 128), 1)).astype(BF16)


def fold(a):
    return jnp.sum(a.reshape(a.shape[0] // 8, 8, a.shape[1]), axis=0)


def span(start, size):
    return pl.ds(pl.multiple_of(start, size), size)


def places():
    group = lax.axis_index("dp")
    return lax.axis_index("section"), group // 4, lax.rem(group, 4), lax.axis_index("tensor")


def x_peer(j):
    return {"tensor": lax.rem(lax.axis_index("tensor") + j, 4)}


def twin():
    return {"section": 1 - lax.axis_index("section")}


def greet(peers):
    for peer in peers:
        pl.semaphore_signal(pltpu.get_barrier_semaphore(), inc=1, device_id=peer, device_id_type=MESH)


def greeted(peers):
    pl.semaphore_wait(pltpu.get_barrier_semaphore(), len(peers))


class Link:
    def __init__(self, send_sems, recv_sems):
        self.send_sems, self.recv_sems = send_sems, recv_sems

    def copy(self, src, dst, at, peer):
        return pltpu.make_async_remote_copy(
            src_ref=src,
            dst_ref=dst,
            send_sem=self.send_sems.at[at],
            recv_sem=self.recv_sems.at[at],
            device_id=peer,
            device_id_type=MESH,
        )

    def start(self, src, dst, at, peer):
        self.copy(src, dst, at, peer).start()

    def arrived(self, like, at):
        self.copy(like, like, at, twin()).wait_recv()

    def sent(self, like, at):
        self.copy(like, like, at, twin()).wait_send()


SCRATCH = dict(
    wall0=((16, 64, COLS), BF16),
    wall1=((16, 64, COLS), BF16),
    dw1=((16, 64, COLS), BF16),
    theirs=((2, 16, HALF, COLS), BF16),
    first_in=((2, 3, 4, HALF, COLS), BF16),
    mid=((2, 4, HALF, COLS), BF16),
    last_in=((2, 4, HALF, COLS), BF16),
    half=((2, HALF, COLS), F32),
    other_half=((HALF, COLS), F32),
    own=((64, COLS), BF16),
    bc_in=((4, 64, 128), BF16),
    par_own=((16, CH), F32),
    par_x=((8, 128), F32),
    par_in=((4, 8, 128), F32),
    run=((3, 16, CH), F32),
    square=((128, 128), F32),
    par_all=((2, 16, CH), F32),
    tok=((T, D), BF16),
    hid=((T, D), BF16),
    gb1=((T, D), BF16),
    gb0=((T, D), BF16),
    pa=((T, D), BF16),
    pb=((T, D), BF16),
    pc=((T, D), BF16),
    ra=((NB, 3, HALF, D), BF16),
    rb=((NB, 3, HALF, D), BF16),
    p1_in=((3, ROWS, D), BF16),
    dn0_in=((3, ROWS, D), BF16),
    ptot0=((NB, HALF, D), F32),
    sq_tile=((2, NB, 8, 128), F32),
    sq_in=((2, NB, 4, 8, 128), F32),
    sums=((2, NB, 8, 128), F32),
    inner_in=((NB, 4, 8, 128), F32),
    factors=((ROWS, 128), F32),
    dno=((T, CH), F32),
    blkx=((L + 8, CH), F32),
    blkbc=((L + 8, 256), F32),
    dcx=((L + 8, CH), F32),
    dcbc=((L + 8, 256), F32),
    gate=((T, CH), BF16),
    dproj=((T, 1408), BF16),
    state=((NST, CH), F32),
    ggo=((8, CH), F32),
    gsk=((8, CH), F32),
    gdt=((8, 128), F32),
    gdl=((8, 128), F32),
    tapx=((5, 8, CH), F32),
    tapbc=((5, 8, 256), F32),
    gi=((2, 8, D), F32),
    pack=((2, 16, CH), F32),
    pack_in=((10, 16, CH), F32),
    bc_last=((2, 4, 4, HALF, 128), BF16),
    los=((2, ROWS, D), BF16),
    igs=((2, ROWS, D), F32),
)
SAVED = dict(
    n=((T, D), BF16),
    px=((T + 8, CH), F32),
    cx=((T, CH), F32),
    pz=((T, CH), F32),
    pbc=((T + 8, 256), F32),
    cbc=((T, 256), F32),
    v=((T, 128), F32),
    y=((T, CH), F32),
    h=((NB, NST, CH), BF16),
)
LINKS = dict(
    early=(2,),
    rows1=(2, 2),
    rows2=(2,),
    params=(1,),
    g_first=(4, 4),
    g_second=(4, 3),
    g_twin=(4,),
    p0=(NB,),
    sq0=(NB,),
    hids=(NB,),
    sq1=(NB,),
    dn1=(NB,),
    gbs=(NB,),
    in0=(NB,),
    p1=(1,),
    dn0=(1,),
    d_twin=(2, 2),
    d_first=(2, 2),
    d_second=(2, 2),
    shard=(1,),
    small=(4,),
    bcx=(2,),
    outs=(2,),
)
GROUPS = ((0, X0, O0 - X0), (0, B0, X0), (0, O0, COLS - O0), (1, 0, COLS))
PARTS = (((Z0, COLS - Z0), (0, Z0)), ((0, COLS),))
INPUTS = (
    "gain_in", "weight_x", "weight_z", "weight_bc", "weight_dt", "conv_x", "conv_bc", "bias_x", "bias_bc", "dt_bias",
    "decay_log", "skip_gain", "gain_out", "weight_out", "lens", "tokens", "cot",
)
OUTPUTS = ("lo", "ig", "shard_out", "small_out")


class Names:
    def __init__(self, **kw):
        self.__dict__.update(kw)


def layer_kernel(*refs):
    names = list(INPUTS) + list(OUTPUTS) + list(SCRATCH)
    names += [f"{n}{k}" for k in range(2) for n in SAVED]
    k_ = Names(**dict(zip(names, refs)))
    rest = refs[len(names) :]
    lsem = rest[0]
    links = Names(**{n: Link(rest[1 + 2 * i], rest[2 + 2 * i]) for i, n in enumerate(LINKS)})
    saved = [Names(**{n: getattr(k_, f"{n}{k}") for n in SAVED}) for k in range(2)]
    walls = (k_.wall0, k_.wall1)
    s, z, y, t = places()
    own_d = z * 4 + y
    a1 = (1 - s) * y + s * z
    a2 = (1 - s) * z + s * y

    def index(first, second):
        return (1 - s) * (4 * second + first) + s * (4 * first + second)

    def first_peer(j):
        return {"dp": index(lax.rem(a1 + j, 4), a2)}

    def second_peer(j):
        return {"dp": index(a1, lax.rem(a2 + j, 4))}

    def x_of(j):
        return lax.rem(t + j, 4)

    my_half = span(HALF * s, HALF)
    twin_half = span(HALF * (1 - s), HALF)

    def y_peer(j, section):
        return {"section": section, "dp": z * 4 + lax.rem(y + j, 4)}

    def z_peer(j, section):
        return {"section": section, "dp": lax.rem(z + j, 4) * 4 + y}

    everyone = [x_peer(j) for j in ORDER] + [twin()]
    everyone += [peer(j, section) for peer in (y_peer, z_peer) for section in range(2) for j in ORDER]
    everyone += [{"dp": index(a1, lax.rem(a2 + j, 4)), "tensor": x_of(i)} for j in ORDER for i in ORDER]
    greet(everyone)

    k_.par_own[...] = jnp.zeros((16, CH), F32)
    k_.par_own[0:4, :] = k_.conv_x[0]
    k_.par_own[4:5, :] = k_.bias_x[...]
    k_.par_own[5:6, :] = k_.gain_out[...]
    k_.par_own[6:7, :] = k_.gain_in[:, 0:CH]
    k_.par_own[7:8, :] = k_.gain_in[:, CH:D]
    k_.par_own[8:9, 0:8] = k_.dt_bias[...]
    k_.par_own[8:9, 128:136] = k_.decay_log[...]
    k_.par_own[8:9, 256:264] = k_.skip_gain[...]
    k_.par_x[...] = jnp.zeros((8, 128), F32)
    k_.par_x[0:4, 0:64] = k_.conv_bc[0]
    k_.par_x[4:5, 0:64] = k_.bias_bc[...]
    k_.par_in[0] = k_.par_x[...]
    k_.bc_in[0] = jnp.zeros((64, 128), BF16)
    k_.bc_in[0, :, 0:64] = k_.weight_bc[0]
    k_.own[:, X0:Z0] = k_.weight_x[0]
    k_.own[:, Z0:O0] = k_.weight_z[0]
    k_.own[:, O0:COLS] = k_.weight_out[0]
    k_.square[...] = jnp.zeros((128, 128), F32)
    k_.square[0:8, 0:64] = k_.weight_dt[0].astype(F32)
    k_.own[:, S0:X0] = k_.square[...].T[0:64, :].astype(BF16)
    rows_t = span(t * ROWS, ROWS)
    local_tok = pltpu.make_async_copy(k_.tokens.at[s], k_.tok.at[rows_t], lsem.at[0])
    local_cot = pltpu.make_async_copy(k_.cot.at[s], k_.gb1.at[rows_t], lsem.at[1])
    local_tok.start()
    local_cot.start()
    greeted(everyone)
    for j in ORDER:
        links.early.start(k_.bc_in.at[0], k_.bc_in.at[j], 0, x_peer(j))
        links.early.start(k_.par_x, k_.par_in.at[j], 1, x_peer(j))

    def shard_to_all(group):
        k, start, size = GROUPS[group]
        cols = pl.ds(start, size)

        def part(half):
            rows = pl.ds(half * HALF, HALF)
            return k_.own.at[rows, cols], walls[k].at[own_d, rows, cols]

        for half, peer in enumerate((y_peer, z_peer)):
            for i, j in enumerate(ORDER):
                links.g_first.start(*part(half), (group, i), peer(j, half))
        links.g_first.start(*part(1 - k), (group, 3), twin())
        rows = pl.ds(k * HALF, HALF)
        walls[k][own_d, rows, cols] = k_.own[rows, cols]

    def gather_first(group):
        pl.when(s == GROUPS[group][0])(lambda: shard_to_all(group))

    def gather_second(group):
        k, start, size = GROUPS[group]
        for r in (0,) + ORDER:
            piece = walls[k].at[index(lax.rem(a1 - r + 4, 4), a2), my_half, pl.ds(start, size)]
            if r:
                links.g_first.arrived(piece, (group, ORDER.index(r)))
            else:
                pl.when(s != k)(lambda: links.g_first.arrived(piece, (group, 3)))
            for i, j in enumerate(ORDER):
                links.g_second.start(piece, piece, (group, i), second_peer(j))
            links.g_twin.start(piece, piece, group, twin())

    def gather_twin(group):
        k, start, size = GROUPS[group]
        for i, j in enumerate(ORDER):
            links.g_second.arrived(k_.mid.at[0, :, :, pl.ds(start, size)], (group, i))
            for r in (0,) + ORDER:
                place = index(lax.rem(a1 - r + 4, 4), lax.rem(a2 - j + 4, 4))
                piece = walls[k].at[place, my_half, pl.ds(start, size)]
                links.g_twin.start(piece, piece, group, twin())

    def gather_done(group):
        links.g_twin.arrived(k_.theirs.at[0, :, :, pl.ds(*GROUPS[group][1:])], group)

    def gather_sent(group):
        cols = pl.ds(*GROUPS[group][1:])
        for i in range(3):
            links.g_second.sent(k_.mid.at[0, :, :, cols], (group, i))
        links.g_twin.sent(k_.theirs.at[0, :, :, cols], group)

    def rows_first(a, src, dst):
        links.rows1.start(src.at[s], dst.at[rows_t], (a, 0), x_peer(1))
        links.rows1.start(src.at[s], dst.at[rows_t], (a, 1), x_peer(3))

    def rows_second(a, dst):
        links.rows1.arrived(dst.at[rows_t], (a, 0))
        upper = dst.at[span(x_of(3) * ROWS, ROWS // 2)]
        links.rows2.start(upper, upper, a, x_peer(1))
        links.rows1.arrived(dst.at[rows_t], (a, 1))
        lower_rows = dst.at[span(x_of(1) * ROWS + ROWS // 2, ROWS // 2)]
        links.rows2.start(lower_rows, lower_rows, a, x_peer(3))

    gather_first(0)
    rows_first(0, k_.tokens, k_.tok)
    gather_second(0)
    links.early.arrived(k_.bc_in.at[pl.ds(1, 3)], 0)
    links.early.arrived(k_.par_in.at[pl.ds(1, 3)], 1)
    left = iota((64, 128), 1) < 64
    left8 = iota((8, 128), 1) < 64
    slots = [lax.rem(t - i + 4, 4) for i in range(4)]
    for i in range(2):
        cols = slice(128 * i, 128 * i + 128)
        right = pltpu.roll(k_.bc_in[slots[2 * i + 1]].astype(F32), 64, 1)
        k_.own[:, cols] = jnp.where(left, k_.bc_in[slots[2 * i]].astype(F32), right).astype(BF16)
        right = pltpu.roll(k_.par_in[slots[2 * i + 1]], 64, 1)
        k_.par_own[9:14, cols] = jnp.where(left8, k_.par_in[slots[2 * i]], right)[0:5, :]
    gather_first(1)
    gather_first(2)
    k_.par_all[s] = k_.par_own[...]
    links.params.start(k_.par_own, k_.par_all.at[s], 0, twin())
    rows_second(0, k_.tok)
    gather_second(1)
    gather_second(2)
    links.params.arrived(k_.par_own, 0)

    length = jnp.where(s == 0, k_.lens[:, 0:1], k_.lens[:, 1:2])

    def row_mask(start, rows):
        return (iota((rows, 1), 0) + start < length).astype(F32)

    lower = iota((L, L), 0) >= iota((L, L), 1)
    tri = lower.astype(F32)
    off = jnp.where(lower, 0.0, -1e30)
    first_half = iota((L, 128), 1) < 64
    lanes = iota((L, 128), 1)

    def make_par(k):
        def par(row, start, size):
            return k_.par_all[k, row : row + 1, start : start + size]

        return par

    def weight(k, start, size):
        return walls[k][:, :, start : start + size].reshape(D, size)

    def project_block(k, b):
        par, keep = make_par(k), saved[k]
        rows = span(b * L, L)
        n = keep.n[rows, :]
        k_.blkbc[0:8, :] = k_.blkbc[L : L + 8, :]
        k_.blkx[0:8, :] = k_.blkx[L : L + 8, :]
        k_.blkbc[8 : 8 + L, :] = mm(n, weight(k, B0, 256))
        v = mm(n, weight(k, S0, 128)) + par(8, 0, 128)
        keep.v[rows, :] = v
        for j in range(2):
            k_.blkx[8 : 8 + L, 256 * j : 256 * j + 256] = mm(n, weight(k, X0 + 256 * j, 256))
        for j in range(2):
            keep.pz[rows, 256 * j : 256 * j + 256] = mm(n, weight(k, Z0 + 256 * j, 256))
        shifted = pl.ds(pl.multiple_of(b * L + 8, 8), L)
        keep.px[shifted, :] = k_.blkx[8 : 8 + L, :]
        keep.pbc[shifted, :] = k_.blkbc[8 : 8 + L, :]
        for j in range(4):
            cols = slice(128 * j, 128 * j + 128)
            c = par(4, 128 * j, 128)
            for tap in range(4):
                c = c + par(tap, 128 * j, 128) * k_.blkx[5 + tap : 5 + tap + L, cols]
            keep.cx[rows, cols] = c
        for j in range(2):
            cols = slice(128 * j, 128 * j + 128)
            c = par(13, 128 * j, 128)
            for tap in range(4):
                c = c + par(9 + tap, 128 * j, 128) * k_.blkbc[5 + tap : 5 + tap + L, cols]
            keep.cbc[rows, cols] = c

    def forward_block(k, b):
        par, keep = make_par(k), saved[k]
        rows = span(b * L, L)
        spread = head_spread()
        rate = -jnp.exp(par(8, 128, 128))
        skip = mm_exact(jnp.broadcast_to(par(8, 256, 128), (8, 128)), spread.astype(F32))[0:1, :]
        st = softplus(keep.v[rows, :])
        cu = mm_exact(tri, st * rate)
        cut = cu.T
        ea = jnp.exp(cu)
        tail = jnp.exp(cu[L - 1 : L, :] - cu)
        st_e = mm_split(st, spread)
        ea_e = mm_split(ea, spread)
        tail_e = mm_split(tail, spread)
        cx = keep.cx[rows, :]
        xs = cx * jax.nn.sigmoid(cx)
        cbc = keep.cbc[rows, :]
        bc = (cbc * jax.nn.sigmoid(cbc)).astype(BF16)
        bb, cc = bc[:, :NST], bc[:, NST:]
        xd = xs * st_e
        h_in = k_.state[...].astype(BF16)
        keep.h[b] = h_in
        gram = mm(cc, bb, NT)
        yy = mm(cc, h_in) * ea_e
        k_.state[...] = k_.state[...] * ea_e[L - 1 : L, :] + mm(bb, (xd * tail_e).astype(BF16), TN)
        inside = []
        for pair in range(4):
            xp = xd[:, 128 * pair : 128 * pair + 128]
            parts, mixes = [], []
            for part in range(2):
                h = 2 * pair + part
                mixes.append((gram * jnp.exp(cu[:, h : h + 1] - cut[h : h + 1, :] + off)).astype(BF16))
                parts.append(jnp.where(first_half == (part == 0), xp, 0.0).astype(BF16))
            inside.append(mm(jnp.concatenate(mixes, axis=1), jnp.concatenate(parts, axis=0)))
        yy = yy + jnp.concatenate(inside, axis=1)
        keep.y[rows, :] = yy
        zz = keep.pz[rows, :]
        gated = (yy + xs * skip) * (zz * jax.nn.sigmoid(zz))
        k_.sq_tile[k, b, 0:1, :] = as_row(jnp.sum(gated * gated, axis=-1, keepdims=True))
        weighted = gated * par(5, 0, CH)
        k_.gate[rows, :] = weighted.astype(BF16)
        if k == 1:
            gb = (k_.gb1[rows, :].astype(F32) * row_mask(b * L, L)).astype(BF16)
            k_.gb1[rows, :] = gb
            dno = jnp.concatenate([mm(gb, weight(k, O0, 256)), mm(gb, weight(k, O0 + 256, 256))], axis=1)
            k_.dno[rows, :] = dno
            k_.sq_tile[k, b, 1:2, :] = as_row(jnp.sum(dno * weighted, axis=-1, keepdims=True))

    def norm_block(k, b, u):
        par = make_par(k)
        gain = jnp.concatenate([par(6, 0, CH), par(7, 0, CH)], axis=1)
        for i in range(4):
            part = span(b * L + 32 * i, 32)
            a = u[part, :].astype(F32)
            r = lax.rsqrt(jnp.mean(a * a, axis=-1, keepdims=True) + EPS)
            saved[k].n[part, :] = (a * r * gain).astype(BF16)

    def reset_forward(k):
        k_.blkx[...] = jnp.zeros((L + 8, CH), F32)
        k_.blkbc[...] = jnp.zeros((L + 8, 256), F32)
        saved[k].px[0:8, :] = jnp.zeros((8, CH), F32)
        saved[k].pbc[0:8, :] = jnp.zeros((8, 256), F32)
        k_.state[...] = jnp.zeros((NST, CH), F32)

    def output_rows(k, rows, dst):
        for j in range(4):
            wo = walls[k][4 * j : 4 * j + 4, :, O0 : O0 + CH].reshape(256, CH)
            dst[rows, 256 * j : 256 * j + 256] = mm(k_.gate[rows, :], wo, NT).astype(BF16)

    def slice_of(b, place):
        return span(b * L + place * HALF, HALF)

    def spread_slices(link, buf, into, b):
        for j in ORDER:
            link.start(buf.at[slice_of(b, x_of(j))], into.at[b, j - 1], b, x_peer(j))

    def slice_sum(link, buf, into, b):
        link.arrived(into.at[b], b)
        total = buf[slice_of(b, t), :].astype(F32)
        for j in (1, 2, 3):
            total = total + into[b, j - 1].astype(F32)
        return total

    def share_slice(link, buf, b):
        rows = buf.at[slice_of(b, t)]
        for j in ORDER:
            link.start(rows, rows, b, x_peer(j))

    def spread_tile(link, k, b):
        for j in ORDER:
            link.start(k_.sq_tile.at[k, b], k_.sq_in.at[k, b, j], b, x_peer(j))

    def tile_sum(link, k, b):
        link.arrived(k_.sq_in.at[k, b, pl.ds(1, 3)], b)
        k_.sums[k, b] = (
            k_.sq_tile[k, b] + k_.sq_in[k, b, 1] + k_.sq_in[k, b, 2] + k_.sq_in[k, b, 3]
        )

    def factor_column(k, b):
        return as_column(lax.rsqrt(k_.sums[k, b, 0:1, :] / INNER + EPS))

    def hidden_block(b):
        tile_sum(links.sq0, 0, b)
        k_.factors[...] = jnp.broadcast_to(factor_column(0, b), (ROWS, 128))
        factor = k_.factors[span(t * HALF, HALF), :][:, 0:1]
        total = slice_sum(links.p0, k_.pa, k_.ra, b)
        k_.ptot0[b] = total
        rows = slice_of(b, t)
        mask = row_mask(b * L + t * HALF, HALF)
        k_.hid[rows, :] = (mask * (k_.tok[rows, :].astype(F32) + factor * total)).astype(BF16)
        share_slice(links.hids, k_.hid, b)

    links.rows2.arrived(k_.tok.at[pl.ds(0, ROWS)], 0)
    local_tok.wait()
    rows_first(1, k_.cot, k_.gb1)
    for b in range(NB):
        norm_block(0, b, k_.tok)
    reset_forward(0)
    k_.sq_tile[...] = jnp.zeros((2, NB, 8, 128), F32)
    gather_first(3)
    gather_twin(0)
    gather_twin(1)
    gather_done(0)
    gather_done(1)

    def first_forward(b, carry):
        project_block(0, b)
        forward_block(0, b)
        pl.when(b == 0)(lambda: gather_twin(2))
        spread_tile(links.sq0, 0, b)
        pl.when(b == 0)(lambda: gather_done(2))
        output_rows(0, span(b * L, L), k_.pa)
        spread_slices(links.p0, k_.pa, k_.ra, b)
        pl.when(b == 0)(lambda: gather_second(3))
        pl.when(b == 0)(lambda: rows_second(1, k_.gb1))
        pl.when(b >= 2)(lambda: hidden_block(b - 2))
        pl.when(b == 3)(lambda: gather_twin(3))
        return carry

    lax.fori_loop(0, NB, first_forward, 0)

    links.rows2.arrived(k_.tok.at[pl.ds(0, ROWS)], 1)
    links.rows2.sent(k_.tok.at[pl.ds(0, ROWS)], 1)
    local_cot.wait()
    reset_forward(1)
    gather_done(3)

    def second_forward(b, carry):
        pl.when(b < 2)(lambda: hidden_block(b + 2))
        links.hids.arrived(k_.ra.at[b], b)
        norm_block(1, b, k_.hid)
        project_block(1, b)
        forward_block(1, b)
        spread_tile(links.sq1, 1, b)
        return carry

    lax.fori_loop(0, NB, second_forward, 0)
    output_rows(1, pl.ds(0, T), k_.pb)

    upper_low = (iota((L, L), 1) >= iota((L, L), 0)).astype(BF16)
    strict = (iota((L, L), 1) < iota((L, L), 0)).astype(F32)
    strict_low = strict.astype(BF16)

    def reset_backward():
        k_.state[...] = jnp.zeros((NST, CH), F32)
        k_.ggo[...] = jnp.zeros((8, CH), F32)
        k_.gsk[...] = jnp.zeros((8, CH), F32)
        k_.gdt[...] = jnp.zeros((8, 128), F32)
        k_.gdl[...] = jnp.zeros((8, 128), F32)
        k_.tapx[...] = jnp.zeros((5, 8, CH), F32)
        k_.tapbc[...] = jnp.zeros((5, 8, 256), F32)
        k_.dcx[...] = jnp.zeros((L + 8, CH), F32)
        k_.dcbc[...] = jnp.zeros((L + 8, 256), F32)

    def gate_back(k, b, inner, xs, skip):
        par, keep = make_par(k), saved[k]
        rows = span(b * L, L)
        gain_out = par(5, 0, CH)
        factor = factor_column(k, b)
        if k == 1:
            dno = k_.dno[rows, :]
        else:
            gb = k_.gb0[rows, :]
            dno = jnp.concatenate([mm(gb, weight(k, O0, 256)), mm(gb, weight(k, O0 + 256, 256))], axis=1)
        out = keep.y[rows, :] + xs * skip
        zz = keep.pz[rows, :]
        sz = jax.nn.sigmoid(zz)
        silu_z = zz * sz
        gated = out * silu_z
        scaled = gated * factor
        k_.gate[rows, :] = (scaled * gain_out).astype(BF16)
        k_.ggo[...] += fold(dno * scaled)
        dgated = factor * (dno * gain_out) - gated * (factor * factor * factor * (1.0 / INNER) * inner)
        dy = dgated * silu_z
        k_.dproj[rows, Z0 : Z0 + CH] = (dgated * out * (sz * (1.0 + zz - silu_z))).astype(BF16)
        k_.gsk[...] += fold(dy * xs)
        return dy

    def skip_row(k):
        skip = jnp.broadcast_to(make_par(k)(8, 256, 128), (8, 128))
        return mm_exact(skip, head_spread().astype(F32))[0:1, :]

    def gate_block(k, b, inner):
        rows = span(b * L, L)
        cx = saved[k].cx[rows, :]
        k_.dno[rows, :] = gate_back(k, b, inner, cx * jax.nn.sigmoid(cx), skip_row(k))

    def backward_block(k, b, inner, dn_ref, between):
        par, keep = make_par(k), saved[k]
        rows = span(b * L, L)
        spread, collect = head_spread(), head_collect()
        rate = -jnp.exp(par(8, 128, 128))
        skip = skip_row(k)
        v = keep.v[rows, :]
        st = softplus(v)
        cu = mm_exact(tri, st * rate)
        cut = cu.T
        ea = jnp.exp(cu)
        tail = jnp.exp(cu[L - 1 : L, :] - cu)
        st_e = mm_split(st, spread)
        ea_e = mm_split(ea, spread)
        tail_e = mm_split(tail, spread)
        cx = keep.cx[rows, :]
        sx = jax.nn.sigmoid(cx)
        xs = cx * sx
        cbc = keep.cbc[rows, :]
        sbc = jax.nn.sigmoid(cbc)
        bc = (cbc * sbc).astype(BF16)
        bb, cc = bc[:, :NST], bc[:, NST:]
        xd = xs * st_e
        dy = k_.dno[rows, :] if inner is None else gate_back(k, b, inner, xs, skip)
        h_in = keep.h[b]
        h_back = k_.state[...]
        hb_low = h_back.astype(BF16)
        gram = mm(cc, bb, NT)
        xdt = (xd * tail_e).astype(BF16)
        dye = (dy * ea_e).astype(BF16)
        y_in = mm(cc, h_in) * ea_e
        dxd_in = mm(bb, hb_low) * tail_e
        dcc = mm(dye, h_in, NT)
        dbb = mm(xdt, hb_low, NT)
        dgram = jnp.zeros((L, L), F32)
        inside = []
        crossing = jnp.zeros((L, 128), F32)
        for pair in range(4):
            sl = slice(128 * pair, 128 * pair + 128)
            xp = xd[:, sl].astype(BF16)
            dyp = dy[:, sl]
            decs, mixes, parts = [], [], []
            for part in range(2):
                h = 2 * pair + part
                dec = jnp.exp(cu[:, h : h + 1] - cut[h : h + 1, :] + off)
                decs.append(dec)
                mixes.append(gram * dec)
                parts.append(jnp.where(first_half == (part == 0), dyp, 0.0).astype(BF16))
            dy2 = jnp.concatenate(parts, axis=0)
            dmix = mm(dy2, xp, NT)
            dm0, dm1 = dmix[:L, :], dmix[L:, :]
            dgram = dgram + dm0 * decs[0] + dm1 * decs[1]
            inside.append(mm(jnp.concatenate([mixes[0].astype(BF16), mixes[1].astype(BF16)], axis=0), dy2, TN))
            both = jnp.concatenate([(mixes[0] * dm0).astype(BF16), (mixes[1] * dm1).astype(BF16)], axis=1)
            cross = mm(upper_low, both)
            c0 = (cross[:, :L] * strict).astype(BF16)
            c1 = (cross[:, L:] * strict).astype(BF16)
            pick = jnp.concatenate(
                [(lanes == 2 * pair).astype(BF16), (lanes == 2 * pair + 1).astype(BF16)], axis=0
            )
            crossing = crossing + mm(jnp.concatenate([c0, c1], axis=1), pick)
        dgl = dgram.astype(BF16)
        dcc = dcc + mm(dgl, bb)
        dbb = dbb + mm(dgl, cc, TN)
        dxd = jnp.concatenate(inside, axis=1) + dxd_in
        kept = mm_split(jnp.broadcast_to(jnp.sum(h_in.astype(F32) * h_back, axis=0, keepdims=True), (8, CH)), collect)
        kept = kept[0:1, :] * ea[L - 1 : L, :]
        p_in = mm_split(dy * y_in, collect)
        q_in = mm_split(xd * dxd_in, collect)
        dls = crossing + mm_split_right(upper_low, p_in) + mm_split_right(strict_low, q_in) + kept
        k_.state[...] = h_back * ea_e[L - 1 : L, :] + mm(cc, dye, TN)
        dst = dls * rate + mm_split(dxd * xs, collect)
        dv = jnp.where(lanes < 8, dst * jax.nn.sigmoid(v), 0.0)
        k_.dproj[rows, S0:X0] = dv.astype(BF16)
        k_.gdt[...] += fold(dv)
        k_.gdl[...] += fold(dls * st)
        dxs = dy * skip + dxd * st_e
        between()
        k_.dcx[L : L + 8, :] = k_.dcx[0:8, :]
        k_.dcbc[L : L + 8, :] = k_.dcbc[0:8, :]
        k_.dcx[0:L, :] = dxs * (sx * (1.0 + cx - xs))
        k_.dcbc[0:L, :] = jnp.concatenate([dbb, dcc], axis=1) * (sbc * (1.0 + cbc - cbc * sbc))
        window = pl.ds(pl.multiple_of(b * L, 8), L + 8)
        k_.blkx[...] = keep.px[window, :]
        k_.blkbc[...] = keep.pbc[window, :]

        def conv_back(width, first_row, dc, blk, taps, start):
            for j in range(width // 128):
                cols = slice(128 * j, 128 * j + 128)
                d = dc[0:L, cols]
                taps[4, :, cols] += fold(d)
                total = jnp.zeros((L, 128), F32)
                for tap in range(4):
                    taps[tap, :, cols] += fold(d * blk[5 + tap : 5 + tap + L, cols])
                    total = total + par(first_row + tap, 128 * j, 128) * dc[3 - tap : 3 - tap + L, cols]
                k_.dproj[rows, start + 128 * j : start + 128 * j + 128] = total.astype(BF16)

        conv_back(CH, 0, k_.dcx, k_.blkx, k_.tapx, X0)
        conv_back(256, 9, k_.dcbc, k_.blkbc, k_.tapbc, B0)
        for j in range(4):
            wr = slice(4 * j, 4 * j + 4)
            if k == 1:
                d = mm(k_.dproj[rows, 0:D], k_.dw1[:, :, 256 * j : 256 * j + 256].reshape(D, 256))
                rest = k_.dproj[rows, D:O0]
                if j < 3:
                    d = d + mm(rest, k_.dw1[0:6, :, D + 256 * j : D + 256 * j + 256].reshape(O0 - D, 256))
                else:
                    tail_cols = (k_.dw1[0:6, :, COLS - 128 : COLS], k_.dw1[6:12, :, D : D + 128])
                    d = d + jnp.concatenate([mm(rest, a.reshape(O0 - D, 128)) for a in tail_cols], axis=1)
            else:
                d = mm(k_.dproj[rows, :], walls[k][wr, :, 0:O0].reshape(256, O0), NT)
            cols = slice(256 * j, 256 * j + 256)
            dn_ref[rows, cols] = d.astype(BF16)
            k_.gi[k, :, cols] += fold(d * keep.n[rows, cols].astype(F32))

    def small_grads(k):
        par = make_par(k)
        rate = -jnp.exp(par(8, 128, 128))
        k_.pack[k] = jnp.zeros((16, CH), F32)
        for tap in range(5):
            k_.pack[k, tap : tap + 1, :] = jnp.sum(k_.tapx[tap], axis=0, keepdims=True)
            k_.pack[k, 9 + tap : 10 + tap, 0:256] = jnp.sum(k_.tapbc[tap], axis=0, keepdims=True)
        k_.pack[k, 5:6, :] = jnp.sum(k_.ggo[...], axis=0, keepdims=True)
        k_.pack[k, 8:9, 0:128] = jnp.sum(k_.gdt[...], axis=0, keepdims=True)
        k_.pack[k, 8:9, 128:256] = jnp.sum(k_.gdl[...], axis=0, keepdims=True) * rate
        gs = mm_split(jnp.broadcast_to(jnp.sum(k_.gsk[...], axis=0, keepdims=True), (8, CH)), head_collect())
        k_.pack[k, 8:9, 256:384] = gs[0:1, :]
        gi = jnp.sum(k_.gi[k], axis=0, keepdims=True)
        k_.pack[k, 6:7, :] = gi[:, 0:CH] / par(6, 0, CH)
        k_.pack[k, 7:8, :] = gi[:, CH:D] / par(7, 0, CH)

    def weight_grads(k, part, gb_ref, dst):
        start, size = PARTS[k][part]
        for j in range(4):
            nt = saved[k].n[:, 256 * j : 256 * j + 256].T
            wr = slice(4 * j, 4 * j + 4)

            def put(c, value):
                width = value.shape[1]
                dst[wr, :, c : c + width] = value.astype(BF16).reshape(4, 64, width)

            for c in range(start, min(start + size, O0), 256):
                put(c, mm(nt, k_.dproj[:, c : min(c + 256, start + size, O0)]))
            if start + size > O0:
                gt = gb_ref[:, 256 * j : 256 * j + 256].T
                for c in range(2):
                    put(O0 + 256 * c, mm(gt, k_.gate[:, 256 * c : 256 * c + 256]))
            cols = pl.ds(start, size)
            links.d_twin.start(dst.at[wr, twin_half, cols], k_.theirs.at[k, wr, :, cols], (k, part), twin())

    def input_grad(k, total, u, upstream):
        par = make_par(k)
        gain = jnp.concatenate([par(6, 0, CH), par(7, 0, CH)], axis=1)
        r = lax.rsqrt(jnp.mean(u * u, axis=-1, keepdims=True) + EPS)
        c = total * gain
        back = upstream + r * c - u * (r * r * r * (1.0 / D)) * jnp.sum(c * u, axis=-1, keepdims=True)
        return back

    def turn_block(b):
        rows = slice_of(b, t)
        u = k_.hid[rows, :].astype(F32)
        total = slice_sum(links.dn1, k_.pc, k_.rb, b)
        back = input_grad(1, total, u, k_.gb1[rows, :].astype(F32))
        low = (row_mask(b * L + t * HALF, HALF) * back).astype(BF16)
        k_.gb0[rows, :] = low
        share_slice(links.gbs, k_.gb0, b)
        inner = jnp.sum(low.astype(F32) * k_.ptot0[b], axis=-1, keepdims=True)
        inner = jnp.broadcast_to(inner, (HALF, 128)).T[0:8, :]
        k_.inner_in[b, t] = jnp.concatenate([inner, jnp.zeros((8, 128 - HALF), F32)], axis=1)
        for j in ORDER:
            links.in0.start(k_.inner_in.at[b, t], k_.inner_in.at[b, t], b, x_peer(j))

    def to_owner(b):
        j = lax.rem(b - t + 4, 4)

        def go():
            links.dn0.start(k_.pa.at[span(b * L, L)], k_.dn0_in.at[j - 1], 0, {"tensor": b})

        pl.when(j != 0)(go)

    def reduce_first(k, part, dst):
        cols = pl.ds(*PARTS[k][part])
        links.d_twin.arrived(k_.theirs.at[k, :, :, cols], (k, part))

        def add(i, carry):
            dst[i, my_half, cols] = (
                dst[i, my_half, cols].astype(F32) + k_.theirs[k, i, :, cols].astype(F32)
            ).astype(BF16)
            return carry

        lax.fori_loop(0, 16, add, 0)
        for j in ORDER:
            for r in range(4):
                piece = dst.at[index(lax.rem(a1 + j, 4), r), my_half, cols]
                links.d_first.start(piece, k_.first_in.at[k, j - 1, r, :, cols], (k, part), first_peer(j))

    def bc_direct(k):
        for j in (0,) + ORDER:
            for i in (0,) + ORDER:
                place = lax.rem(a2 + j, 4)
                block = k_.mid.at[k, place, :, span((x_of(i) // 2) * 128, 128)]
                if (j, i) == (0, 0):
                    k_.bc_last[k, 0, 0] = k_.mid[k, place, :, span((t // 2) * 128, 128)]
                else:
                    peer = {"dp": index(a1, place), "tensor": x_of(i)}
                    links.bcx.start(block, k_.bc_last.at[k, j, i], k, peer)

    def bc_sum(k):
        links.bcx.arrived(k_.first_in.at[0, 0, 0, :, pl.ds(0, 15 * 128)], k)
        total = jnp.zeros((HALF, 128), F32)
        for j in range(4):
            for i in range(4):
                total = total + k_.bc_last[k, j, i].astype(F32)
        k_.half[k, :, B0 : B0 + 64] = jnp.where(lax.rem(t, 2) == 0, total[:, 0:64], total[:, 64:128])

    def reduce_second(k, part, dst):
        cols = pl.ds(*PARTS[k][part])
        links.d_first.arrived(k_.first_in.at[k, :, :, :, cols], (k, part))

        def add(r, carry):
            total = dst[index(a1, r), my_half, cols].astype(F32)
            for j in (1, 2, 3):
                total = total + k_.first_in[k, j - 1, r, :, cols].astype(F32)
            k_.mid[k, r, :, cols] = total.astype(BF16)
            return carry

        lax.fori_loop(0, 4, add, 0)
        for j in ORDER:
            piece = k_.mid.at[k, lax.rem(a2 + j, 4), :, cols]
            links.d_second.start(piece, k_.last_in.at[k, j, :, cols], (k, part), second_peer(j))
        if PARTS[k][part][0] == 0:
            bc_direct(k)

    def reduce_last(k, part):
        cols = pl.ds(*PARTS[k][part])
        links.d_second.arrived(k_.last_in.at[k, pl.ds(1, 3), :, cols], (k, part))
        total = k_.mid[k, a2, :, cols].astype(F32)
        for j in (1, 2, 3):
            total = total + k_.last_in[k, j, :, cols].astype(F32)
        k_.half[k, :, cols] = total
        if PARTS[k][part][0] == 0:
            bc_sum(k)

    reset_backward()
    k_.gi[...] = jnp.zeros((2, 8, D), F32)
    for c in range(0, O0, 256):
        size = min(256, O0 - c)
        turned = weight(1, c, size).T
        n = size // 64
        if c < D:
            k_.dw1[c // 64 : c // 64 + n, :, 0:D] = turned.reshape(n, 64, D)
        else:
            r = (c - D) // 64
            k_.dw1[r : r + n, :, D:COLS] = turned[:, 0 : COLS - D].reshape(n, 64, COLS - D)
            k_.dw1[6 + r : 6 + r + n, :, D : D + 128] = turned[:, COLS - D : D].reshape(n, 64, 128)
    for b in range(NB):
        tile_sum(links.sq1, 1, b)

    def second_backward(i, carry):
        b = NB - 1 - i
        inner = as_column(k_.sums[1, b, 1:2, :])
        backward_block(1, b, inner, k_.pc, lambda: pl.when(i >= 2)(lambda: turn_block(b + 2)))
        spread_slices(links.dn1, k_.pc, k_.rb, b)
        return carry

    lax.fori_loop(0, NB, second_backward, 0)
    small_grads(1)
    weight_grads(1, 0, k_.gb1, k_.dw1)
    turn_block(1)

    reset_backward()
    for b in range(NB):
        links.p0.sent(k_.ra.at[b], b)
    gather_sent(3)

    def first_inner(b):
        links.gbs.arrived(k_.ra.at[b], b)
        links.in0.arrived(k_.inner_in.at[b, pl.ds(1, 3)], b)
        row = k_.inner_in[b, 0, 0:1, :]
        for place in range(1, 4):
            row = row + pltpu.roll(k_.inner_in[b, place], HALF * place, 1)[0:1, :]
        return as_column(row)

    def first_backward(i, carry):
        b = NB - 1 - i

        def between():
            def at0():
                reduce_first(1, 0, k_.dw1)

            def at1():
                for j in ORDER:
                    links.p1.start(k_.pb.at[span(x_of(j) * ROWS, ROWS)], k_.p1_in.at[j - 1], 0, x_peer(j))

            pl.when(i == 0)(at0)
            pl.when(i == 1)(at1)

        backward_block(0, b, first_inner(b), k_.pa, between)
        pl.when(i == 0)(lambda: turn_block(0))
        return carry

    lax.fori_loop(0, 2, first_backward, 0)
    gate_block(0, 1, first_inner(1))
    gate_block(0, 0, first_inner(0))
    to_owner(3)
    to_owner(2)
    weight_grads(0, 0, k_.gb0, k_.wall1)

    def last_backward(i, carry):
        b = 1 - i

        def between():
            pl.when(i == 0)(lambda: reduce_first(0, 0, k_.wall1))
            pl.when(i == 1)(lambda: reduce_second(1, 0, k_.dw1))

        backward_block(0, b, None, k_.pa, between)
        to_owner(b)
        return carry

    lax.fori_loop(0, 2, last_backward, 0)
    small_grads(0)
    links.small.start(k_.pack.at[1 - s], k_.pack_in.at[0], 0, twin())
    weight_grads(0, 1, k_.gb0, k_.wall1)

    links.small.arrived(k_.pack_in.at[0], 0)
    k_.run[0] = k_.pack[s] + k_.pack_in[0]
    for j in ORDER:
        links.small.start(k_.run.at[0], k_.pack_in.at[j], 1, first_peer(j))
    reduce_first(0, 1, k_.wall1)
    reduce_second(0, 0, k_.wall1)

    def small_step(stage, peers):
        first = 3 * stage - 2
        links.small.arrived(k_.pack_in.at[pl.ds(first, 3)], stage)
        k_.run[stage] = (
            k_.run[stage - 1] + k_.pack_in[first] + k_.pack_in[first + 1] + k_.pack_in[first + 2]
        )
        for j in ORDER:
            links.small.start(k_.run.at[stage], k_.pack_in.at[first + 2 + j], stage + 1, peers(j))

    small_step(1, second_peer)
    reduce_second(0, 1, k_.wall1)
    small_step(2, x_peer)
    reduce_last(1, 0)
    reduce_last(0, 0)
    links.p1.arrived(k_.p1_in, 0)
    total = k_.pb[rows_t, :].astype(F32)
    for j in range(3):
        total = total + k_.p1_in[j].astype(F32)
    mask = row_mask(t * ROWS, ROWS)
    factor = factor_column(1, t)
    k_.los[0] = k_.hid[rows_t, :]
    k_.los[1] = (mask * (k_.hid[rows_t, :].astype(F32) + factor * total)).astype(BF16)
    links.outs.start(k_.los.at[1 - s], k_.lo.at[s], 0, twin())
    keep_lo = pltpu.make_async_copy(k_.los.at[s], k_.lo.at[s], lsem.at[2])
    keep_lo.start()
    links.dn0.arrived(k_.dn0_in, 0)
    total = k_.pa[rows_t, :].astype(F32)
    for j in range(3):
        total = total + k_.dn0_in[j].astype(F32)
    k_.igs[0] = input_grad(0, total, k_.tok[rows_t, :].astype(F32), k_.gb0[rows_t, :].astype(F32))
    k_.igs[1] = k_.gb0[rows_t, :].astype(F32)
    links.outs.start(k_.igs.at[1 - s], k_.ig.at[s], 1, twin())
    keep_ig = pltpu.make_async_copy(k_.igs.at[s], k_.ig.at[s], lsem.at[3])
    keep_ig.start()
    reduce_last(0, 1)
    links.shard.start(k_.half.at[1 - s], k_.other_half, 0, twin())
    links.shard.arrived(k_.other_half, 0)
    mine, others = k_.half[s], k_.other_half[...]
    k_.shard_out[my_half, :] = mine
    k_.shard_out[twin_half, :] = others
    links.small.arrived(k_.pack_in.at[pl.ds(7, 3)], 3)
    over_x = k_.run[2] + k_.pack_in[7] + k_.pack_in[8] + k_.pack_in[9]
    row = iota((16, CH), 0)
    shared = (row == 6) | (row == 7) | (row >= 9)
    over_x = jnp.where(shared, over_x, k_.run[2])
    k_.small_out[...] = over_x
    chosen = over_x[8:16, 0:64]
    for i in range(1, 4):
        chosen = jnp.where(t == i, over_x[8:16, 64 * i : 64 * i + 64], chosen)
    k_.small_out[9:14, 0:64] = chosen[1:6, :]

    keep_lo.wait()
    keep_ig.wait()
    links.outs.arrived(k_.los.at[0], 0)
    links.outs.arrived(k_.igs.at[0], 1)
    links.outs.sent(k_.los.at[0], 0)
    links.outs.sent(k_.igs.at[0], 1)
    links.params.sent(k_.par_own, 0)
    links.shard.sent(k_.other_half, 0)
    links.small.sent(k_.run.at[0], 0)
    for i in range(1, 4):
        links.small.sent(k_.run, i)
    links.early.sent(k_.bc_in.at[pl.ds(1, 3)], 0)
    links.early.sent(k_.par_in.at[pl.ds(1, 3)], 1)
    for a in range(2):
        links.rows1.sent(k_.tok.at[rows_t], (a, 0))
        links.rows1.sent(k_.tok.at[rows_t], (a, 1))
    links.rows2.sent(k_.tok.at[pl.ds(0, ROWS)], 0)
    links.p1.sent(k_.p1_in, 0)
    links.dn0.sent(k_.dn0_in, 0)
    for k in range(2):
        links.bcx.sent(k_.first_in.at[0, 0, 0, :, pl.ds(0, 15 * 128)], k)
    for group in range(3):
        gather_sent(group)

    def shard_sent(group):
        cols = pl.ds(*GROUPS[group][1:])
        for i in range(3):
            links.g_first.sent(k_.mid.at[0, pl.ds(0, 2), :, cols], (group, i))
        links.g_first.sent(k_.mid.at[0, 0, :, cols], (group, 3))

    for group in range(4):
        pl.when(s == GROUPS[group][0])(lambda: shard_sent(group))
    for k in range(2):
        for part in range(len(PARTS[k])):
            cols = pl.ds(*PARTS[k][part])
            links.d_twin.sent(k_.theirs.at[k, :, :, cols], (k, part))
            links.d_first.sent(k_.first_in.at[k, :, :, :, cols], (k, part))
            links.d_second.sent(k_.last_in.at[k, pl.ds(1, 3), :, cols], (k, part))
    for b in range(NB):
        links.sq0.sent(k_.sq_in.at[0, b, pl.ds(1, 3)], b)
        links.sq1.sent(k_.sq_in.at[1, b, pl.ds(1, 3)], b)
        links.in0.sent(k_.inner_in.at[b, pl.ds(1, 3)], b)
        for link in (links.hids, links.gbs, links.dn1):
            link.sent(k_.ra.at[b], b)


def unpack_kernel(
    shard, small, lo, ig,
    o_lo, o_ig, o_gi, o_wx, o_wz, o_bc, o_dt, o_cx, o_cb, o_bx, o_bb, o_db, o_dl, o_sk, o_go, o_wo,
):
    o_lo[...] = lo[...]
    o_ig[...] = ig[...]
    o_gi[:, 0:CH] = small[6:7, :]
    o_gi[:, CH:D] = small[7:8, :]
    o_wx[...] = shard[:, X0:Z0]
    o_wz[...] = shard[:, Z0:O0]
    o_bc[...] = shard[:, B0 : B0 + 64]
    steps = shard[:, S0:X0]
    o_dt[...] = jnp.concatenate([steps, steps], axis=0).T[0:8, 0:64]
    o_wo[...] = shard[:, O0:COLS]
    o_cx[...] = small[0:4, :]
    o_bx[...] = small[4:5, :]
    o_go[...] = small[5:6, :]
    o_db[...] = small[8:9, 0:8]
    o_dl[...] = small[8:9, 128:136]
    o_sk[...] = small[8:9, 256:264]
    o_cb[...] = small[9:13, 0:64]
    o_bb[...] = small[13:14, 0:64]


def sds(shape, dtype):
    return jax.ShapeDtypeStruct(shape, dtype)


VM = pl.BlockSpec(memory_space=pltpu.VMEM)
ANY = pl.BlockSpec(memory_space=pl.ANY)


def body(
    tokens_in, cotangent, seq_lengths, gain_in, weight_x, weight_z, weight_bc, weight_dt, conv_x, conv_bc,
    bias_x, bias_bc, dt_bias, decay_log, skip_gain, gain_out, weight_out,
):
    ins = [
        gain_in, weight_x, weight_z, weight_bc, weight_dt.swapaxes(1, 2), conv_x, conv_bc, bias_x, bias_bc, dt_bias,
        decay_log, skip_gain, gain_out, weight_out.swapaxes(1, 2), seq_lengths.T, tokens_in, cotangent,
    ]
    scratch = [pltpu.VMEM(*a) for a in SCRATCH.values()]
    scratch += [pltpu.VMEM(*a) for _ in range(2) for a in SAVED.values()]
    scratch += [pltpu.SemaphoreType.DMA((4,))]
    for shape in LINKS.values():
        scratch += [pltpu.SemaphoreType.DMA(shape)] * 2
    lo, ig, shard, small = pl.pallas_call(
        layer_kernel,
        out_shape=[
            sds((2, ROWS, D), BF16),
            sds((2, ROWS, D), F32),
            sds((64, COLS), F32),
            sds((16, CH), F32),
        ],
        in_specs=[VM] * 15 + [ANY] * 2,
        out_specs=[ANY, ANY, VM, VM],
        scratch_shapes=scratch,
        compiler_params=pltpu.CompilerParams(collective_id=0, has_side_effects=True, vmem_limit_bytes=VMEM_LIMIT),
    )(*ins)
    shapes = [
        (2, ROWS, D), (2, ROWS, D), (1, D), (64, CH), (64, CH), (64, 64), (8, 64), (4, CH), (4, 64), (1, CH), (1, 64),
        (1, 8), (1, 8), (1, 8), (1, CH), (64, CH),
    ]
    found = pl.pallas_call(
        unpack_kernel,
        out_shape=[sds(a, BF16 if i == 0 else F32) for i, a in enumerate(shapes)],
        in_specs=[VM] * 4,
        out_specs=[VM] * 16,
        compiler_params=pltpu.CompilerParams(vmem_limit_bytes=VMEM_LIMIT),
    )(shard, small, lo, ig)
    found = list(found)
    found[6] = found[6].T
    found[15] = found[15].T
    return tuple(a if i in (2, 9, 10, 11, 12, 13, 14) else a[None] for i, a in enumerate(found))


def solution(mesh):
    in_specs = (
        P(None, ("dp", "tensor"), None),
        P(None, ("dp", "tensor"), None),
        P(None, "dp"),
        P("section", None),
        P("section", "dp", "tensor"),
        P("section", "dp", "tensor"),
        P("section", "dp", "tensor"),
        P("section", "dp", "tensor"),
        P("section", None, "tensor"),
        P("section", None, "tensor"),
        P("section", "tensor"),
        P("section", "tensor"),
        P("section", "tensor"),
        P("section", "tensor"),
        P("section", "tensor"),
        P("section", "tensor"),
        P("section", "tensor", "dp"),
    )
    out_specs = (
        P("section", None, ("dp", "tensor"), None),
        P("section", None, ("dp", "tensor"), None),
        P("section", None),
        P("section", "dp", "tensor"),
        P("section", "dp", "tensor"),
        P("section", "dp", "tensor"),
        P("section", "dp", "tensor"),
        P("section", None, "tensor"),
        P("section", None, "tensor"),
        P("section", "tensor"),
        P("section", "tensor"),
        P("section", "tensor"),
        P("section", "tensor"),
        P("section", "tensor"),
        P("section", "tensor"),
        P("section", "tensor", "dp"),
    )
    return jax.shard_map(body, mesh=mesh, in_specs=in_specs, out_specs=out_specs, check_vma=False)
```
